256 devices in a mesh: prow: 8 (over z), pcol: 32 (over x, y, core).
Axes of the slice: x: 4, y: 4, z: 8, core: 2. Of those that a mesh axis runs over, the one named last changes fastest.
Arguments:
- trailing: bfloat16 [196608, 4096], P('prow', 'pcol'), may hold values from -6 to 6
- panel_t: bfloat16 [256, 196608], P('pcol', 'prow'), may hold values from -0.25 to 0.25
- pivots: int32 [256], replicated, may hold values from 256 to 196607, as said below
Outputs:
- updated: bfloat16 [196608, 4096], P('prow', 'pcol')
The draws below stay inside these ranges and needn't reach their ends.
Inputs may be any that keep to these rules, and one draw needn't show every extreme that they name: The 256 pivots are distinct, and each is 256 or more; pivots[0] is 196607 and pivots[1] is 256.
All inputs are finite; a program needn't handle non-finite values.
Results may differ from the reference program's by a relative error of at most 0.0035.
Values may be sent and summed in bfloat16 or wider, within the bound.
No kernel may reach another device: no remote copies, remote signals or barrier semaphores. Data moves between devices by JAX's collectives and lax.ppermute only.
A program may use at most 64 MiB of HBM per device.

```python
import jax
import jax.numpy as jnp
from jax import lax

NB = 256
ROWS = 196608
COLS = 4096


def draw_pivots(key, part):
    key = jax.random.fold_in(key, 7)
    span = ROWS - NB - 2
    order = jax.random.permutation(key, span).astype(jnp.int32)
    inner = order[:NB - 2] + 1 + NB
    ends = jnp.array([ROWS - 1, NB], dtype=jnp.int32)
    return jnp.concatenate([ends, inner.astype(jnp.int32)]).astype(jnp.int32)


def steps_of(stream_key, shape, shards, low, top_value):
    def one(position, parts):
        draws = jax.random.uniform(jax.random.fold_in(jax.random.fold_in(stream_key, 6), position), (parts,), jnp.float32, low / len(shards), top_value / len(shards))
        return jnp.repeat(jnp.exp(draws), shape[position] // parts).reshape((-1,) + (1,) * (len(shape) - position - 1))

    loudness = one(*shards[0])
    for cut in shards[1:]:
        loudness = loudness * one(*cut)
    return loudness


def bell_draw(key, dims, deviation, most, split=(), kind=jnp.bfloat16):
    values = deviation * jax.random.normal(key, dims, jnp.float32)
    if split:
        values = values * steps_of(key, dims, split, -0.22, 0.18)
    return jnp.clip(values, -most, most).astype(kind)


def setup_inputs(seed: int = 0) -> dict:
    streams_of = jax.random.split(jax.random.key(seed), 4)
    return {
        "trailing": bell_draw(streams_of[0], (ROWS, COLS), 1.0, 6.0, ((0, 8), (1, 32))),
        "panel_t": bell_draw(streams_of[1], (NB, ROWS), (2 * NB) ** -0.5, 0.25, ((0, 32), (1, 8))),
        "pivots": draw_pivots(jax.random.fold_in(streams_of[3], 71), 0),
    }


def reference(trailing, panel_t, pivots):

    def swap(i, perm):
        target = pivots[i]
        first = perm[i]
        second = perm[target]
        return perm.at[i].set(second).at[target].set(first)
    perm = lax.fori_loop(0, NB, swap, jnp.arange(ROWS, dtype=jnp.int32))
    swapped = trailing[perm]
    top_block = panel_t[:, :NB].astype(jnp.float32).T
    diag = jnp.tril(top_block, -1) + jnp.eye(NB, dtype=jnp.float32)
    urows = lax.linalg.triangular_solve(diag, swapped[:NB].astype(jnp.float32), left_side=True, lower=True, unit_diagonal=True).astype(jnp.bfloat16)
    product = lax.dot_general(panel_t.astype(jnp.float32), urows.astype(jnp.float32), (((0,), (0,)), ((), ())), preferred_element_type=jnp.float32)
    lower = (swapped.astype(jnp.float32) - product).astype(jnp.bfloat16)
    return jnp.concatenate([urows, lower[NB:]], axis=0)
```

```python
import functools

import jax
import jax.numpy as jnp
from jax import lax
from jax.experimental import pallas as pl
from jax.experimental.pallas import tpu as pltpu
from jax.sharding import PartitionSpec as P

NX = 4
NY = 4
OFFSETS = (0, -1, 1, 2)
HIGHEST = lax.Precision.HIGHEST


def place(x, y, c):
    return ((x % NX) * NY + (y % NY)) * 2 + c


def hop(dx, dy, turn):
    pairs = []
    for x in range(NX):
        for y in range(NY):
            for c in range(2):
                a, b = (dy, dx) if turn and c == 1 else (dx, dy)
                pairs.append((place(x, y, c), place(x + a, y + b, c)))
    return pairs


CORES = [(p, p ^ 1) for p in range(NX * NY * 2)]


def send(block, pairs):
    return lax.ppermute(block, "pcol", pairs)


def pick_kernel(blk, piv_ref, first_ref, trailing_ref, top_ref, out_ref, cnt_ref, lst_ref, rows_ref):
    width = piv_ref.shape[0]
    rows = trailing_ref.shape[0]
    first = first_ref[0]
    for b in range(cnt_ref.shape[0]):
        cnt_ref[b] = 0
    rows_ref[...] = jnp.zeros_like(rows_ref)
    sub = lax.broadcasted_iota(jnp.int32, (16, 128), 0)

    def step(i, carry):
        loc = piv_ref[i] - first

        @pl.when((loc >= 0) & (loc < rows))
        def _():
            b = lax.div(loc, blk)
            k = cnt_ref[b]
            lst_ref[b * width + k] = i
            cnt_ref[b] = k + 1
            base = pl.multiple_of(loc & ~15, 16)
            tile = trailing_ref[pl.ds(base, 16), :].astype(jnp.float32)
            row = jnp.sum(jnp.where(sub == (loc & 15), tile, 0.0), axis=0, keepdims=True)
            rows_ref[pl.ds(i, 1), :] = row

        return carry

    lax.fori_loop(0, width, step, 0)
    out_ref[:width, :] = rows_ref[...].astype(jnp.bfloat16)
    keep = (first == 0).astype(jnp.float32)
    head = trailing_ref[:width, :].astype(jnp.float32)
    out_ref[width : 2 * width, :] = (head * keep).astype(jnp.bfloat16)
    top = top_ref[...].astype(jnp.float32) * keep
    both = jnp.concatenate([top[:, :128], top[:, 128:]], axis=0)
    out_ref[2 * width :, :] = both.astype(jnp.bfloat16)


def pick(trailing, panel_t, pivots, first, blk):
    rows, cols = trailing.shape
    width = pivots.shape[0]
    nblk = rows // blk
    return pl.pallas_call(
        functools.partial(pick_kernel, blk),
        grid=(1,),
        in_specs=[
            pl.BlockSpec(memory_space=pltpu.SMEM),
            pl.BlockSpec(memory_space=pltpu.SMEM),
            pl.BlockSpec((rows, cols), lambda i: (0, 0), pipeline_mode=pl.Buffered(1)),
            pl.BlockSpec((8, width), lambda i: (0, 0)),
        ],
        out_specs=[
            pl.BlockSpec((2 * width + 16, cols), lambda i: (0, 0)),
            pl.BlockSpec(memory_space=pltpu.SMEM),
            pl.BlockSpec(memory_space=pltpu.SMEM),
        ],
        out_shape=[
            jax.ShapeDtypeStruct((2 * width + 16, cols), jnp.bfloat16),
            jax.ShapeDtypeStruct((nblk,), jnp.int32),
            jax.ShapeDtypeStruct((nblk * width,), jnp.int32),
        ],
        scratch_shapes=[pltpu.VMEM((width, cols), jnp.float32)],
        compiler_params=pltpu.CompilerParams(vmem_limit_bytes=24 << 20),
        name="pick",
    )(pivots, first, trailing, panel_t)


def dot(a, b):
    return lax.dot_general(
        a, b, (((1,), (0,)), ((), ())), precision=HIGHEST, preferred_element_type=jnp.float32
    )


def solve_kernel(from_ref, to_ref, own_ref, other_ref, top_ref, nat_ref, perm_ref, a_ref, u_ref):
    n = nat_ref.shape[0]
    half = n // 16
    for b in range(n // 8):
        src = own_ref if b < half else other_ref
        k = (b % half) * 16
        piece = src[k : k + 16, :].astype(jnp.float32)
        at = pl.ds(pl.multiple_of(from_ref[b] * 8, 8), 8)
        a_ref[at, :128] = piece[:8]
        a_ref[at, 128:] = piece[8:]
    r = lax.broadcasted_iota(jnp.int32, (n, n), 0)
    c = lax.broadcasted_iota(jnp.int32, (n, n), 1)
    strict = jnp.where(r > c, a_ref[...].T, 0.0)
    d = jnp.where((r >> 4) == (c >> 4), strict, 0.0)
    x = jnp.where(r == c, 1.0, 0.0) - d
    for _ in range(3):
        d = dot(d, d)
        x = x + dot(x, d)
    for lg in (4, 5, 6, 7):
        inside = ((r >> (lg + 1)) == (c >> (lg + 1))) & ((r >> lg) != (c >> lg))
        x = x - dot(x, dot(jnp.where(inside, strict, 0.0), x))
    u = dot(x, top_ref[...].astype(jnp.float32))
    u = u.astype(jnp.bfloat16).astype(jnp.float32)
    u_ref[...] = u
    nat_ref[...] = u.astype(jnp.bfloat16)
    for b in range(n // 8):
        a_ref[8 * b : 8 * b + 8, :128] = u_ref[pl.ds(pl.multiple_of(to_ref[b] * 8, 8), 8), :]
    perm_ref[...] = a_ref[:, :128].astype(jnp.bfloat16)


def solve(order_l, order_u, own, other, top):
    n, cols = top.shape
    smem = pl.BlockSpec(memory_space=pltpu.SMEM)
    vmem = pl.BlockSpec(memory_space=pltpu.VMEM)
    return pl.pallas_call(
        solve_kernel,
        in_specs=[smem, smem, vmem, vmem, vmem],
        out_specs=[vmem, vmem],
        out_shape=[jax.ShapeDtypeStruct((n, cols), jnp.bfloat16)] * 2,
        scratch_shapes=[pltpu.VMEM((n, n), jnp.float32), pltpu.VMEM((n, cols), jnp.float32)],
        compiler_params=pltpu.CompilerParams(vmem_limit_bytes=24 << 20),
        name="solve",
    )(order_l, order_u, own, other, top)


def update_kernel(nblk, cnt_ref, lst_ref, piv_ref, first_ref, *refs):
    tr_ref, u_ref, nat_ref, disp_ref = refs[:4]
    parts = refs[4:14]
    out_ref, acc_ref, drow_ref = refs[14:]
    blk = tr_ref.shape[0]
    width = nat_ref.shape[0]
    b = pl.program_id(0)
    first = first_ref[0]

    @pl.when(b == 0)
    def _():
        drow_ref[...] = disp_ref[...].astype(jnp.float32)

    early = b < nblk // 2
    pieces = []
    for s in (parts[:5], parts[5:]):
        pieces += [s[0][...], s[1][...], s[2][...], jnp.where(early, s[3][...], s[4][...])]
    panel = jnp.concatenate(pieces, axis=0)
    acc_ref[...] = lax.dot_general(
        panel, u_ref[...], (((0,), (0,)), ((), ())), preferred_element_type=jnp.float32
    )
    out_ref[...] = (tr_ref[...].astype(jnp.float32) - acc_ref[...]).astype(jnp.bfloat16)
    sub = lax.broadcasted_iota(jnp.int32, (16, 128), 0)

    def fix(k, carry):
        i = lst_ref[b * width + k]
        loc = piv_ref[i] - first - b * blk
        at = pl.ds(pl.multiple_of(loc & ~15, 16), 16)
        new = drow_ref[pl.ds(i, 1), :] - acc_ref[at, :]
        old = out_ref[at, :].astype(jnp.float32)
        out_ref[at, :] = jnp.where(sub == (loc & 15), new, old).astype(jnp.bfloat16)
        return carry

    lax.fori_loop(0, cnt_ref[b], fix, 0)

    @pl.when((b == 0) & (first == 0))
    def _():
        out_ref[:width, :] = nat_ref[...]


def update(cnt, lst, pivots, first, trailing, u, nat, disp, own, other, blk):
    rows, cols = trailing.shape
    width = nat.shape[0]
    nblk = rows // blk
    hb = nblk // 2

    def whole(shape):
        return pl.BlockSpec(shape, lambda b, *_: (0, 0))

    tall = pl.BlockSpec((blk, cols), lambda b, *_: (b, 0))
    wide = pl.BlockSpec((32, blk), lambda b, *_: (0, b))
    low = pl.BlockSpec((32, blk), lambda b, *_: (0, jnp.minimum(b, hb - 1)))
    high = pl.BlockSpec((32, blk), lambda b, *_: (0, jnp.maximum(b - hb, 0)))
    group = [wide, wide, wide, low, high]
    return pl.pallas_call(
        functools.partial(update_kernel, nblk),
        grid_spec=pltpu.PrefetchScalarGridSpec(
            num_scalar_prefetch=4,
            grid=(nblk,),
            in_specs=[tall, whole((width, cols)), whole((width, cols)), whole((width, cols))]
            + group
            + group,
            out_specs=tall,
            scratch_shapes=[
                pltpu.VMEM((blk, cols), jnp.float32),
                pltpu.VMEM((width, cols), jnp.float32),
            ],
        ),
        out_shape=jax.ShapeDtypeStruct((rows, cols), jnp.bfloat16),
        compiler_params=pltpu.CompilerParams(vmem_limit_bytes=32 << 20),
        name="update",
    )(cnt, lst, pivots, first, trailing, u, nat, disp, *own, *other)


def around(block, hops):
    return jnp.concatenate([block] + [send(block, h) for h in hops], axis=0)


def body(trailing, panel_t, pivots):
    rows = trailing.shape[0]
    width = pivots.shape[0]
    blk = rows // 12
    first = (lax.axis_index("prow") * rows).astype(jnp.int32).reshape(1)
    me = lax.axis_index("pcol")
    mx, my, mc = me // (NY * 2), (me // 2) % NY, me % 2

    block = around(panel_t, [hop(1, 0, True), hop(-1, 0, True), hop(2, 0, True)])
    up, down = hop(0, 1, True), hop(0, -1, True)
    half = rows // 2
    near, far = send(block, up), send(block, down)
    own = [block, near, far, send(near[:, :half], up), send(far[:, half:], down)]
    other = [send(t, CORES) for t in own]

    load, cnt, lst = pick(trailing, panel_t, pivots, first, blk)
    nz = lax.axis_size("prow")
    for d in (1, 2, 4):
        load = load + lax.ppermute(load, "prow", [(i, i ^ d) for i in range(nz)])
    top, disp, diag = load[:width], load[width : 2 * width], load[2 * width :]
    diag = around(diag, [hop(1, 0, False), hop(-1, 0, False), hop(2, 0, False)])
    diag = around(diag, [hop(0, 1, False), hop(0, -1, False), hop(0, 2, False)])
    diag_other = send(diag, CORES)

    offs = jnp.array(OFFSETS, jnp.int32)
    outer = jnp.repeat(offs, 4)
    inner = jnp.tile(offs, 4)
    order_l = jnp.concatenate([place(mx + inner, my + outer, mc), place(mx + inner, my + outer, 1 - mc)])
    cross = [place(mx + inner, my + outer, 0), place(mx + outer, my + inner, 1)]
    order_u = jnp.concatenate(
        [jnp.where(mc == 0, cross[0], cross[1]), jnp.where(mc == 0, cross[1], cross[0])]
    )
    nat, perm = solve(order_l.astype(jnp.int32), order_u.astype(jnp.int32), diag, diag_other, top)
    return update(cnt, lst, pivots, first, trailing, perm, nat, disp, own, other, blk)


def solution(mesh):
    return jax.shard_map(
        body,
        mesh=mesh,
        in_specs=(P("prow", "pcol"), P("pcol", "prow"), P()),
        out_specs=P("prow", "pcol"),
        check_vma=False,
    )
```

```python
import functools

import jax
import jax.numpy as jnp
from jax import lax
from jax.experimental import pallas as pl
from jax.experimental.pallas import tpu as pltpu
from jax.sharding import PartitionSpec as P

NX = 4
NY = 4
OFFSETS = (0, -1, 1, 2)
NBLK = 12
UPD_LIMIT = 16 << 20
SMEM = pl.BlockSpec(memory_space=pltpu.SMEM)
VMEM = pl.BlockSpec(memory_space=pltpu.VMEM)
HIGHEST = lax.Precision.HIGHEST


def place(x, y, c):
    return ((x % NX) * NY + (y % NY)) * 2 + c


def hop(dx, dy, turn):
    pairs = []
    for x in range(NX):
        for y in range(NY):
            for c in range(2):
                a, b = (dy, dx) if turn and c == 1 else (dx, dy)
                pairs.append((place(x, y, c), place(x + a, y + b, c)))
    return pairs


CORES = [(p, p ^ 1) for p in range(NX * NY * 2)]


def send(block, pairs):
    return lax.ppermute(block, "pcol", pairs)


def pick_kernel(blk, piv_ref, first_ref, trailing_ref, out_ref, copy_ref, cnt_ref, lst_ref, own_ref, rows_ref, sem):
    width = piv_ref.shape[0]
    rows = trailing_ref.shape[0]
    first = first_ref[0]
    copy = pltpu.make_async_copy(trailing_ref, copy_ref, sem)
    copy.start()
    for b in range(cnt_ref.shape[0]):
        cnt_ref[b] = 0

    def filt(i, n):
        loc = piv_ref[i] - first
        own_ref[n] = i
        return n + ((loc >= 0) & (loc < rows)).astype(jnp.int32)

    n = lax.fori_loop(0, width, filt, 0, unroll=8)

    def bucket(k, carry):
        i = own_ref[k]
        b = lax.div(piv_ref[i] - first, blk)
        m = cnt_ref[b]
        lst_ref[b * width + m] = i
        cnt_ref[b] = m + 1
        return carry

    lax.fori_loop(0, n, bucket, 0)
    rows_ref[...] = jnp.zeros_like(rows_ref)
    sub = lax.broadcasted_iota(jnp.int32, (16, 128), 0)
    copy.wait()

    def extract(k, carry):
        i = own_ref[k]
        loc = piv_ref[i] - first
        base = pl.multiple_of(loc & ~15, 16)
        tile = copy_ref[pl.ds(base, 16), :].astype(jnp.float32)
        row = jnp.sum(jnp.where(sub == (loc & 15), tile, 0.0), axis=0, keepdims=True)
        rows_ref[pl.ds(i, 1), :] = row
        return carry

    lax.fori_loop(0, n, extract, 0)
    out_ref[:width, :] = rows_ref[...].astype(jnp.bfloat16)
    keep = jnp.where(first == 0, 1.0, 0.0)
    out_ref[width:, :] = (copy_ref[:width, :].astype(jnp.float32) * keep).astype(jnp.bfloat16)


def pick(trailing, pivots, first, blk):
    rows, cols = trailing.shape
    width = pivots.shape[0]
    nblk = rows // blk
    return pl.pallas_call(
        functools.partial(pick_kernel, blk),
        in_specs=[SMEM, SMEM, pl.BlockSpec(memory_space=pltpu.HBM)],
        out_specs=[VMEM, VMEM, SMEM, SMEM],
        out_shape=[
            jax.ShapeDtypeStruct((2 * width, cols), jnp.bfloat16),
            jax.ShapeDtypeStruct((rows, cols), jnp.bfloat16),
            jax.ShapeDtypeStruct((nblk,), jnp.int32),
            jax.ShapeDtypeStruct((nblk * width,), jnp.int32),
        ],
        scratch_shapes=[
            pltpu.SMEM((width + 8,), jnp.int32),
            pltpu.VMEM((width, cols), jnp.float32),
            pltpu.SemaphoreType.DMA,
        ],
        compiler_params=pltpu.CompilerParams(vmem_limit_bytes=12 << 20),
        name="pick",
    )(pivots, first, pltpu.with_memory_space_constraint(trailing, pltpu.HBM))


def dot(a, b):
    return lax.dot_general(
        a, b, (((1,), (0,)), ((), ())), precision=HIGHEST, preferred_element_type=jnp.float32
    )


def dot_exact(a, b):
    n = b.shape[1]
    hi = b.astype(jnp.bfloat16)
    rest = b - hi.astype(jnp.float32)
    mid = rest.astype(jnp.bfloat16)
    low = (rest - mid.astype(jnp.float32)).astype(jnp.bfloat16)
    r = lax.dot_general(
        a, jnp.concatenate([hi, mid, low], axis=1), (((1,), (0,)), ((), ())),
        preferred_element_type=jnp.float32,
    )
    return r[:, 2 * n :] + r[:, n : 2 * n] + r[:, :n]


def unit_inverse(strict):
    n = strict.shape[0]
    r = lax.broadcasted_iota(jnp.int32, (n, n), 0)
    c = lax.broadcasted_iota(jnp.int32, (n, n), 1)
    d = jnp.where((r >> 4) == (c >> 4), strict, 0.0)
    x = jnp.where(r == c, 1.0, 0.0) - d
    for step in range(3):
        d = dot_exact(d.astype(jnp.bfloat16), d) if step == 0 else dot(d, d)
        x = x + dot(x, d)
    for lg in (4, 5, 6):
        inside = ((r >> (lg + 1)) == (c >> (lg + 1))) & ((r >> lg) != (c >> lg))
        part = jnp.where(inside, strict, 0.0).astype(jnp.bfloat16)
        x = x - dot(x, dot_exact(part, x))
    return x


def solve_kernel(me_ref, own_ref, other_ref, top_ref, nat_ref, perm_ref, a_ref, u_ref):
    n = nat_ref.shape[0]
    h = n // 2
    me = me_ref[0]
    mx, my, mc = me >> 3, (me >> 1) & 3, me & 1

    def at(x, y, c):
        p = (((x & 3) << 2) + (y & 3)) * 2 + c
        return pl.ds(pl.multiple_of(p * 8, 8), 8)

    blocks = [(k, outer, inner) for k in range(2) for outer in OFFSETS for inner in OFFSETS]
    for b, (k, outer, inner) in enumerate(blocks):
        src = other_ref if k else own_ref
        t = (b % 16) * 16
        piece = src[t : t + 16, :].astype(jnp.float32)
        to = at(mx + inner, my + outer, mc ^ k)
        a_ref[to, :h] = piece[:8]
        a_ref[to, h:] = piece[8:]
    r = lax.broadcasted_iota(jnp.int32, (h, h), 0)
    c = lax.broadcasted_iota(jnp.int32, (h, h), 1)
    s11 = jnp.where(r > c, a_ref[:h, :h].T, 0.0)
    s22 = jnp.where(r > c, a_ref[h:, h:].T, 0.0)
    s21 = a_ref[:h, h:].T
    x1 = unit_inverse(s11)
    x2 = unit_inverse(s22)
    u1 = dot(x1, top_ref[:h, :].astype(jnp.float32))
    u2 = dot(x2, top_ref[h:, :].astype(jnp.float32) - dot_exact(s21.astype(jnp.bfloat16), u1))
    u = jnp.concatenate([u1, u2], axis=0).astype(jnp.bfloat16)
    nat_ref[...] = u
    u_ref[...] = u.astype(jnp.float32)
    for b, (k, outer, inner) in enumerate(blocks):
        core = mc ^ k
        dx = jnp.where(core == 0, inner, outer)
        dy = jnp.where(core == 0, outer, inner)
        a_ref[8 * b : 8 * b + 8, :h] = u_ref[at(mx + dx, my + dy, core), :]
    perm_ref[...] = a_ref[:, :h].astype(jnp.bfloat16)


def solve(me, own, other, top):
    n, cols = top.shape
    return pl.pallas_call(
        solve_kernel,
        in_specs=[SMEM, VMEM, VMEM, VMEM],
        out_specs=[VMEM, VMEM],
        out_shape=[jax.ShapeDtypeStruct((n, cols), jnp.bfloat16)] * 2,
        scratch_shapes=[pltpu.VMEM((n, n), jnp.float32), pltpu.VMEM((n, cols), jnp.float32)],
        compiler_params=pltpu.CompilerParams(vmem_limit_bytes=12 << 20),
        name="solve",
    )(me, own, other, top)


def update_kernel(nblk, cnt_ref, lst_ref, piv_ref, first_ref, tr_ref, u_ref, nat_ref, disp_ref, *refs):
    parts = refs[:10]
    out_ref, acc_ref, drow_ref = refs[10:]
    blk = out_ref.shape[0]
    width = nat_ref.shape[0]
    b = pl.program_id(0)
    first = first_ref[0]

    @pl.when(b == 0)
    def _():
        drow_ref[...] = disp_ref[...].astype(jnp.float32)

    def cols(start):
        return pl.ds(pl.multiple_of(start, 128), blk)

    def compute(s, late):
        here = cols(b * blk)
        there = cols(b * blk - (nblk // 2) * blk) if late else here
        pieces = []
        for s in (parts[:5], parts[5:]):
            pieces += [s[0][:, here], s[1][:, here], s[2][:, here], s[3 + late][:, there]]
        acc_ref[...] = lax.dot_general(
            jnp.concatenate(pieces, axis=0), u_ref[...], (((0,), (0,)), ((), ())),
            preferred_element_type=jnp.float32,
        )

    @pl.when(b < nblk // 2)
    def _():
        compute(parts, 0)

    @pl.when(b >= nblk // 2)
    def _():
        compute(parts, 1)

    tr = tr_ref[pl.ds(pl.multiple_of(b * blk, 16), blk), :].astype(jnp.float32)
    out_ref[...] = (tr - acc_ref[...]).astype(jnp.bfloat16)
    sub = lax.broadcasted_iota(jnp.int32, (16, 128), 0)

    def fix(k, carry):
        i = lst_ref[b * width + k]
        loc = piv_ref[i] - first - b * blk
        at = pl.ds(pl.multiple_of(loc & ~15, 16), 16)
        new = drow_ref[pl.ds(i, 1), :] - acc_ref[at, :]
        old = out_ref[at, :].astype(jnp.float32)
        out_ref[at, :] = jnp.where(sub == (loc & 15), new, old).astype(jnp.bfloat16)
        return carry

    lax.fori_loop(0, cnt_ref[b], fix, 0)

    @pl.when((b == 0) & (first == 0))
    def _():
        out_ref[:width, :] = nat_ref[...]


def update(cnt, lst, pivots, first, trailing, u, nat, disp, own, other, blk):
    rows, cols = trailing.shape
    width = nat.shape[0]
    nblk = rows // blk
    return pl.pallas_call(
        functools.partial(update_kernel, nblk),
        grid=(nblk,),
        in_specs=[SMEM] * 4 + [VMEM] * 14,
        out_specs=pl.BlockSpec((blk, cols), lambda b: (b, 0)),
        scratch_shapes=[
            pltpu.VMEM((blk, cols), jnp.float32),
            pltpu.VMEM((width, cols), jnp.float32),
        ],
        out_shape=jax.ShapeDtypeStruct((rows, cols), jnp.bfloat16),
        compiler_params=pltpu.CompilerParams(vmem_limit_bytes=UPD_LIMIT),
        name="update",
    )(cnt, lst, pivots, first, trailing, u, nat, disp, *own, *other)


def after(x, *deps):
    return lax.optimization_barrier((x,) + deps)[0]


def body(trailing, panel_t, pivots):
    rows = trailing.shape[0]
    width = pivots.shape[0]
    blk = rows // NBLK
    half = rows // 2
    nz = lax.axis_size("prow")
    zi = lax.axis_index("prow")
    first = (zi * rows).astype(jnp.int32).reshape(1)
    me = lax.axis_index("pcol")

    def around(x, hops):
        return jnp.concatenate([x] + [send(x, h) for h in hops], axis=0)

    def zsend(x, pairs):
        return lax.ppermute(x, "prow", pairs)

    def shift(k):
        return [(i, (i + k) % nz) for i in range(nz)]

    hops = [hop(1, 0, True), hop(-1, 0, True), hop(2, 0, True)]
    first_hops = [send(panel_t, h) for h in hops]

    diag = panel_t[:, :width]
    diag = jnp.concatenate([diag[:, :128], diag[:, 128:]], axis=0)
    diag = jnp.where(zi == 0, diag, jnp.zeros_like(diag))

    def spread(x, d):
        return x + zsend(x, [(i, i + d) for i in range(0, nz, 2 * d)])

    diag = spread(diag, 4)
    load, copy, cnt, lst = pick(trailing, pivots, first, blk)
    diag = spread(diag, 2)

    diag, load, p, m, q = lax.optimization_barrier((diag, load, *first_hops))
    block = jnp.concatenate([panel_t, p, m, q], axis=0)
    up, down = hop(0, 1, True), hop(0, -1, True)
    near, far = send(block, up), send(block, down)

    diag, load = lax.optimization_barrier((diag, load, block))[:2]
    diag = spread(diag, 1)
    a, b = zsend(load, shift(1)), zsend(load, shift(-1))
    diag = around(diag, [hop(1, 0, False), hop(-1, 0, False), hop(2, 0, False)])
    load = jnp.where(load != 0, load, jnp.where(a != 0, a, b))
    load = after(load, diag)
    a, b = zsend(load, shift(3)), zsend(load, shift(-3))
    diag = around(diag, [hop(0, 1, False), hop(0, -1, False), hop(0, 2, False)])
    diag, near, far = lax.optimization_barrier((diag, near, far))
    own = [block, near, far, send(near[:, :half], up), send(far[:, half:], down)]
    diag_other = send(diag, CORES)
    load = jnp.where(load != 0, load, jnp.where(a != 0, a, b))
    top, disp = load[:width], load[width:]
    other = [send(t, CORES) for t in own]
    nat, perm = solve(me.astype(jnp.int32).reshape(1), diag, diag_other, top)
    return update(cnt, lst, pivots, first, copy, perm, nat, disp, own, other, blk)


def solution(mesh):
    return jax.shard_map(
        body,
        mesh=mesh,
        in_specs=(P("prow", "pcol"), P("pcol", "prow"), P()),
        out_specs=P("prow", "pcol"),
        check_vma=False,
    )
```

```python
import functools

import jax
import jax.numpy as jnp
from jax import lax
from jax.experimental import pallas as pl
from jax.experimental.pallas import tpu as pltpu
from jax.sharding import PartitionSpec as P

NX = 4
NY = 4
OFFSETS = (0, -1, 1, 2)
NBLK = 12
SMEM = pl.BlockSpec(memory_space=pltpu.SMEM)
VMEM = pl.BlockSpec(memory_space=pltpu.VMEM)
HIGHEST = lax.Precision.HIGHEST


def place(x, y, c):
    return ((x % NX) * NY + (y % NY)) * 2 + c


def hop(dx, dy, turn):
    pairs = []
    for x in range(NX):
        for y in range(NY):
            for c in range(2):
                a, b = (dy, dx) if turn and c == 1 else (dx, dy)
                pairs.append((place(x, y, c), place(x + a, y + b, c)))
    return pairs


CORES = [(p, p ^ 1) for p in range(NX * NY * 2)]


def send(block, pairs):
    return lax.ppermute(block, "pcol", pairs)


def params(mib):
    return pltpu.CompilerParams(vmem_limit_bytes=mib << 20)


def cost(us):
    return pl.CostEstimate(flops=int(us * 1.1e9), bytes_accessed=int(us * 3.5e6), transcendentals=0)


def stack_kernel(*refs):
    refs[-1][...] = jnp.concatenate([r[...] for r in refs[:-1]], axis=0)


def stack(parts, start, cols, name):
    rows = sum(p.shape[0] for p in parts)
    step = min(cols, 4096)
    return pl.pallas_call(
        stack_kernel,
        grid=(cols // step,),
        in_specs=[pl.BlockSpec((p.shape[0], step), lambda i: (0, i + start // step)) for p in parts],
        out_specs=pl.BlockSpec((rows, step), lambda i: (0, i)),
        out_shape=jax.ShapeDtypeStruct((rows, cols), jnp.bfloat16),
        compiler_params=params(6),
        name=name,
    )(*parts)


def add_kernel(a_ref, b_ref, out_ref):
    out_ref[...] = (a_ref[...].astype(jnp.float32) + b_ref[...].astype(jnp.float32)).astype(jnp.bfloat16)


def add(a, b):
    return pl.pallas_call(
        add_kernel,
        in_specs=[VMEM, VMEM],
        out_specs=VMEM,
        out_shape=jax.ShapeDtypeStruct(a.shape, a.dtype),
        compiler_params=params(2),
        name="add",
    )(a, b)


def choose_kernel(limit, first_ref, a_ref, b_ref, out_ref):
    @pl.when(first_ref[0] < limit)
    def _():
        out_ref[...] = a_ref[...]

    @pl.when(first_ref[0] >= limit)
    def _():
        out_ref[...] = b_ref[...]


def choose(first, limit, a, b):
    return pl.pallas_call(
        functools.partial(choose_kernel, limit),
        in_specs=[SMEM, VMEM, VMEM],
        out_specs=VMEM,
        out_shape=jax.ShapeDtypeStruct(a.shape, a.dtype),
        compiler_params=params(2),
        name="choose",
    )(first, a, b)


def pick_kernel(blk, piv_ref, first_ref, trailing_ref, out_ref, cnt_ref, lst_ref, own_ref, group_ref, rows_ref, sem):
    width = piv_ref.shape[0]
    rows = trailing_ref.shape[0]
    first = first_ref[0]
    nblk = cnt_ref.shape[0]
    for b in range(nblk):
        cnt_ref[b] = 0

    def filt(i, n):
        loc = piv_ref[i] - first
        own_ref[n] = i
        return n + ((loc >= 0) & (loc < rows)).astype(jnp.int32)

    n = lax.fori_loop(0, width, filt, 0, unroll=8)

    def group(k):
        loc = piv_ref[own_ref[k]] - first
        base = pl.multiple_of(loc & ~15, 16)
        return pltpu.make_async_copy(trailing_ref.at[pl.ds(base, 16)], group_ref.at[k], sem)

    def begin(k, carry):
        group(k).start()
        i = own_ref[k]
        b = lax.div(piv_ref[i] - first, blk)
        m = cnt_ref[b]
        lst_ref[b * width + m] = i
        cnt_ref[b] = m + 1
        return carry

    def finish(k, carry):
        group(k).wait()
        return carry

    lax.fori_loop(0, n, begin, 0)
    rows_ref[...] = jnp.zeros_like(rows_ref)
    lax.fori_loop(0, n, finish, 0)
    sub = lax.broadcasted_iota(jnp.int32, (16, 128), 0)

    def extract(k, carry):
        i = own_ref[k]
        loc = piv_ref[i] - first
        tile = group_ref[k].astype(jnp.float32)
        row = jnp.sum(jnp.where(sub == (loc & 15), tile, 0.0), axis=0, keepdims=True)
        rows_ref[pl.ds(i, 1), :] = row
        return carry

    lax.fori_loop(0, n, extract, 0)
    out_ref[...] = rows_ref[...].astype(jnp.bfloat16)


def pick(trailing, pivots, first, blk):
    rows, cols = trailing.shape
    width = pivots.shape[0]
    nblk = rows // blk
    return pl.pallas_call(
        functools.partial(pick_kernel, blk),
        in_specs=[SMEM, SMEM, pl.BlockSpec(memory_space=pltpu.HBM)],
        out_specs=[VMEM, SMEM, SMEM],
        out_shape=[
            jax.ShapeDtypeStruct((width, cols), jnp.bfloat16),
            jax.ShapeDtypeStruct((nblk,), jnp.int32),
            jax.ShapeDtypeStruct((nblk * width,), jnp.int32),
        ],
        scratch_shapes=[
            pltpu.SMEM((width + 8,), jnp.int32),
            pltpu.VMEM((width, 16, cols), jnp.bfloat16),
            pltpu.VMEM((width, cols), jnp.float32),
            pltpu.SemaphoreType.DMA,
        ],
        compiler_params=params(6),
        cost_estimate=cost(12),
        name="pick",
    )(pivots, first, trailing)


def dot(a, b):
    return lax.dot_general(
        a, b, (((1,), (0,)), ((), ())), precision=HIGHEST, preferred_element_type=jnp.float32
    )


def dot_exact(a, b):
    n = b.shape[1]
    hi = b.astype(jnp.bfloat16)
    rest = b - hi.astype(jnp.float32)
    mid = rest.astype(jnp.bfloat16)
    low = (rest - mid.astype(jnp.float32)).astype(jnp.bfloat16)
    r = lax.dot_general(
        a, jnp.concatenate([hi, mid, low], axis=1), (((1,), (0,)), ((), ())),
        preferred_element_type=jnp.float32,
    )
    return r[:, 2 * n :] + r[:, n : 2 * n] + r[:, :n]


def unit_inverse(strict):
    n = strict.shape[0]
    r = lax.broadcasted_iota(jnp.int32, (n, n), 0)
    c = lax.broadcasted_iota(jnp.int32, (n, n), 1)
    d = jnp.where((r >> 4) == (c >> 4), strict, 0.0)
    x = jnp.where(r == c, 1.0, 0.0) - d
    for step in range(3):
        d = dot_exact(d.astype(jnp.bfloat16), d) if step == 0 else dot(d, d)
        x = x + dot(x, d)
    for lg in (4, 5, 6):
        inside = ((r >> (lg + 1)) == (c >> (lg + 1))) & ((r >> lg) != (c >> lg))
        part = jnp.where(inside, strict, 0.0).astype(jnp.bfloat16)
        x = x - dot(x, dot_exact(part, x))
    return x


def blocks():
    return [(k, outer, inner) for k in range(2) for outer in OFFSETS for inner in OFFSETS]


def block_at(me, k, outer, inner):
    core = (me & 1) ^ k
    dx = jnp.where(core == 0, inner, outer)
    dy = jnp.where(core == 0, outer, inner)
    x = ((me >> 3) + dx) & 3
    y = ((me >> 1) + dy) & 3
    return pl.ds(pl.multiple_of(((x * 4 + y) * 2 + core) * 8, 8), 8)


def solve_kernel(me_ref, own_ref, other_ref, top_ref, more_ref, head_ref, out_ref, a_ref, g_ref):
    n = top_ref.shape[0]
    h = n // 2
    me = me_ref[0]
    g_ref[:h, :] = own_ref[...].astype(jnp.float32)
    g_ref[h:, :] = other_ref[...].astype(jnp.float32)
    for b, where in enumerate(blocks()):
        a_ref[block_at(me, *where), :] = g_ref[8 * b : 8 * b + 8, :]
    r = lax.broadcasted_iota(jnp.int32, (h, h), 0)
    c = lax.broadcasted_iota(jnp.int32, (h, h), 1)
    s11 = jnp.where(r > c, a_ref[:h, :h].T, 0.0)
    s22 = jnp.where(r > c, a_ref[h:, h:].T, 0.0)
    s21 = a_ref[:h, h:].T
    x1 = unit_inverse(s11)
    x2 = unit_inverse(s22)
    top = top_ref[...].astype(jnp.float32) + more_ref[...].astype(jnp.float32)
    u1 = dot(x1, top[:h])
    u2 = dot(x2, top[h:] - dot_exact(s21.astype(jnp.bfloat16), u1))
    out_ref[:n, :] = jnp.concatenate([u1, u2], axis=0).astype(jnp.bfloat16)
    out_ref[n:, :] = head_ref[...]


def solve(me, own, other, top, more, trailing):
    n, cols = top.shape
    whole = pl.BlockSpec((n // 2, n), lambda i: (0, 0))
    tall = pl.BlockSpec((n, cols), lambda i: (0, 0))
    return pl.pallas_call(
        solve_kernel,
        grid=(1,),
        in_specs=[SMEM, whole, whole, tall, tall, tall],
        out_specs=pl.BlockSpec((2 * n, cols), lambda i: (0, 0)),
        out_shape=jax.ShapeDtypeStruct((2 * n, cols), jnp.bfloat16),
        scratch_shapes=[pltpu.VMEM((n, n), jnp.float32), pltpu.VMEM((n, n), jnp.float32)],
        compiler_params=params(10),
        cost_estimate=cost(20),
        name="solve",
    )(me, own, other, top, more, trailing)


def update_kernel(nblk, late, cnt_ref, lst_ref, piv_ref, first_ref, me_ref, tr_ref, ud_ref, rest_ref, *refs):
    parts = refs[:16]
    out_ref, acc_ref, nat_ref, drow_ref, u_ref, tmp_ref = refs[16:]
    blk = out_ref.shape[0]
    width = nat_ref.shape[0]
    b = pl.program_id(0)
    first = first_ref[0]

    @pl.when(b == 0)
    def _():
        @pl.when(first < late)
        def _():
            nat_ref[...] = ud_ref[:width, :].astype(jnp.float32)
            drow_ref[...] = ud_ref[width:, :].astype(jnp.float32)

        @pl.when(first >= late)
        def _():
            nat_ref[...] = rest_ref[:width, :].astype(jnp.float32)
            drow_ref[...] = rest_ref[width:, :].astype(jnp.float32)

        for i, where in enumerate(blocks()):
            tmp_ref[8 * i : 8 * i + 8, :] = nat_ref[block_at(me_ref[0], *where), :]
        u_ref[...] = tmp_ref[...].astype(jnp.bfloat16)

    def compute(half):
        here = pl.ds(pl.multiple_of((b - half * (nblk // 2)) * blk, 128), blk)
        pieces = [r[:, here] for r in parts[half::2]]
        acc_ref[...] = lax.dot_general(
            jnp.concatenate(pieces, axis=0), u_ref[...], (((0,), (0,)), ((), ())),
            preferred_element_type=jnp.float32,
        )

    @pl.when(b < nblk // 2)
    def _():
        compute(0)

    @pl.when(b >= nblk // 2)
    def _():
        compute(1)

    out_ref[...] = (tr_ref[...].astype(jnp.float32) - acc_ref[...]).astype(jnp.bfloat16)
    sub = lax.broadcasted_iota(jnp.int32, (16, 128), 0)

    def fix(k, carry):
        i = lst_ref[b * width + k]
        loc = piv_ref[i] - first - b * blk
        at = pl.ds(pl.multiple_of(loc & ~15, 16), 16)
        new = drow_ref[pl.ds(i, 1), :] - acc_ref[at, :]
        old = out_ref[at, :].astype(jnp.float32)
        out_ref[at, :] = jnp.where(sub == (loc & 15), new, old).astype(jnp.bfloat16)
        return carry

    lax.fori_loop(0, cnt_ref[b], fix, 0)

    @pl.when((b == 0) & (first == 0))
    def _():
        out_ref[:width, :] = nat_ref[...].astype(jnp.bfloat16)


def update(cnt, lst, pivots, first, me, trailing, ud, rest, parts, blk):
    rows, cols = trailing.shape
    width = pivots.shape[0]
    nblk = rows // blk
    tall = pl.BlockSpec((blk, cols), lambda b: (b, 0))
    pair = pl.BlockSpec((2 * width, cols), lambda b: (0, 0))
    return pl.pallas_call(
        functools.partial(update_kernel, nblk, 4 * rows),
        grid=(nblk,),
        in_specs=[SMEM] * 5 + [tall, pair, pair] + [VMEM] * 16,
        out_specs=tall,
        scratch_shapes=[
            pltpu.VMEM((blk, cols), jnp.float32),
            pltpu.VMEM((width, cols), jnp.float32),
            pltpu.VMEM((width, cols), jnp.float32),
            pltpu.VMEM((width, cols), jnp.bfloat16),
            pltpu.VMEM((width, cols), jnp.float32),
        ],
        out_shape=jax.ShapeDtypeStruct((rows, cols), jnp.bfloat16),
        compiler_params=params(12),
        name="update",
    )(cnt, lst, pivots, first, me, trailing, ud, rest, *parts)


def body(trailing, panel_t, pivots):
    rows = trailing.shape[0]
    width = pivots.shape[0]
    blk = rows // NBLK
    half = rows // 2
    barrier = lax.optimization_barrier
    first = (lax.axis_index("prow") * rows).astype(jnp.int32).reshape(1)
    me = lax.axis_index("pcol").astype(jnp.int32).reshape(1)
    trailing = pltpu.with_memory_space_constraint(trailing, pltpu.HBM)

    def zsend(x, pairs):
        return lax.ppermute(x, "prow", pairs)

    p, m, q = [send(panel_t, hop(d, 0, True)) for d in (1, -1, 2)]

    top, cnt, lst = pick(trailing, pivots, first, blk)
    p, m, q, top = barrier((p, m, q, top))
    more = zsend(top, [(i + 4, i) for i in range(4)])

    up, down, across = hop(0, 1, True), hop(0, -1, True), hop(0, 2, True)
    diag = stack([panel_t, p, m, q], 0, width, "stack_d")
    diag_q, diag_m = send(diag, across), send(diag, down)
    p, m, q, diag_q = barrier((p, m, q, diag_q))
    xa = stack([panel_t, p, m, q], 0, half, "stack_a")
    p, m, q, diag_m, xa = barrier((p, m, q, diag_m, xa))
    xb = stack([panel_t, p, m, q], half, half, "stack_b")
    pa, mb = send(xa, up), send(xb, down)
    top = add(top, more)
    xa, xb, top = barrier((xa, xb, top))
    pb, ma = send(xb, up), send(xa, down)
    more = zsend(top, [(2, 0), (3, 1)])
    oxa, oxb = send(xa, CORES), send(xb, CORES)
    pa, mb, diag_q, diag_m = barrier((pa, mb, diag_q, diag_m))
    qa, qb = send(pa, up), send(mb, down)
    own = stack([diag, pa, diag_m, diag_q], 0, width, "stack_l")
    other = send(own, CORES)
    opa, omb = send(pa, CORES), send(mb, CORES)
    top = add(top, more)
    more = zsend(top, [(1, 0)])

    other, pb, ma = barrier((other, pb, ma))
    ud = solve(me, own, other, top, more, trailing)
    opb, oma = send(pb, CORES), send(ma, CORES)
    ud = choose(first, rows, ud, zsend(ud, [(0, 1)]))
    ud, qa, qb = barrier((ud, qa, qb))
    oqa, oqb = send(qa, CORES), send(qb, CORES)
    ud = choose(first, 2 * rows, ud, zsend(ud, [(0, 2), (1, 3)]))
    rest = zsend(ud, [(i, i + 4) for i in range(4)])

    parts = [xa, xb, pa, pb, ma, mb, qa, qb, oxa, oxb, opa, opb, oma, omb, oqa, oqb]
    return update(cnt, lst, pivots, first, me, trailing, ud, rest, parts, blk)


def solution(mesh):
    return jax.shard_map(
        body,
        mesh=mesh,
        in_specs=(P("prow", "pcol"), P("pcol", "prow"), P()),
        out_specs=P("prow", "pcol"),
        check_vma=False,
    )
```

```python
import functools

import jax
import jax.numpy as jnp
from jax import lax
from jax.experimental import pallas as pl
from jax.experimental.pallas import tpu as pltpu
from jax.sharding import PartitionSpec as P

NX = 4
NY = 4
OFFSETS = (0, -1, 1, 2)
NBLK = 6
SMEM = pl.BlockSpec(memory_space=pltpu.SMEM)
VMEM = pl.BlockSpec(memory_space=pltpu.VMEM)
HIGHEST = lax.Precision.HIGHEST


def place(x, y, c):
    return ((x % NX) * NY + (y % NY)) * 2 + c


def hop(dx, dy, turn):
    pairs = []
    for x in range(NX):
        for y in range(NY):
            for c in range(2):
                a, b = (dy, dx) if turn and c == 1 else (dx, dy)
                pairs.append((place(x, y, c), place(x + a, y + b, c)))
    return pairs


CORES = [(p, p ^ 1) for p in range(NX * NY * 2)]


def send(block, pairs):
    return lax.ppermute(block, "pcol", pairs)


def params(mib):
    return pltpu.CompilerParams(vmem_limit_bytes=mib << 20)


def cost(us):
    return pl.CostEstimate(flops=int(us * 1.1e9), bytes_accessed=int(us * 3.5e6), transcendentals=0)


def stack_kernel(*refs):
    refs[-1][...] = jnp.concatenate([r[...] for r in refs[:-1]], axis=0)


def stack(parts, start, cols, name, us=1):
    rows = sum(p.shape[0] for p in parts)
    step = min(cols, 4096)
    return pl.pallas_call(
        stack_kernel,
        grid=(cols // step,),
        in_specs=[pl.BlockSpec((p.shape[0], step), lambda i: (0, i + start // step)) for p in parts],
        out_specs=pl.BlockSpec((rows, step), lambda i: (0, i)),
        out_shape=jax.ShapeDtypeStruct((rows, cols), jnp.bfloat16),
        compiler_params=params(6),
        cost_estimate=cost(us),
        name=name,
    )(*parts)


def add_kernel(a_ref, b_ref, out_ref):
    out_ref[...] = (a_ref[...].astype(jnp.float32) + b_ref[...].astype(jnp.float32)).astype(jnp.bfloat16)


def add(a, b):
    return pl.pallas_call(
        add_kernel,
        in_specs=[VMEM, VMEM],
        out_specs=VMEM,
        out_shape=jax.ShapeDtypeStruct(a.shape, a.dtype),
        compiler_params=params(2),
        name="add",
    )(a, b)


def choose_kernel(rows, first_ref, *refs):
    z = lax.div(first_ref[0], rows)
    for k, ref in enumerate(refs[:-1]):

        @pl.when((z >> 1) == k)
        def _():
            refs[-1][...] = ref[...]


def choose(first, rows, parts):
    return pl.pallas_call(
        functools.partial(choose_kernel, rows),
        in_specs=[SMEM] + [VMEM] * len(parts),
        out_specs=VMEM,
        out_shape=jax.ShapeDtypeStruct(parts[0].shape, parts[0].dtype),
        compiler_params=params(2),
        name="choose",
    )(first, *parts)


def pick_kernel(blk, piv_ref, first_ref, trailing_ref, out_ref, cnt_ref, lst_ref, own_ref, group_ref, rows_ref, sem):
    width = piv_ref.shape[0]
    rows = trailing_ref.shape[0]
    first = first_ref[0]
    nblk = cnt_ref.shape[0]
    for b in range(nblk):
        cnt_ref[b] = 0

    def filt(i, n):
        loc = piv_ref[i] - first
        own_ref[n] = i
        return n + ((loc >= 0) & (loc < rows)).astype(jnp.int32)

    n = lax.fori_loop(0, width, filt, 0, unroll=8)

    def group(k):
        loc = piv_ref[own_ref[k]] - first
        base = pl.multiple_of(loc & ~15, 16)
        return pltpu.make_async_copy(trailing_ref.at[pl.ds(base, 16)], group_ref.at[k], sem)

    def begin(k, carry):
        group(k).start()
        i = own_ref[k]
        b = lax.div(piv_ref[i] - first, blk)
        m = cnt_ref[b]
        lst_ref[b * width + m] = i
        cnt_ref[b] = m + 1
        return carry

    def finish(k, carry):
        group(k).wait()
        return carry

    lax.fori_loop(0, n, begin, 0)
    rows_ref[...] = jnp.zeros_like(rows_ref)
    lax.fori_loop(0, n, finish, 0)
    sub = lax.broadcasted_iota(jnp.int32, (16, 128), 0)

    def extract(k, carry):
        i = own_ref[k]
        loc = piv_ref[i] - first
        tile = group_ref[k].astype(jnp.float32)
        row = jnp.sum(jnp.where(sub == (loc & 15), tile, 0.0), axis=0, keepdims=True)
        rows_ref[pl.ds(i, 1), :] = row
        return carry

    lax.fori_loop(0, n, extract, 0)
    out_ref[...] = rows_ref[...].astype(jnp.bfloat16)


def pick(trailing, pivots, first, blk):
    rows, cols = trailing.shape
    width = pivots.shape[0]
    nblk = rows // blk
    return pl.pallas_call(
        functools.partial(pick_kernel, blk),
        in_specs=[SMEM, SMEM, pl.BlockSpec(memory_space=pltpu.HBM)],
        out_specs=[VMEM, SMEM, SMEM],
        out_shape=[
            jax.ShapeDtypeStruct((width, cols), jnp.bfloat16),
            jax.ShapeDtypeStruct((nblk,), jnp.int32),
            jax.ShapeDtypeStruct((nblk * width,), jnp.int32),
        ],
        scratch_shapes=[
            pltpu.SMEM((width + 8,), jnp.int32),
            pltpu.VMEM((width, 16, cols), jnp.bfloat16),
            pltpu.VMEM((width, cols), jnp.float32),
            pltpu.SemaphoreType.DMA,
        ],
        compiler_params=params(6),
        cost_estimate=cost(12),
        name="pick",
    )(pivots, first, trailing)


def dot(a, b):
    return lax.dot_general(
        a, b, (((1,), (0,)), ((), ())), precision=HIGHEST, preferred_element_type=jnp.float32
    )


def dot_exact(a, b):
    n = b.shape[1]
    hi = b.astype(jnp.bfloat16)
    rest = b - hi.astype(jnp.float32)
    mid = rest.astype(jnp.bfloat16)
    low = (rest - mid.astype(jnp.float32)).astype(jnp.bfloat16)
    r = lax.dot_general(
        a, jnp.concatenate([hi, mid, low], axis=1), (((1,), (0,)), ((), ())),
        preferred_element_type=jnp.float32,
    )
    return r[:, 2 * n :] + r[:, n : 2 * n] + r[:, :n]


def unit_inverse(strict):
    n = strict.shape[0]
    r = lax.broadcasted_iota(jnp.int32, (n, n), 0)
    c = lax.broadcasted_iota(jnp.int32, (n, n), 1)
    d = jnp.where((r >> 4) == (c >> 4), strict, 0.0)
    x = jnp.where(r == c, 1.0, 0.0) - d
    for step in range(3):
        d = dot_exact(d.astype(jnp.bfloat16), d) if step == 0 else dot(d, d)
        x = x + dot(x, d)
    for lg in (4, 5, 6):
        inside = ((r >> (lg + 1)) == (c >> (lg + 1))) & ((r >> lg) != (c >> lg))
        part = jnp.where(inside, strict, 0.0).astype(jnp.bfloat16)
        x = x - dot(x, dot_exact(part, x))
    return x


def blocks():
    return [(k, outer, inner) for k in range(2) for outer in OFFSETS for inner in OFFSETS]


def block_at(me, k, outer, inner):
    core = (me & 1) ^ k
    dx = jnp.where(core == 0, inner, outer)
    dy = jnp.where(core == 0, outer, inner)
    x = ((me >> 3) + dx) & 3
    y = ((me >> 1) + dy) & 3
    return pl.ds(pl.multiple_of(((x * 4 + y) * 2 + core) * 8, 8), 8)


def solve_kernel(me_ref, own_ref, other_ref, top_ref, more_ref, head_ref, out_ref, a_ref, g_ref):
    n = top_ref.shape[0]
    h = n // 2
    me = me_ref[0]
    g_ref[:h, :] = own_ref[...].astype(jnp.float32)
    g_ref[h:, :] = other_ref[...].astype(jnp.float32)
    for b, where in enumerate(blocks()):
        a_ref[block_at(me, *where), :] = g_ref[8 * b : 8 * b + 8, :]
    r = lax.broadcasted_iota(jnp.int32, (h, h), 0)
    c = lax.broadcasted_iota(jnp.int32, (h, h), 1)
    s11 = jnp.where(r > c, a_ref[:h, :h].T, 0.0)
    s22 = jnp.where(r > c, a_ref[h:, h:].T, 0.0)
    s21 = a_ref[:h, h:].T
    x1 = unit_inverse(s11)
    x2 = unit_inverse(s22)
    top = top_ref[...].astype(jnp.float32) + more_ref[...].astype(jnp.float32)
    u1 = dot(x1, top[:h])
    u2 = dot(x2, top[h:] - dot_exact(s21.astype(jnp.bfloat16), u1))
    out_ref[:n, :] = jnp.concatenate([u1, u2], axis=0).astype(jnp.bfloat16)
    out_ref[n:, :] = head_ref[...]


def solve(me, own, other, top, more, trailing):
    n, cols = top.shape
    whole = pl.BlockSpec((n // 2, n), lambda i: (0, 0))
    tall = pl.BlockSpec((n, cols), lambda i: (0, 0))
    return pl.pallas_call(
        solve_kernel,
        grid=(1,),
        in_specs=[SMEM, whole, whole, tall, tall, tall],
        out_specs=pl.BlockSpec((2 * n, cols), lambda i: (0, 0)),
        out_shape=jax.ShapeDtypeStruct((2 * n, cols), jnp.bfloat16),
        scratch_shapes=[pltpu.VMEM((n, n), jnp.float32), pltpu.VMEM((n, n), jnp.float32)],
        compiler_params=params(10),
        cost_estimate=cost(20),
        name="solve",
    )(me, own, other, top, more, trailing)


def update_kernel(nblk, cnt_ref, lst_ref, piv_ref, first_ref, me_ref, tr_ref, ud_ref, rest_ref, *refs):
    parts = refs[1:11]
    out_ref, acc_ref, nat_ref, drow_ref, u_ref, tmp_ref = refs[11:]
    blk = out_ref.shape[0]
    width = nat_ref.shape[0]
    b = pl.program_id(0)
    first = first_ref[0]

    @pl.when(b == 0)
    def _():
        odd = lax.div(first, nblk * blk) & 1

        @pl.when(odd == 0)
        def _():
            nat_ref[...] = ud_ref[:width, :].astype(jnp.float32)
            drow_ref[...] = ud_ref[width:, :].astype(jnp.float32)

        @pl.when(odd == 1)
        def _():
            nat_ref[...] = rest_ref[:width, :].astype(jnp.float32)
            drow_ref[...] = rest_ref[width:, :].astype(jnp.float32)

        for i, where in enumerate(blocks()):
            tmp_ref[8 * i : 8 * i + 8, :] = nat_ref[block_at(me_ref[0], *where), :]
        u_ref[...] = tmp_ref[...].astype(jnp.bfloat16)

    def compute(half):
        here = pl.ds(pl.multiple_of(b * blk, 128), blk)
        there = pl.ds(pl.multiple_of((b - half * (nblk // 2)) * blk, 128), blk)
        pieces = []
        for s in (parts[:5], parts[5:]):
            pieces += [s[0][:, here], s[1][:, here], s[2][:, here], s[3 + half][:, there]]
        acc_ref[...] = lax.dot_general(
            jnp.concatenate(pieces, axis=0), u_ref[...], (((0,), (0,)), ((), ())),
            preferred_element_type=jnp.float32,
        )

    @pl.when(b < nblk // 2)
    def _():
        compute(0)

    @pl.when(b >= nblk // 2)
    def _():
        compute(1)

    out_ref[...] = (tr_ref[...].astype(jnp.float32) - acc_ref[...]).astype(jnp.bfloat16)
    sub = lax.broadcasted_iota(jnp.int32, (16, 128), 0)

    def fix(k, carry):
        i = lst_ref[b * width + k]
        loc = piv_ref[i] - first - b * blk
        at = pl.ds(pl.multiple_of(loc & ~15, 16), 16)
        new = drow_ref[pl.ds(i, 1), :] - acc_ref[at, :]
        old = out_ref[at, :].astype(jnp.float32)
        out_ref[at, :] = jnp.where(sub == (loc & 15), new, old).astype(jnp.bfloat16)
        return carry

    lax.fori_loop(0, cnt_ref[b], fix, 0)

    @pl.when((b == 0) & (first == 0))
    def _():
        out_ref[:width, :] = nat_ref[...].astype(jnp.bfloat16)


def update(cnt, lst, pivots, first, me, trailing, ud, rest, ahead, parts, blk):
    rows, cols = trailing.shape
    width = pivots.shape[0]
    nblk = rows // blk
    tall = pl.BlockSpec((blk, cols), lambda b: (b, 0))
    pair = pl.BlockSpec((2 * width, cols), lambda b: (0, 0))
    return pl.pallas_call(
        functools.partial(update_kernel, nblk),
        grid=(nblk,),
        in_specs=[SMEM] * 5 + [tall, pair, pair] + [VMEM] * 11,
        out_specs=tall,
        scratch_shapes=[
            pltpu.VMEM((blk, cols), jnp.float32),
            pltpu.VMEM((width, cols), jnp.float32),
            pltpu.VMEM((width, cols), jnp.float32),
            pltpu.VMEM((width, cols), jnp.bfloat16),
            pltpu.VMEM((width, cols), jnp.float32),
        ],
        out_shape=jax.ShapeDtypeStruct((rows, cols), jnp.bfloat16),
        compiler_params=params(16),
        name="update",
    )(cnt, lst, pivots, first, me, trailing, ud, rest, ahead, *parts)


def body(trailing, panel_t, pivots):
    rows = trailing.shape[0]
    width = pivots.shape[0]
    blk = rows // NBLK
    half = rows // 2
    barrier = lax.optimization_barrier
    first = (lax.axis_index("prow") * rows).astype(jnp.int32).reshape(1)
    me = lax.axis_index("pcol").astype(jnp.int32).reshape(1)
    trailing = pltpu.with_memory_space_constraint(trailing, pltpu.HBM)

    def zsend(x, pairs):
        return lax.ppermute(x, "prow", pairs)

    p, m, q = [send(panel_t, hop(d, 0, True)) for d in (1, -1, 2)]

    top, cnt, lst = pick(trailing, pivots, first, blk)
    more = zsend(top, [(1, 0), (3, 2), (5, 4), (7, 6)])
    top = add(top, more)
    p, m, q, top = barrier((p, m, q, top))
    more = zsend(top, [(2, 0), (6, 4)])

    up, down, across = hop(0, 1, True), hop(0, -1, True), hop(0, 2, True)
    diag = stack([panel_t, p, m, q], 0, width, "stack_d")
    diag_q, diag_p, diag_m = send(diag, across), send(diag, up), send(diag, down)
    top = add(top, more)
    p, m, q, diag_q, diag_p, diag_m, top = barrier((p, m, q, diag_q, diag_p, diag_m, top))
    more = zsend(top, [(4, 0)])
    block = stack([panel_t, p, m, q], 0, rows, "stack_p")
    near, far = send(block, up), send(block, down)
    own = stack([diag, diag_p, diag_m, diag_q], 0, width, "stack_l")
    other = send(own, CORES)
    ud = solve(me, own, other, top, more, trailing)
    swap = send(block, CORES)
    ud, near, far, swap = barrier((ud, near, far, swap))
    fa, fb = stack([near], 0, half, "stack_a"), stack([far], half, half, "stack_b")
    qa, qb = send(fa, up), send(fb, down)

    spread = [zsend(ud, [(0, d)]) for d in (2, 4, 6)]
    ud = choose(first, rows, [ud] + spread)
    ud, near, far = barrier((ud, near, far))
    rest = zsend(ud, [(0, 1), (2, 3), (4, 5), (6, 7)])
    other_near, other_far = send(near, CORES), send(far, CORES)
    ahead = stack([qa, qb], 0, 128, "stack_q", 30)
    own = [block, near, far, qa, qb]
    parts = own + [swap, other_near, other_far, send(qa, CORES), send(qb, CORES)]
    return update(cnt, lst, pivots, first, me, trailing, ud, rest, ahead, parts, blk)


def solution(mesh):
    return jax.shard_map(
        body,
        mesh=mesh,
        in_specs=(P("prow", "pcol"), P("pcol", "prow"), P()),
        out_specs=P("prow", "pcol"),
        check_vma=False,
    )
```

```python
import functools

import jax
import jax.numpy as jnp
from jax import lax
from jax.experimental import pallas as pl
from jax.experimental.pallas import tpu as pltpu
from jax.sharding import PartitionSpec as P

NX = 4
NY = 4
OFFSETS = (0, -1, 1, 2)
NBLK = 6
SMEM = pl.BlockSpec(memory_space=pltpu.SMEM)
VMEM = pl.BlockSpec(memory_space=pltpu.VMEM)
HIGHEST = lax.Precision.HIGHEST


def place(x, y, c):
    return ((x % NX) * NY + (y % NY)) * 2 + c


def hop(dx, dy, turn):
    pairs = []
    for x in range(NX):
        for y in range(NY):
            for c in range(2):
                a, b = (dy, dx) if turn and c == 1 else (dx, dy)
                pairs.append((place(x, y, c), place(x + a, y + b, c)))
    return pairs


CORES = [(p, p ^ 1) for p in range(NX * NY * 2)]


def send(block, pairs):
    return lax.ppermute(block, "pcol", pairs)


def params(mib):
    return pltpu.CompilerParams(vmem_limit_bytes=mib << 20)


def cost(us):
    return pl.CostEstimate(flops=int(us * 1.1e9), bytes_accessed=int(us * 3.5e6), transcendentals=0)


def stack_kernel(*refs):
    refs[-1][...] = jnp.concatenate([r[...] for r in refs[:-1]], axis=0)


def stack(parts, start, cols, name, us=1):
    rows = sum(p.shape[0] for p in parts)
    step = min(cols, 4096)
    return pl.pallas_call(
        stack_kernel,
        grid=(cols // step,),
        in_specs=[pl.BlockSpec((p.shape[0], step), lambda i: (0, i + start // step)) for p in parts],
        out_specs=pl.BlockSpec((rows, step), lambda i: (0, i)),
        out_shape=jax.ShapeDtypeStruct((rows, cols), jnp.bfloat16),
        compiler_params=params(6),
        cost_estimate=cost(us),
        name=name,
    )(*parts)


def add_kernel(a_ref, b_ref, out_ref):
    out_ref[...] = (a_ref[...].astype(jnp.float32) + b_ref[...].astype(jnp.float32)).astype(jnp.bfloat16)


def add(a, b):
    return pl.pallas_call(
        add_kernel,
        in_specs=[VMEM, VMEM],
        out_specs=VMEM,
        out_shape=jax.ShapeDtypeStruct(a.shape, a.dtype),
        compiler_params=params(2),
        name="add",
    )(a, b)


def choose_kernel(rows, mask, first_ref, a_ref, b_ref, out_ref):
    other = (jnp.int32(mask) >> lax.div(first_ref[0], rows)) & 1

    @pl.when(other == 0)
    def _():
        out_ref[...] = a_ref[...]

    @pl.when(other == 1)
    def _():
        out_ref[...] = b_ref[...]


def choose(first, rows, others, a, b):
    return pl.pallas_call(
        functools.partial(choose_kernel, rows, sum(1 << z for z in others)),
        in_specs=[SMEM, VMEM, VMEM],
        out_specs=VMEM,
        out_shape=jax.ShapeDtypeStruct(a.shape, a.dtype),
        compiler_params=params(2),
        name="choose",
    )(first, a, b)


def pick_kernel(blk, piv_ref, first_ref, trailing_ref, out_ref, cnt_ref, lst_ref, own_ref, group_ref, rows_ref, sem):
    width = piv_ref.shape[0]
    rows = trailing_ref.shape[0]
    first = first_ref[0]
    nblk = cnt_ref.shape[0]
    for b in range(nblk):
        cnt_ref[b] = 0

    def filt(i, n):
        loc = piv_ref[i] - first
        own_ref[n] = i
        return n + ((loc >= 0) & (loc < rows)).astype(jnp.int32)

    n = lax.fori_loop(0, width, filt, 0, unroll=8)

    def group(k):
        loc = piv_ref[own_ref[k]] - first
        base = pl.multiple_of(loc & ~15, 16)
        return pltpu.make_async_copy(trailing_ref.at[pl.ds(base, 16)], group_ref.at[k], sem)

    def begin(k, carry):
        group(k).start()
        i = own_ref[k]
        b = lax.div(piv_ref[i] - first, blk)
        m = cnt_ref[b]
        lst_ref[b * width + m] = i
        cnt_ref[b] = m + 1
        return carry

    def finish(k, carry):
        group(k).wait()
        return carry

    lax.fori_loop(0, n, begin, 0)
    rows_ref[...] = jnp.zeros_like(rows_ref)
    lax.fori_loop(0, n, finish, 0)
    sub = lax.broadcasted_iota(jnp.int32, (16, 128), 0)

    def extract(k, carry):
        i = own_ref[k]
        loc = piv_ref[i] - first
        tile = group_ref[k].astype(jnp.float32)
        row = jnp.sum(jnp.where(sub == (loc & 15), tile, 0.0), axis=0, keepdims=True)
        rows_ref[pl.ds(i, 1), :] = row
        return carry

    lax.fori_loop(0, n, extract, 0)
    out_ref[...] = rows_ref[...].astype(jnp.bfloat16)


def pick(trailing, pivots, first, blk):
    rows, cols = trailing.shape
    width = pivots.shape[0]
    nblk = rows // blk
    return pl.pallas_call(
        functools.partial(pick_kernel, blk),
        in_specs=[SMEM, SMEM, pl.BlockSpec(memory_space=pltpu.HBM)],
        out_specs=[VMEM, SMEM, SMEM],
        out_shape=[
            jax.ShapeDtypeStruct((width, cols), jnp.bfloat16),
            jax.ShapeDtypeStruct((nblk,), jnp.int32),
            jax.ShapeDtypeStruct((nblk * width,), jnp.int32),
        ],
        scratch_shapes=[
            pltpu.SMEM((width + 8,), jnp.int32),
            pltpu.VMEM((width, 16, cols), jnp.bfloat16),
            pltpu.VMEM((width, cols), jnp.float32),
            pltpu.SemaphoreType.DMA,
        ],
        compiler_params=params(6),
        cost_estimate=cost(12),
        name="pick",
    )(pivots, first, trailing)


def dot(a, b):
    return lax.dot_general(
        a, b, (((1,), (0,)), ((), ())), precision=HIGHEST, preferred_element_type=jnp.float32
    )


def dot_exact(a, b):
    n = b.shape[1]
    hi = b.astype(jnp.bfloat16)
    rest = b - hi.astype(jnp.float32)
    mid = rest.astype(jnp.bfloat16)
    low = (rest - mid.astype(jnp.float32)).astype(jnp.bfloat16)
    r = lax.dot_general(
        a, jnp.concatenate([hi, mid, low], axis=1), (((1,), (0,)), ((), ())),
        preferred_element_type=jnp.float32,
    )
    return r[:, 2 * n :] + r[:, n : 2 * n] + r[:, :n]


def unit_inverse(strict):
    n = strict.shape[0]
    r = lax.broadcasted_iota(jnp.int32, (n, n), 0)
    c = lax.broadcasted_iota(jnp.int32, (n, n), 1)
    d = jnp.where((r >> 4) == (c >> 4), strict, 0.0)
    x = jnp.where(r == c, 1.0, 0.0) - d
    for step in range(3):
        d = dot_exact(d.astype(jnp.bfloat16), d) if step == 0 else dot(d, d)
        x = x + dot(x, d)
    for lg in (4, 5, 6):
        inside = ((r >> (lg + 1)) == (c >> (lg + 1))) & ((r >> lg) != (c >> lg))
        part = jnp.where(inside, strict, 0.0).astype(jnp.bfloat16)
        x = x - dot(x, dot_exact(part, x))
    return x


def blocks():
    return [(k, outer, inner) for k in range(2) for outer in OFFSETS for inner in OFFSETS]


def block_at(me, k, outer, inner):
    core = (me & 1) ^ k
    dx = jnp.where(core == 0, inner, outer)
    dy = jnp.where(core == 0, outer, inner)
    x = ((me >> 3) + dx) & 3
    y = ((me >> 1) + dy) & 3
    return pl.ds(pl.multiple_of(((x * 4 + y) * 2 + core) * 8, 8), 8)


def solve_kernel(me_ref, own_ref, other_ref, top_ref, more_ref, head_ref, out_ref, a_ref, g_ref):
    n = top_ref.shape[0]
    h = n // 2
    me = me_ref[0]
    g_ref[:h, :] = own_ref[...].astype(jnp.float32)
    g_ref[h:, :] = other_ref[...].astype(jnp.float32)
    for b, where in enumerate(blocks()):
        a_ref[block_at(me, *where), :] = g_ref[8 * b : 8 * b + 8, :]
    r = lax.broadcasted_iota(jnp.int32, (h, h), 0)
    c = lax.broadcasted_iota(jnp.int32, (h, h), 1)
    s11 = jnp.where(r > c, a_ref[:h, :h].T, 0.0)
    s22 = jnp.where(r > c, a_ref[h:, h:].T, 0.0)
    s21 = a_ref[:h, h:].T
    x1 = unit_inverse(s11)
    x2 = unit_inverse(s22)
    top = sum(r[...].astype(jnp.float32) for r in (top_ref, more_ref))
    u1 = dot(x1, top[:h])
    u2 = dot(x2, top[h:] - dot_exact(s21.astype(jnp.bfloat16), u1))
    out_ref[:n, :] = jnp.concatenate([u1, u2], axis=0).astype(jnp.bfloat16)
    out_ref[n:, :] = head_ref[...]


def solve(me, own, other, top, more, trailing):
    n, cols = top.shape
    whole = pl.BlockSpec((n // 2, n), lambda i: (0, 0))
    tall = pl.BlockSpec((n, cols), lambda i: (0, 0))
    return pl.pallas_call(
        solve_kernel,
        grid=(1,),
        in_specs=[SMEM, whole, whole] + [tall] * 3,
        out_specs=pl.BlockSpec((2 * n, cols), lambda i: (0, 0)),
        out_shape=jax.ShapeDtypeStruct((2 * n, cols), jnp.bfloat16),
        scratch_shapes=[pltpu.VMEM((n, n), jnp.float32), pltpu.VMEM((n, n), jnp.float32)],
        compiler_params=params(10),
        name="solve",
    )(me, own, other, top, more, trailing)


def update_kernel(nblk, cnt_ref, lst_ref, piv_ref, first_ref, me_ref, tr_ref, ud_ref, rest_ref, *refs):
    parts = refs[1:11]
    out_ref, acc_ref, nat_ref, drow_ref, u_ref, tmp_ref = refs[11:]
    blk = out_ref.shape[0]
    width = nat_ref.shape[0]
    b = pl.program_id(0)
    first = first_ref[0]

    @pl.when(b == 0)
    def _():
        late = lax.div(first, nblk * blk) >> 2

        @pl.when(late == 0)
        def _():
            nat_ref[...] = ud_ref[:width, :].astype(jnp.float32)
            drow_ref[...] = ud_ref[width:, :].astype(jnp.float32)

        @pl.when(late == 1)
        def _():
            nat_ref[...] = rest_ref[:width, :].astype(jnp.float32)
            drow_ref[...] = rest_ref[width:, :].astype(jnp.float32)

        for i, where in enumerate(blocks()):
            tmp_ref[8 * i : 8 * i + 8, :] = nat_ref[block_at(me_ref[0], *where), :]
        u_ref[...] = tmp_ref[...].astype(jnp.bfloat16)

    def compute(half):
        here = pl.ds(pl.multiple_of(b * blk, 128), blk)
        there = pl.ds(pl.multiple_of((b - half * (nblk // 2)) * blk, 128), blk)
        pieces = []
        for s in (parts[:5], parts[5:]):
            pieces += [s[0][:, here], s[1][:, here], s[2][:, here], s[3 + half][:, there]]
        acc_ref[...] = lax.dot_general(
            jnp.concatenate(pieces, axis=0), u_ref[...], (((0,), (0,)), ((), ())),
            preferred_element_type=jnp.float32,
        )

    @pl.when(b < nblk // 2)
    def _():
        compute(0)

    @pl.when(b >= nblk // 2)
    def _():
        compute(1)

    out_ref[...] = (tr_ref[...].astype(jnp.float32) - acc_ref[...]).astype(jnp.bfloat16)
    sub = lax.broadcasted_iota(jnp.int32, (16, 128), 0)

    def fix(k, carry):
        i = lst_ref[b * width + k]
        loc = piv_ref[i] - first - b * blk
        at = pl.ds(pl.multiple_of(loc & ~15, 16), 16)
        new = drow_ref[pl.ds(i, 1), :] - acc_ref[at, :]
        old = out_ref[at, :].astype(jnp.float32)
        out_ref[at, :] = jnp.where(sub == (loc & 15), new, old).astype(jnp.bfloat16)
        return carry

    lax.fori_loop(0, cnt_ref[b], fix, 0)

    @pl.when((b == 0) & (first == 0))
    def _():
        out_ref[:width, :] = nat_ref[...].astype(jnp.bfloat16)


def update(cnt, lst, pivots, first, me, trailing, ud, rest, ahead, parts, blk):
    rows, cols = trailing.shape
    width = pivots.shape[0]
    nblk = rows // blk
    tall = pl.BlockSpec((blk, cols), lambda b: (b, 0))
    pair = pl.BlockSpec((2 * width, cols), lambda b: (0, 0))
    return pl.pallas_call(
        functools.partial(update_kernel, nblk),
        grid=(nblk,),
        in_specs=[SMEM] * 5 + [tall, pair, pair] + [VMEM] * 11,
        out_specs=tall,
        scratch_shapes=[
            pltpu.VMEM((blk, cols), jnp.float32),
            pltpu.VMEM((width, cols), jnp.float32),
            pltpu.VMEM((width, cols), jnp.float32),
            pltpu.VMEM((width, cols), jnp.bfloat16),
            pltpu.VMEM((width, cols), jnp.float32),
        ],
        out_shape=jax.ShapeDtypeStruct((rows, cols), jnp.bfloat16),
        compiler_params=params(16),
        name="update",
    )(cnt, lst, pivots, first, me, trailing, ud, rest, ahead, *parts)


def body(trailing, panel_t, pivots):
    rows = trailing.shape[0]
    width = pivots.shape[0]
    blk = rows // NBLK
    half = rows // 2
    barrier = lax.optimization_barrier
    first = (lax.axis_index("prow") * rows).astype(jnp.int32).reshape(1)
    me = lax.axis_index("pcol").astype(jnp.int32).reshape(1)
    trailing = pltpu.with_memory_space_constraint(trailing, pltpu.HBM)

    def zsend(x, pairs):
        return lax.ppermute(x, "prow", pairs)

    two = hop(2, 0, True)
    diag = stack([panel_t], 0, width, "stack_t")
    diag_q = send(diag, two)
    p, m = send(panel_t, hop(1, 0, True)), send(panel_t, hop(-1, 0, True))
    long, diag_q = barrier((panel_t, diag_q))
    q = send(long, two)

    top, cnt, lst = pick(trailing, pivots, first, blk)
    more = zsend(top, [(1, 0), (3, 2), (5, 4), (7, 6)])

    up, down, across = hop(0, 1, True), hop(0, -1, True), hop(0, 2, True)
    p, m, diag_q, top = barrier((p, m, diag_q, top))
    diag = stack([diag, p, m, diag_q], 0, width, "stack_d")
    diag_q, diag_p, diag_m = send(diag, across), send(diag, up), send(diag, down)
    top = add(top, more)
    more = zsend(top, [(2, 0), (6, 4)])
    p, m, q, diag_q, diag_p, diag_m, top, more = barrier((p, m, q, diag_q, diag_p, diag_m, top, more))
    top = add(top, more)
    more = zsend(top, [(4, 0)])
    block = stack([panel_t, p, m, q], 0, rows, "stack_p")
    near, far = send(block, up), send(block, down)
    swap = send(block, CORES)
    own = stack([diag, diag_p, diag_m, diag_q], 0, width, "stack_l")
    other = send(own, CORES)
    ud = solve(me, own, other, top, more, trailing)
    ud, near, far, swap = barrier((ud, near, far, swap))
    fa, fb = stack([near], 0, half, "stack_a"), stack([far], half, half, "stack_b")
    qa, qb = send(fa, up), send(fb, down)
    ud = choose(first, rows, (2,), ud, zsend(ud, [(0, 2)]))
    ud, near, far = barrier((ud, near, far))
    other_near, other_far = send(near, CORES), send(far, CORES)
    ud = choose(first, rows, (1, 3), ud, zsend(ud, [(0, 1), (2, 3)]))
    rest = zsend(ud, [(i, i + 4) for i in range(4)])
    ahead = stack([qa, qb], 0, 128, "stack_q", 60)
    own = [block, near, far, qa, qb]
    parts = own + [swap, other_near, other_far, send(qa, CORES), send(qb, CORES)]
    return update(cnt, lst, pivots, first, me, trailing, ud, rest, ahead, parts, blk)


def solution(mesh):
    return jax.shard_map(
        body,
        mesh=mesh,
        in_specs=(P("prow", "pcol"), P("pcol", "prow"), P()),
        out_specs=P("prow", "pcol"),
        check_vma=False,
    )
```

```python
import functools

import jax
import jax.numpy as jnp
from jax import lax
from jax.experimental import pallas as pl
from jax.experimental.pallas import tpu as pltpu
from jax.sharding import PartitionSpec as P

NX = 4
NY = 4
OFFSETS = (0, -1, 1, 2)
NBLK = 6
SMEM = pl.BlockSpec(memory_space=pltpu.SMEM)
VMEM = pl.BlockSpec(memory_space=pltpu.VMEM)
HIGHEST = lax.Precision.HIGHEST


def place(x, y, c):
    return ((x % NX) * NY + (y % NY)) * 2 + c


def hop(dx, dy, turn):
    pairs = []
    for x in range(NX):
        for y in range(NY):
            for c in range(2):
                a, b = (dy, dx) if turn and c == 1 else (dx, dy)
                pairs.append((place(x, y, c), place(x + a, y + b, c)))
    return pairs


CORES = [(p, p ^ 1) for p in range(NX * NY * 2)]


def send(block, pairs):
    return lax.ppermute(block, "pcol", pairs)


def params(mib):
    return pltpu.CompilerParams(vmem_limit_bytes=mib << 20)


def cost(us):
    return pl.CostEstimate(flops=int(us * 1.1e9), bytes_accessed=int(us * 3.5e6), transcendentals=0)


def stack_kernel(start, step, *refs):
    def chunk(i, carry):
        src = pl.ds(pl.multiple_of(start + i * step, 128), step)
        dst = pl.ds(pl.multiple_of(i * step, 128), step)
        refs[-1][:, dst] = jnp.concatenate([r[:, src] for r in refs[:-1]], axis=0)
        return carry

    lax.fori_loop(0, refs[-1].shape[1] // step, chunk, 0)


def stack(parts, start, cols, name, us=1):
    rows = sum(p.shape[0] for p in parts)
    return pl.pallas_call(
        functools.partial(stack_kernel, start, min(cols, 1024)),
        in_specs=[VMEM] * len(parts),
        out_specs=VMEM,
        out_shape=jax.ShapeDtypeStruct((rows, cols), jnp.bfloat16),
        compiler_params=params(2),
        cost_estimate=cost(us),
        name=name,
    )(*parts)


def add_kernel(a_ref, b_ref, out_ref):
    out_ref[...] = (a_ref[...].astype(jnp.float32) + b_ref[...].astype(jnp.float32)).astype(jnp.bfloat16)


def add(a, b):
    return pl.pallas_call(
        add_kernel,
        in_specs=[VMEM, VMEM],
        out_specs=VMEM,
        out_shape=jax.ShapeDtypeStruct(a.shape, a.dtype),
        compiler_params=params(2),
        name="add",
    )(a, b)


def choose_kernel(rows, mask, first_ref, a_ref, b_ref, out_ref):
    other = (jnp.int32(mask) >> lax.div(first_ref[0], rows)) & 1

    @pl.when(other == 0)
    def _():
        out_ref[...] = a_ref[...]

    @pl.when(other == 1)
    def _():
        out_ref[...] = b_ref[...]


def choose(first, rows, others, a, b):
    return pl.pallas_call(
        functools.partial(choose_kernel, rows, sum(1 << z for z in others)),
        in_specs=[SMEM, VMEM, VMEM],
        out_specs=VMEM,
        out_shape=jax.ShapeDtypeStruct(a.shape, a.dtype),
        compiler_params=params(2),
        name="choose",
    )(first, a, b)


def pick_kernel(blk, piv_ref, first_ref, trailing_ref, out_ref, cnt_ref, lst_ref, own_ref, group_ref, rows_ref, sem):
    width = piv_ref.shape[0]
    rows = trailing_ref.shape[0]
    first = first_ref[0]
    nblk = cnt_ref.shape[0]
    for b in range(nblk):
        cnt_ref[b] = 0

    def filt(i, n):
        loc = piv_ref[i] - first
        own_ref[n] = i
        return n + ((loc >= 0) & (loc < rows)).astype(jnp.int32)

    n = lax.fori_loop(0, width, filt, 0, unroll=8)

    def group(k):
        loc = piv_ref[own_ref[k]] - first
        base = pl.multiple_of(loc & ~15, 16)
        return pltpu.make_async_copy(trailing_ref.at[pl.ds(base, 16)], group_ref.at[k], sem)

    def begin(k, carry):
        group(k).start()
        i = own_ref[k]
        b = lax.div(piv_ref[i] - first, blk)
        m = cnt_ref[b]
        lst_ref[b * width + m] = i
        cnt_ref[b] = m + 1
        return carry

    def finish(k, carry):
        group(k).wait()
        return carry

    lax.fori_loop(0, n, begin, 0)
    rows_ref[...] = jnp.zeros_like(rows_ref)
    lax.fori_loop(0, n, finish, 0)
    sub = lax.broadcasted_iota(jnp.int32, (16, 128), 0)

    def extract(k, carry):
        i = own_ref[k]
        loc = piv_ref[i] - first
        tile = group_ref[k].astype(jnp.float32)
        row = jnp.sum(jnp.where(sub == (loc & 15), tile, 0.0), axis=0, keepdims=True)
        rows_ref[pl.ds(i, 1), :] = row
        return carry

    lax.fori_loop(0, n, extract, 0)
    out_ref[...] = rows_ref[...].astype(jnp.bfloat16)


def pick(trailing, pivots, first, blk):
    rows, cols = trailing.shape
    width = pivots.shape[0]
    nblk = rows // blk
    return pl.pallas_call(
        functools.partial(pick_kernel, blk),
        in_specs=[SMEM, SMEM, pl.BlockSpec(memory_space=pltpu.HBM)],
        out_specs=[VMEM, SMEM, SMEM],
        out_shape=[
            jax.ShapeDtypeStruct((width, cols), jnp.bfloat16),
            jax.ShapeDtypeStruct((nblk,), jnp.int32),
            jax.ShapeDtypeStruct((nblk * width,), jnp.int32),
        ],
        scratch_shapes=[
            pltpu.SMEM((width + 8,), jnp.int32),
            pltpu.VMEM((width, 16, cols), jnp.bfloat16),
            pltpu.VMEM((width, cols), jnp.float32),
            pltpu.SemaphoreType.DMA,
        ],
        compiler_params=params(6),
        cost_estimate=cost(12),
        name="pick",
    )(pivots, first, trailing)


def dot(a, b):
    return lax.dot_general(
        a, b, (((1,), (0,)), ((), ())), precision=HIGHEST, preferred_element_type=jnp.float32
    )


def dot_exact(a, b):
    n = b.shape[1]
    hi = b.astype(jnp.bfloat16)
    rest = b - hi.astype(jnp.float32)
    mid = rest.astype(jnp.bfloat16)
    low = (rest - mid.astype(jnp.float32)).astype(jnp.bfloat16)
    r = lax.dot_general(
        a, jnp.concatenate([hi, mid, low], axis=1), (((1,), (0,)), ((), ())),
        preferred_element_type=jnp.float32,
    )
    return r[:, 2 * n :] + r[:, n : 2 * n] + r[:, :n]


def unit_inverse(strict):
    n = strict.shape[0]
    r = lax.broadcasted_iota(jnp.int32, (n, n), 0)
    c = lax.broadcasted_iota(jnp.int32, (n, n), 1)
    d = jnp.where((r >> 4) == (c >> 4), strict, 0.0)
    x = jnp.where(r == c, 1.0, 0.0) - d
    for step in range(3):
        d = dot_exact(d.astype(jnp.bfloat16), d) if step == 0 else dot(d, d)
        x = x + dot(x, d)
    for lg in (4, 5, 6):
        inside = ((r >> (lg + 1)) == (c >> (lg + 1))) & ((r >> lg) != (c >> lg))
        part = jnp.where(inside, strict, 0.0).astype(jnp.bfloat16)
        x = x - dot(x, dot_exact(part, x))
    return x


def blocks():
    return [(k, outer, inner) for k in range(2) for outer in OFFSETS for inner in OFFSETS]


def block_at(me, k, outer, inner):
    core = (me & 1) ^ k
    dx = jnp.where(core == 0, inner, outer)
    dy = jnp.where(core == 0, outer, inner)
    x = ((me >> 3) + dx) & 3
    y = ((me >> 1) + dy) & 3
    return pl.ds(pl.multiple_of(((x * 4 + y) * 2 + core) * 8, 8), 8)


def solve_kernel(me_ref, own_ref, other_ref, top_ref, more_ref, head_ref, out_ref, a_ref, g_ref):
    n = top_ref.shape[0]
    h = n // 2
    me = me_ref[0]
    g_ref[:h, :] = own_ref[...].astype(jnp.float32)
    g_ref[h:, :] = other_ref[...].astype(jnp.float32)
    for b, where in enumerate(blocks()):
        a_ref[block_at(me, *where), :] = g_ref[8 * b : 8 * b + 8, :]
    r = lax.broadcasted_iota(jnp.int32, (h, h), 0)
    c = lax.broadcasted_iota(jnp.int32, (h, h), 1)
    s11 = jnp.where(r > c, a_ref[:h, :h].T, 0.0)
    s22 = jnp.where(r > c, a_ref[h:, h:].T, 0.0)
    s21 = a_ref[:h, h:].T
    x1 = unit_inverse(s11)
    x2 = unit_inverse(s22)
    top = sum(r[...].astype(jnp.float32) for r in (top_ref, more_ref))
    u1 = dot(x1, top[:h])
    u2 = dot(x2, top[h:] - dot_exact(s21.astype(jnp.bfloat16), u1))
    out_ref[:n, :] = jnp.concatenate([u1, u2], axis=0).astype(jnp.bfloat16)
    out_ref[n:, :] = head_ref[...]


def solve(me, own, other, top, more, trailing):
    n, cols = top.shape
    whole = pl.BlockSpec((n // 2, n), lambda i: (0, 0))
    tall = pl.BlockSpec((n, cols), lambda i: (0, 0))
    return pl.pallas_call(
        solve_kernel,
        grid=(1,),
        in_specs=[SMEM, whole, whole] + [tall] * 3,
        out_specs=pl.BlockSpec((2 * n, cols), lambda i: (0, 0)),
        out_shape=jax.ShapeDtypeStruct((2 * n, cols), jnp.bfloat16),
        scratch_shapes=[pltpu.VMEM((n, n), jnp.float32), pltpu.VMEM((n, n), jnp.float32)],
        compiler_params=params(10),
        name="solve",
    )(me, own, other, top, more, trailing)


def update_kernel(nblk, cnt_ref, lst_ref, piv_ref, first_ref, me_ref, tr_ref, ud_ref, rest_ref, *refs):
    parts = refs[1:11]
    out_ref, acc_ref, nat_ref, drow_ref, u_ref, tmp_ref = refs[11:]
    blk = out_ref.shape[0]
    width = nat_ref.shape[0]
    b = pl.program_id(0)
    first = first_ref[0]

    @pl.when(b == 0)
    def _():
        late = lax.div(first, nblk * blk) >> 2

        @pl.when(late == 0)
        def _():
            nat_ref[...] = ud_ref[:width, :].astype(jnp.float32)
            drow_ref[...] = ud_ref[width:, :].astype(jnp.float32)

        @pl.when(late == 1)
        def _():
            nat_ref[...] = rest_ref[:width, :].astype(jnp.float32)
            drow_ref[...] = rest_ref[width:, :].astype(jnp.float32)

        for i, where in enumerate(blocks()):
            tmp_ref[8 * i : 8 * i + 8, :] = nat_ref[block_at(me_ref[0], *where), :]
        u_ref[...] = tmp_ref[...].astype(jnp.bfloat16)

    def compute(half):
        here = pl.ds(pl.multiple_of(b * blk, 128), blk)
        there = pl.ds(pl.multiple_of((b - half * (nblk // 2)) * blk, 128), blk)
        pieces = []
        for s in (parts[:5], parts[5:]):
            pieces += [s[0][:, here], s[1][:, here], s[2][:, here], s[3 + half][:, there]]
        acc_ref[...] = lax.dot_general(
            jnp.concatenate(pieces, axis=0), u_ref[...], (((0,), (0,)), ((), ())),
            preferred_element_type=jnp.float32,
        )

    @pl.when(b < nblk // 2)
    def _():
        compute(0)

    @pl.when(b >= nblk // 2)
    def _():
        compute(1)

    out_ref[...] = (tr_ref[...].astype(jnp.float32) - acc_ref[...]).astype(jnp.bfloat16)
    sub = lax.broadcasted_iota(jnp.int32, (16, 128), 0)

    def fix(k, carry):
        i = lst_ref[b * width + k]
        loc = piv_ref[i] - first - b * blk
        at = pl.ds(pl.multiple_of(loc & ~15, 16), 16)
        new = drow_ref[pl.ds(i, 1), :] - acc_ref[at, :]
        old = out_ref[at, :].astype(jnp.float32)
        out_ref[at, :] = jnp.where(sub == (loc & 15), new, old).astype(jnp.bfloat16)
        return carry

    lax.fori_loop(0, cnt_ref[b], fix, 0)

    @pl.when((b == 0) & (first == 0))
    def _():
        out_ref[:width, :] = nat_ref[...].astype(jnp.bfloat16)


def update(cnt, lst, pivots, first, me, trailing, ud, rest, ahead, parts, blk):
    rows, cols = trailing.shape
    width = pivots.shape[0]
    nblk = rows // blk
    tall = pl.BlockSpec((blk, cols), lambda b: (b, 0))
    pair = pl.BlockSpec((2 * width, cols), lambda b: (0, 0))
    return pl.pallas_call(
        functools.partial(update_kernel, nblk),
        grid=(nblk,),
        in_specs=[SMEM] * 5 + [tall, pair, pair] + [VMEM] * 11,
        out_specs=tall,
        scratch_shapes=[
            pltpu.VMEM((blk, cols), jnp.float32),
            pltpu.VMEM((width, cols), jnp.float32),
            pltpu.VMEM((width, cols), jnp.float32),
            pltpu.VMEM((width, cols), jnp.bfloat16),
            pltpu.VMEM((width, cols), jnp.float32),
        ],
        out_shape=jax.ShapeDtypeStruct((rows, cols), jnp.bfloat16),
        compiler_params=params(16),
        name="update",
    )(cnt, lst, pivots, first, me, trailing, ud, rest, ahead, *parts)


def body(trailing, panel_t, pivots):
    rows = trailing.shape[0]
    width = pivots.shape[0]
    blk = rows // NBLK
    half = rows // 2
    barrier = lax.optimization_barrier
    first = (lax.axis_index("prow") * rows).astype(jnp.int32).reshape(1)
    me = lax.axis_index("pcol").astype(jnp.int32).reshape(1)
    trailing = pltpu.with_memory_space_constraint(trailing, pltpu.HBM)

    def zsend(x, pairs):
        return lax.ppermute(x, "prow", pairs)

    p, m, q = [send(panel_t, hop(d, 0, True)) for d in (1, -1, 2)]

    top, cnt, lst = pick(trailing, pivots, first, blk)
    more = zsend(top, [(1, 0), (3, 2), (5, 4), (7, 6)])
    p, m, q, top, more = barrier((p, m, q, top, more))

    up, down, across = hop(0, 1, True), hop(0, -1, True), hop(0, 2, True)
    diag = stack([panel_t, p, m, q], 0, width, "stack_d")
    diag_q = send(diag, across)
    block = stack([panel_t, p, m, q], 0, rows, "stack_p")
    top = add(top, more)
    block, diag_q, top = barrier((block, diag_q, top))
    near, far = send(block, up), send(block, down)
    more = zsend(top, [(2, 0), (6, 4)])
    top = add(top, more)
    top, block2 = barrier((top, block))
    swap = send(block2, CORES)
    more = zsend(top, [(4, 0)])
    more, near, far, swap = barrier((more, near, far, swap))
    own = stack([diag, near, far, diag_q], 0, width, "stack_l")
    other = send(own, CORES)
    fa, fb = stack([near], 0, half, "stack_a"), stack([far], half, half, "stack_b")
    qa, qb = send(fa, up), send(fb, down)
    ud = solve(me, own, other, top, more, trailing)
    ud = choose(first, rows, (2,), ud, zsend(ud, [(0, 2)]))
    ud, near, far = barrier((ud, near, far))
    other_near, other_far = send(near, CORES), send(far, CORES)
    ud = choose(first, rows, (1, 3), ud, zsend(ud, [(0, 1), (2, 3)]))
    rest = zsend(ud, [(i, i + 4) for i in range(4)])
    ahead = stack([qa, qb], 0, 128, "stack_q", 60)
    own = [block, near, far, qa, qb]
    parts = own + [swap, other_near, other_far, send(qa, CORES), send(qb, CORES)]
    return update(cnt, lst, pivots, first, me, trailing, ud, rest, ahead, parts, blk)


def solution(mesh):
    return jax.shard_map(
        body,
        mesh=mesh,
        in_specs=(P("prow", "pcol"), P("pcol", "prow"), P()),
        out_specs=P("prow", "pcol"),
        check_vma=False,
    )
```

```python
import functools

import jax
import jax.numpy as jnp
from jax import lax
from jax.experimental import pallas as pl
from jax.experimental.pallas import tpu as pltpu
from jax.sharding import PartitionSpec as P

NX = 4
NY = 4
OFFSETS = (0, -1, 1, 2)
NBLK = 6
SMEM = pl.BlockSpec(memory_space=pltpu.SMEM)
VMEM = pl.BlockSpec(memory_space=pltpu.VMEM)
HIGHEST = lax.Precision.HIGHEST


def place(x, y, c):
    return ((x % NX) * NY + (y % NY)) * 2 + c


def hop(dx, dy, turn):
    pairs = []
    for x in range(NX):
        for y in range(NY):
            for c in range(2):
                a, b = (dy, dx) if turn and c == 1 else (dx, dy)
                pairs.append((place(x, y, c), place(x + a, y + b, c)))
    return pairs


CORES = [(p, p ^ 1) for p in range(NX * NY * 2)]


def send(block, pairs):
    return lax.ppermute(block, "pcol", pairs)


def params(mib):
    return pltpu.CompilerParams(vmem_limit_bytes=mib << 20)


def cost(us):
    return pl.CostEstimate(flops=int(us * 1.1e9), bytes_accessed=int(us * 3.5e6), transcendentals=0)


def stack_kernel(start, step, *refs):
    def chunk(i, carry):
        src = pl.ds(pl.multiple_of(start + i * step, 128), step)
        dst = pl.ds(pl.multiple_of(i * step, 128), step)
        refs[-1][:, dst] = jnp.concatenate([r[:, src] for r in refs[:-1]], axis=0)
        return carry

    lax.fori_loop(0, refs[-1].shape[1] // step, chunk, 0)


def stack(parts, start, cols, name, us=1):
    rows = sum(p.shape[0] for p in parts)
    return pl.pallas_call(
        functools.partial(stack_kernel, start, min(cols, 1024)),
        in_specs=[VMEM] * len(parts),
        out_specs=VMEM,
        out_shape=jax.ShapeDtypeStruct((rows, cols), jnp.bfloat16),
        compiler_params=params(2),
        cost_estimate=cost(us),
        name=name,
    )(*parts)


def add_kernel(a_ref, b_ref, out_ref):
    out_ref[...] = (a_ref[...].astype(jnp.float32) + b_ref[...].astype(jnp.float32)).astype(jnp.bfloat16)


def add(a, b):
    return pl.pallas_call(
        add_kernel,
        in_specs=[VMEM, VMEM],
        out_specs=VMEM,
        out_shape=jax.ShapeDtypeStruct(a.shape, a.dtype),
        compiler_params=params(2),
        name="add",
    )(a, b)


def choose_kernel(rows, mask, first_ref, a_ref, b_ref, out_ref):
    other = (jnp.int32(mask) >> lax.div(first_ref[0], rows)) & 1

    @pl.when(other == 0)
    def _():
        out_ref[...] = a_ref[...]

    @pl.when(other == 1)
    def _():
        out_ref[...] = b_ref[...]


def choose(first, rows, others, a, b):
    return pl.pallas_call(
        functools.partial(choose_kernel, rows, sum(1 << z for z in others)),
        in_specs=[SMEM, VMEM, VMEM],
        out_specs=VMEM,
        out_shape=jax.ShapeDtypeStruct(a.shape, a.dtype),
        compiler_params=params(2),
        name="choose",
    )(first, a, b)


def join_kernel(rows, mask, first_ref, a_ref, b_ref, below_ref, out_ref):
    width = a_ref.shape[0]
    choose_kernel(rows, mask, first_ref, a_ref, b_ref, out_ref.at[pl.ds(0, width)])
    out_ref[width:, :] = below_ref[...]


def join(first, rows, others, a, b, below):
    width, cols = a.shape
    return pl.pallas_call(
        functools.partial(join_kernel, rows, sum(1 << z for z in others)),
        in_specs=[SMEM] + [VMEM] * 3,
        out_specs=VMEM,
        out_shape=jax.ShapeDtypeStruct((2 * width, cols), a.dtype),
        compiler_params=params(2),
        name="join",
    )(first, a, b, below)


def pick_kernel(blk, piv_ref, first_ref, trailing_ref, out_ref, head_ref, cnt_ref, lst_ref, own_ref, group_ref, rows_ref, sem, head_sem):
    width = piv_ref.shape[0]
    rows = trailing_ref.shape[0]
    first = first_ref[0]
    nblk = cnt_ref.shape[0]
    head = pltpu.make_async_copy(trailing_ref.at[pl.ds(0, width)], head_ref, head_sem)
    head.start()
    for b in range(nblk):
        cnt_ref[b] = 0

    def filt(i, n):
        loc = piv_ref[i] - first
        own_ref[n] = i
        return n + ((loc >= 0) & (loc < rows)).astype(jnp.int32)

    n = lax.fori_loop(0, width, filt, 0, unroll=8)

    def group(k):
        loc = piv_ref[own_ref[k]] - first
        base = pl.multiple_of(loc & ~15, 16)
        return pltpu.make_async_copy(trailing_ref.at[pl.ds(base, 16)], group_ref.at[k], sem)

    def begin(k, carry):
        group(k).start()
        i = own_ref[k]
        b = lax.div(piv_ref[i] - first, blk)
        m = cnt_ref[b]
        lst_ref[b * width + m] = i
        cnt_ref[b] = m + 1
        return carry

    def finish(k, carry):
        group(k).wait()
        return carry

    lax.fori_loop(0, n, begin, 0)
    rows_ref[...] = jnp.zeros_like(rows_ref)
    lax.fori_loop(0, n, finish, 0)
    sub = lax.broadcasted_iota(jnp.int32, (16, 128), 0)

    def extract(k, carry):
        i = own_ref[k]
        loc = piv_ref[i] - first
        tile = group_ref[k].astype(jnp.float32)
        row = jnp.sum(jnp.where(sub == (loc & 15), tile, 0.0), axis=0, keepdims=True)
        rows_ref[pl.ds(i, 1), :] = row
        return carry

    lax.fori_loop(0, n, extract, 0)
    out_ref[...] = rows_ref[...].astype(jnp.bfloat16)
    head.wait()


def pick(trailing, pivots, first, blk):
    rows, cols = trailing.shape
    width = pivots.shape[0]
    nblk = rows // blk
    return pl.pallas_call(
        functools.partial(pick_kernel, blk),
        in_specs=[SMEM, SMEM, pl.BlockSpec(memory_space=pltpu.HBM)],
        out_specs=[VMEM, VMEM, SMEM, SMEM],
        out_shape=[
            jax.ShapeDtypeStruct((width, cols), jnp.bfloat16),
            jax.ShapeDtypeStruct((width, cols), jnp.bfloat16),
            jax.ShapeDtypeStruct((nblk,), jnp.int32),
            jax.ShapeDtypeStruct((nblk * width,), jnp.int32),
        ],
        scratch_shapes=[
            pltpu.SMEM((width + 8,), jnp.int32),
            pltpu.VMEM((width, 16, cols), jnp.bfloat16),
            pltpu.VMEM((width, cols), jnp.float32),
            pltpu.SemaphoreType.DMA,
            pltpu.SemaphoreType.DMA,
        ],
        compiler_params=params(6),
        cost_estimate=cost(12),
        name="pick",
    )(pivots, first, trailing)


def dot(a, b):
    return lax.dot_general(
        a, b, (((1,), (0,)), ((), ())), precision=HIGHEST, preferred_element_type=jnp.float32
    )


def dot_exact(a, b):
    n = b.shape[1]
    hi = b.astype(jnp.bfloat16)
    rest = b - hi.astype(jnp.float32)
    mid = rest.astype(jnp.bfloat16)
    low = (rest - mid.astype(jnp.float32)).astype(jnp.bfloat16)
    r = lax.dot_general(
        a, jnp.concatenate([hi, mid, low], axis=1), (((1,), (0,)), ((), ())),
        preferred_element_type=jnp.float32,
    )
    return r[:, 2 * n :] + r[:, n : 2 * n] + r[:, :n]


def unit_inverse(strict):
    n = strict.shape[0]
    r = lax.broadcasted_iota(jnp.int32, (n, n), 0)
    c = lax.broadcasted_iota(jnp.int32, (n, n), 1)
    d = jnp.where((r >> 4) == (c >> 4), strict, 0.0)
    x = jnp.where(r == c, 1.0, 0.0) - d
    for step in range(3):
        d = dot_exact(d.astype(jnp.bfloat16), d) if step == 0 else dot(d, d)
        x = x + dot(x, d)
    for lg in (4, 5, 6):
        inside = ((r >> (lg + 1)) == (c >> (lg + 1))) & ((r >> lg) != (c >> lg))
        part = jnp.where(inside, strict, 0.0).astype(jnp.bfloat16)
        x = x - dot(x, dot_exact(part, x))
    return x


def blocks():
    return [(k, outer, inner) for k in range(2) for outer in OFFSETS for inner in OFFSETS]


def block_at(me, k, outer, inner):
    core = (me & 1) ^ k
    dx = jnp.where(core == 0, inner, outer)
    dy = jnp.where(core == 0, outer, inner)
    x = ((me >> 3) + dx) & 3
    y = ((me >> 1) + dy) & 3
    return pl.ds(pl.multiple_of(((x * 4 + y) * 2 + core) * 8, 8), 8)


def solve_kernel(me_ref, own_ref, other_ref, top_ref, more_ref, out_ref, a_ref, g_ref):
    n = top_ref.shape[0]
    h = n // 2
    me = me_ref[0]
    g_ref[:h, :] = own_ref[...].astype(jnp.float32)
    g_ref[h:, :] = other_ref[...].astype(jnp.float32)
    for b, where in enumerate(blocks()):
        a_ref[block_at(me, *where), :] = g_ref[8 * b : 8 * b + 8, :]
    r = lax.broadcasted_iota(jnp.int32, (h, h), 0)
    c = lax.broadcasted_iota(jnp.int32, (h, h), 1)
    s11 = jnp.where(r > c, a_ref[:h, :h].T, 0.0)
    s22 = jnp.where(r > c, a_ref[h:, h:].T, 0.0)
    s21 = a_ref[:h, h:].T
    x1 = unit_inverse(s11)
    x2 = unit_inverse(s22)
    top = sum(r[...].astype(jnp.float32) for r in (top_ref, more_ref))
    u1 = dot(x1, top[:h])
    u2 = dot(x2, top[h:] - dot_exact(s21.astype(jnp.bfloat16), u1))
    out_ref[...] = jnp.concatenate([u1, u2], axis=0).astype(jnp.bfloat16)


def solve(me, own, other, top, more):
    n, cols = top.shape
    return pl.pallas_call(
        solve_kernel,
        in_specs=[SMEM] + [VMEM] * 4,
        out_specs=VMEM,
        out_shape=jax.ShapeDtypeStruct((n, cols), jnp.bfloat16),
        scratch_shapes=[pltpu.VMEM((n, n), jnp.float32), pltpu.VMEM((n, n), jnp.float32)],
        compiler_params=params(10),
        name="solve",
    )(me, own, other, top, more)


def update_kernel(nblk, cnt_ref, lst_ref, piv_ref, first_ref, me_ref, tr_ref, ud_ref, rest_ref, *refs):
    parts = refs[1:11]
    out_ref, acc_ref, nat_ref, drow_ref, u_ref, tmp_ref = refs[11:]
    blk = out_ref.shape[0]
    width = nat_ref.shape[0]
    b = pl.program_id(0)
    first = first_ref[0]

    @pl.when(b == 0)
    def _():
        late = lax.div(first, nblk * blk) >> 2

        @pl.when(late == 0)
        def _():
            nat_ref[...] = ud_ref[:width, :].astype(jnp.float32)
            drow_ref[...] = ud_ref[width:, :].astype(jnp.float32)

        @pl.when(late == 1)
        def _():
            nat_ref[...] = rest_ref[:width, :].astype(jnp.float32)
            drow_ref[...] = rest_ref[width:, :].astype(jnp.float32)

        for i, where in enumerate(blocks()):
            tmp_ref[8 * i : 8 * i + 8, :] = nat_ref[block_at(me_ref[0], *where), :]
        u_ref[...] = tmp_ref[...].astype(jnp.bfloat16)

    def compute(half):
        here = pl.ds(pl.multiple_of(b * blk, 128), blk)
        there = pl.ds(pl.multiple_of((b - half * (nblk // 2)) * blk, 128), blk)
        pieces = []
        for s in (parts[:5], parts[5:]):
            pieces += [s[0][:, here], s[1][:, here], s[2][:, here], s[3 + half][:, there]]
        acc_ref[...] = lax.dot_general(
            jnp.concatenate(pieces, axis=0), u_ref[...], (((0,), (0,)), ((), ())),
            preferred_element_type=jnp.float32,
        )

    @pl.when(b < nblk // 2)
    def _():
        compute(0)

    @pl.when(b >= nblk // 2)
    def _():
        compute(1)

    out_ref[...] = (tr_ref[...].astype(jnp.float32) - acc_ref[...]).astype(jnp.bfloat16)
    sub = lax.broadcasted_iota(jnp.int32, (16, 128), 0)

    def fix(k, carry):
        i = lst_ref[b * width + k]
        loc = piv_ref[i] - first - b * blk
        at = pl.ds(pl.multiple_of(loc & ~15, 16), 16)
        new = drow_ref[pl.ds(i, 1), :] - acc_ref[at, :]
        old = out_ref[at, :].astype(jnp.float32)
        out_ref[at, :] = jnp.where(sub == (loc & 15), new, old).astype(jnp.bfloat16)
        return carry

    lax.fori_loop(0, cnt_ref[b], fix, 0)

    @pl.when((b == 0) & (first == 0))
    def _():
        out_ref[:width, :] = nat_ref[...].astype(jnp.bfloat16)


def update(cnt, lst, pivots, first, me, trailing, ud, rest, ahead, parts, blk):
    rows, cols = trailing.shape
    width = pivots.shape[0]
    nblk = rows // blk
    tall = pl.BlockSpec((blk, cols), lambda b: (b, 0))
    pair = pl.BlockSpec((2 * width, cols), lambda b: (0, 0))
    return pl.pallas_call(
        functools.partial(update_kernel, nblk),
        grid=(nblk,),
        in_specs=[SMEM] * 5 + [tall, pair, pair] + [VMEM] * 11,
        out_specs=tall,
        scratch_shapes=[
            pltpu.VMEM((blk, cols), jnp.float32),
            pltpu.VMEM((width, cols), jnp.float32),
            pltpu.VMEM((width, cols), jnp.float32),
            pltpu.VMEM((width, cols), jnp.bfloat16),
            pltpu.VMEM((width, cols), jnp.float32),
        ],
        out_shape=jax.ShapeDtypeStruct((rows, cols), jnp.bfloat16),
        compiler_params=params(16),
        name="update",
    )(cnt, lst, pivots, first, me, trailing, ud, rest, ahead, *parts)


def body(trailing, panel_t, pivots):
    rows = trailing.shape[0]
    width = pivots.shape[0]
    blk = rows // NBLK
    half = rows // 2
    barrier = lax.optimization_barrier
    first = (lax.axis_index("prow") * rows).astype(jnp.int32).reshape(1)
    me = lax.axis_index("pcol").astype(jnp.int32).reshape(1)
    trailing = pltpu.with_memory_space_constraint(trailing, pltpu.HBM)

    def zsend(x, pairs):
        return lax.ppermute(x, "prow", pairs)

    p, m, q = [send(panel_t, hop(d, 0, True)) for d in (1, -1, 2)]

    top, disp, cnt, lst = pick(trailing, pivots, first, blk)
    more = zsend(top, [(1, 0), (3, 2), (5, 4), (7, 6)])
    lower = zsend(disp, [(0, 2)])
    p, m, q, top, more, lower = barrier((p, m, q, top, more, lower))

    up, down, across = hop(0, 1, True), hop(0, -1, True), hop(0, 2, True)
    diag = stack([panel_t, p, m, q], 0, width, "stack_d")
    diag_q, diag_p, diag_m = send(diag, across), send(diag, up), send(diag, down)
    block = stack([panel_t, p, m, q], 0, rows, "stack_p")
    block, diag_q, diag_p, diag_m = barrier((block, diag_q, diag_p, diag_m))
    near, far = send(block, up), send(block, down)
    own = stack([diag, diag_p, diag_m, diag_q], 0, width, "stack_l")
    top, more, block2 = barrier((top, more, block))
    top = add(top, more)
    more = zsend(top, [(2, 0), (6, 4)])
    top = add(top, more)
    more = zsend(top, [(4, 0)])
    other = send(own, CORES)
    disp = choose(first, rows, (2,), disp, lower)
    disp = choose(first, rows, (1, 3), disp, zsend(disp, [(0, 1), (2, 3)]))
    swap = send(block, CORES)
    u = solve(me, own, other, top, more)
    u, near, far, swap, disp = barrier((u, near, far, swap, disp))
    fa, fb = stack([near], 0, half, "stack_a"), stack([far], half, half, "stack_b")
    qa, qb = send(fa, up), send(fb, down)
    u = choose(first, rows, (2,), u, zsend(u, [(0, 2)]))
    u, near, far = barrier((u, near, far))
    other_near, other_far = send(near, CORES), send(far, CORES)
    ud = join(first, rows, (1, 3), u, zsend(u, [(0, 1), (2, 3)]), disp)
    rest = zsend(ud, [(i, i + 4) for i in range(4)])
    ahead = stack([qa, qb], 0, 128, "stack_q", 60)
    own = [block, near, far, qa, qb]
    parts = own + [swap, other_near, other_far, send(qa, CORES), send(qb, CORES)]
    return update(cnt, lst, pivots, first, me, trailing, ud, rest, ahead, parts, blk)


def solution(mesh):
    return jax.shard_map(
        body,
        mesh=mesh,
        in_specs=(P("prow", "pcol"), P("pcol", "prow"), P()),
        out_specs=P("prow", "pcol"),
        check_vma=False,
    )
```

```python
import functools

import jax
import jax.numpy as jnp
from jax import lax
from jax.experimental import pallas as pl
from jax.experimental.pallas import tpu as pltpu
from jax.sharding import PartitionSpec as P

NX = 4
NY = 4
OFFSETS = (0, -1, 1, 2)
NBLK = 6
SMEM = pl.BlockSpec(memory_space=pltpu.SMEM)
VMEM = pl.BlockSpec(memory_space=pltpu.VMEM)
HIGHEST = lax.Precision.HIGHEST


def place(x, y, c):
    return ((x % NX) * NY + (y % NY)) * 2 + c


def hop(dx, dy, turn):
    pairs = []
    for x in range(NX):
        for y in range(NY):
            for c in range(2):
                a, b = (dy, dx) if turn and c == 1 else (dx, dy)
                pairs.append((place(x, y, c), place(x + a, y + b, c)))
    return pairs


CORES = [(p, p ^ 1) for p in range(NX * NY * 2)]


def send(block, pairs):
    return lax.ppermute(block, "pcol", pairs)


def params(mib):
    return pltpu.CompilerParams(vmem_limit_bytes=mib << 20)


def cost(us):
    return pl.CostEstimate(flops=int(us * 1.1e9), bytes_accessed=int(us * 3.5e6), transcendentals=0)


def stack_kernel(start, step, *refs):
    def chunk(i, carry):
        src = pl.ds(pl.multiple_of(start + i * step, 128), step)
        dst = pl.ds(pl.multiple_of(i * step, 128), step)
        refs[-1][:, dst] = jnp.concatenate([r[:, src] for r in refs[:-1]], axis=0)
        return carry

    lax.fori_loop(0, refs[-1].shape[1] // step, chunk, 0)


def stack(parts, start, cols, name, us=1):
    rows = sum(p.shape[0] for p in parts)
    return pl.pallas_call(
        functools.partial(stack_kernel, start, min(cols, 1024)),
        in_specs=[VMEM] * len(parts),
        out_specs=VMEM,
        out_shape=jax.ShapeDtypeStruct((rows, cols), jnp.bfloat16),
        compiler_params=params(2),
        cost_estimate=cost(us),
        name=name,
    )(*parts)


def add_kernel(a_ref, b_ref, out_ref):
    out_ref[...] = (a_ref[...].astype(jnp.float32) + b_ref[...].astype(jnp.float32)).astype(jnp.bfloat16)


def add(a, b):
    return pl.pallas_call(
        add_kernel,
        in_specs=[VMEM, VMEM],
        out_specs=VMEM,
        out_shape=jax.ShapeDtypeStruct(a.shape, a.dtype),
        compiler_params=params(2),
        name="add",
    )(a, b)


def choose_kernel(rows, mask, first_ref, a_ref, b_ref, out_ref):
    other = (jnp.int32(mask) >> lax.div(first_ref[0], rows)) & 1

    @pl.when(other == 0)
    def _():
        out_ref[...] = a_ref[...]

    @pl.when(other == 1)
    def _():
        out_ref[...] = b_ref[...]


def choose(first, rows, others, a, b):
    return pl.pallas_call(
        functools.partial(choose_kernel, rows, sum(1 << z for z in others)),
        in_specs=[SMEM, VMEM, VMEM],
        out_specs=VMEM,
        out_shape=jax.ShapeDtypeStruct(a.shape, a.dtype),
        compiler_params=params(2),
        name="choose",
    )(first, a, b)


def join_kernel(rows, mask, first_ref, a_ref, b_ref, below_ref, out_ref):
    width = a_ref.shape[0]
    choose_kernel(rows, mask, first_ref, a_ref, b_ref, out_ref.at[pl.ds(0, width)])
    out_ref[width:, :] = below_ref[...]


def join(first, rows, others, a, b, below):
    width, cols = a.shape
    return pl.pallas_call(
        functools.partial(join_kernel, rows, sum(1 << z for z in others)),
        in_specs=[SMEM] + [VMEM] * 3,
        out_specs=VMEM,
        out_shape=jax.ShapeDtypeStruct((2 * width, cols), a.dtype),
        compiler_params=params(2),
        name="join",
    )(first, a, b, below)


def pick_kernel(blk, piv_ref, first_ref, trailing_ref, out_ref, head_ref, cnt_ref, lst_ref, own_ref, group_ref, rows_ref, sem, head_sem):
    width = piv_ref.shape[0]
    rows = trailing_ref.shape[0]
    first = first_ref[0]
    nblk = cnt_ref.shape[0]
    head = pltpu.make_async_copy(trailing_ref.at[pl.ds(0, width)], head_ref, head_sem)
    head.start()
    for b in range(nblk):
        cnt_ref[b] = 0

    def filt(i, n):
        loc = piv_ref[i] - first
        own_ref[n] = i
        return n + ((loc >= 0) & (loc < rows)).astype(jnp.int32)

    n = lax.fori_loop(0, width, filt, 0, unroll=8)

    def group(k):
        loc = piv_ref[own_ref[k]] - first
        base = pl.multiple_of(loc & ~15, 16)
        return pltpu.make_async_copy(trailing_ref.at[pl.ds(base, 16)], group_ref.at[k], sem)

    def begin(k, carry):
        group(k).start()
        i = own_ref[k]
        b = lax.div(piv_ref[i] - first, blk)
        m = cnt_ref[b]
        lst_ref[b * width + m] = i
        cnt_ref[b] = m + 1
        return carry

    def finish(k, carry):
        group(k).wait()
        return carry

    lax.fori_loop(0, n, begin, 0)
    rows_ref[...] = jnp.zeros_like(rows_ref)
    lax.fori_loop(0, n, finish, 0)
    sub = lax.broadcasted_iota(jnp.int32, (16, 128), 0)

    def extract(k, carry):
        i = own_ref[k]
        loc = piv_ref[i] - first
        tile = group_ref[k].astype(jnp.float32)
        row = jnp.sum(jnp.where(sub == (loc & 15), tile, 0.0), axis=0, keepdims=True)
        rows_ref[pl.ds(i, 1), :] = row
        return carry

    lax.fori_loop(0, n, extract, 0)
    out_ref[...] = rows_ref[...].astype(jnp.bfloat16)
    head.wait()


def pick(trailing, pivots, first, blk):
    rows, cols = trailing.shape
    width = pivots.shape[0]
    nblk = rows // blk
    return pl.pallas_call(
        functools.partial(pick_kernel, blk),
        in_specs=[SMEM, SMEM, pl.BlockSpec(memory_space=pltpu.HBM)],
        out_specs=[VMEM, VMEM, SMEM, SMEM],
        out_shape=[
            jax.ShapeDtypeStruct((width, cols), jnp.bfloat16),
            jax.ShapeDtypeStruct((width, cols), jnp.bfloat16),
            jax.ShapeDtypeStruct((nblk,), jnp.int32),
            jax.ShapeDtypeStruct((nblk * width,), jnp.int32),
        ],
        scratch_shapes=[
            pltpu.SMEM((width + 8,), jnp.int32),
            pltpu.VMEM((width, 16, cols), jnp.bfloat16),
            pltpu.VMEM((width, cols), jnp.float32),
            pltpu.SemaphoreType.DMA,
            pltpu.SemaphoreType.DMA,
        ],
        compiler_params=params(6),
        cost_estimate=cost(12),
        name="pick",
    )(pivots, first, trailing)


def dot(a, b):
    return lax.dot_general(
        a, b, (((1,), (0,)), ((), ())), precision=HIGHEST, preferred_element_type=jnp.float32
    )


def dot_exact(a, b):
    n = b.shape[1]
    hi = b.astype(jnp.bfloat16)
    rest = b - hi.astype(jnp.float32)
    mid = rest.astype(jnp.bfloat16)
    low = (rest - mid.astype(jnp.float32)).astype(jnp.bfloat16)
    r = lax.dot_general(
        a, jnp.concatenate([hi, mid, low], axis=1), (((1,), (0,)), ((), ())),
        preferred_element_type=jnp.float32,
    )
    return r[:, 2 * n :] + r[:, n : 2 * n] + r[:, :n]


def unit_inverse(strict):
    n = strict.shape[0]
    r = lax.broadcasted_iota(jnp.int32, (n, n), 0)
    c = lax.broadcasted_iota(jnp.int32, (n, n), 1)
    d = jnp.where((r >> 4) == (c >> 4), strict, 0.0)
    x = jnp.where(r == c, 1.0, 0.0) - d
    for step in range(3):
        d = dot_exact(d.astype(jnp.bfloat16), d) if step == 0 else dot(d, d)
        x = x + dot(x, d)
    for lg in (4, 5, 6):
        inside = ((r >> (lg + 1)) == (c >> (lg + 1))) & ((r >> lg) != (c >> lg))
        part = jnp.where(inside, strict, 0.0).astype(jnp.bfloat16)
        x = x - dot(x, dot_exact(part, x))
    return x


def blocks():
    return [(k, outer, inner) for k in range(2) for outer in OFFSETS for inner in OFFSETS]


def block_at(me, k, outer, inner):
    core = (me & 1) ^ k
    dx = jnp.where(core == 0, inner, outer)
    dy = jnp.where(core == 0, outer, inner)
    x = ((me >> 3) + dx) & 3
    y = ((me >> 1) + dy) & 3
    return pl.ds(pl.multiple_of(((x * 4 + y) * 2 + core) * 8, 8), 8)


def solve_kernel(me_ref, own_ref, other_ref, top_ref, more_ref, out_ref, a_ref, g_ref):
    n = top_ref.shape[0]
    h = n // 2
    me = me_ref[0]
    g_ref[:h, :] = own_ref[...].astype(jnp.float32)
    g_ref[h:, :] = other_ref[...].astype(jnp.float32)
    for b, where in enumerate(blocks()):
        a_ref[block_at(me, *where), :] = g_ref[8 * b : 8 * b + 8, :]
    r = lax.broadcasted_iota(jnp.int32, (h, h), 0)
    c = lax.broadcasted_iota(jnp.int32, (h, h), 1)
    s11 = jnp.where(r > c, a_ref[:h, :h].T, 0.0)
    s22 = jnp.where(r > c, a_ref[h:, h:].T, 0.0)
    s21 = a_ref[:h, h:].T
    x1 = unit_inverse(s11)
    x2 = unit_inverse(s22)
    top = sum(r[...].astype(jnp.float32) for r in (top_ref, more_ref))
    u1 = dot(x1, top[:h])
    u2 = dot(x2, top[h:] - dot_exact(s21.astype(jnp.bfloat16), u1))
    out_ref[...] = jnp.concatenate([u1, u2], axis=0).astype(jnp.bfloat16)


def solve(me, own, other, top, more):
    n, cols = top.shape
    return pl.pallas_call(
        solve_kernel,
        in_specs=[SMEM] + [VMEM] * 4,
        out_specs=VMEM,
        out_shape=jax.ShapeDtypeStruct((n, cols), jnp.bfloat16),
        scratch_shapes=[pltpu.VMEM((n, n), jnp.float32), pltpu.VMEM((n, n), jnp.float32)],
        compiler_params=params(10),
        name="solve",
    )(me, own, other, top, more)


def update_kernel(nblk, cnt_ref, lst_ref, piv_ref, first_ref, me_ref, tr_ref, ud_ref, rest_ref, *refs):
    parts = refs[1:11]
    out_ref, acc_ref, nat_ref, drow_ref, u_ref, tmp_ref = refs[11:]
    blk = out_ref.shape[0]
    width = nat_ref.shape[0]
    b = pl.program_id(0)
    first = first_ref[0]

    @pl.when(b == 0)
    def _():
        late = lax.div(first, nblk * blk) >> 2

        @pl.when(late == 0)
        def _():
            nat_ref[...] = ud_ref[:width, :].astype(jnp.float32)
            drow_ref[...] = ud_ref[width:, :].astype(jnp.float32)

        @pl.when(late == 1)
        def _():
            nat_ref[...] = rest_ref[:width, :].astype(jnp.float32)
            drow_ref[...] = rest_ref[width:, :].astype(jnp.float32)

        for i, where in enumerate(blocks()):
            tmp_ref[8 * i : 8 * i + 8, :] = nat_ref[block_at(me_ref[0], *where), :]
        u_ref[...] = tmp_ref[...].astype(jnp.bfloat16)

    def compute(half):
        here = pl.ds(pl.multiple_of(b * blk, 128), blk)
        there = pl.ds(pl.multiple_of((b - half * (nblk // 2)) * blk, 128), blk)
        pieces = []
        for s in (parts[:5], parts[5:]):
            pieces += [s[0][:, here], s[1][:, here], s[2][:, here], s[3 + half][:, there]]
        acc_ref[...] = lax.dot_general(
            jnp.concatenate(pieces, axis=0), u_ref[...], (((0,), (0,)), ((), ())),
            preferred_element_type=jnp.float32,
        )

    @pl.when(b < nblk // 2)
    def _():
        compute(0)

    @pl.when(b >= nblk // 2)
    def _():
        compute(1)

    out_ref[...] = (tr_ref[...].astype(jnp.float32) - acc_ref[...]).astype(jnp.bfloat16)
    sub = lax.broadcasted_iota(jnp.int32, (16, 128), 0)

    def fix(k, carry):
        i = lst_ref[b * width + k]
        loc = piv_ref[i] - first - b * blk
        at = pl.ds(pl.multiple_of(loc & ~15, 16), 16)
        new = drow_ref[pl.ds(i, 1), :] - acc_ref[at, :]
        old = out_ref[at, :].astype(jnp.float32)
        out_ref[at, :] = jnp.where(sub == (loc & 15), new, old).astype(jnp.bfloat16)
        return carry

    lax.fori_loop(0, cnt_ref[b], fix, 0)

    @pl.when((b == 0) & (first == 0))
    def _():
        out_ref[:width, :] = nat_ref[...].astype(jnp.bfloat16)


def update(cnt, lst, pivots, first, me, trailing, ud, rest, ahead, parts, blk):
    rows, cols = trailing.shape
    width = pivots.shape[0]
    nblk = rows // blk
    tall = pl.BlockSpec((blk, cols), lambda b: (b, 0))
    pair = pl.BlockSpec((2 * width, cols), lambda b: (0, 0))
    return pl.pallas_call(
        functools.partial(update_kernel, nblk),
        grid=(nblk,),
        in_specs=[SMEM] * 5 + [tall, pair, pair] + [VMEM] * 11,
        out_specs=tall,
        scratch_shapes=[
            pltpu.VMEM((blk, cols), jnp.float32),
            pltpu.VMEM((width, cols), jnp.float32),
            pltpu.VMEM((width, cols), jnp.float32),
            pltpu.VMEM((width, cols), jnp.bfloat16),
            pltpu.VMEM((width, cols), jnp.float32),
        ],
        out_shape=jax.ShapeDtypeStruct((rows, cols), jnp.bfloat16),
        compiler_params=params(16),
        name="update",
    )(cnt, lst, pivots, first, me, trailing, ud, rest, ahead, *parts)


def body(trailing, panel_t, pivots):
    rows = trailing.shape[0]
    width = pivots.shape[0]
    blk = rows // NBLK
    half = rows // 2
    barrier = lax.optimization_barrier
    first = (lax.axis_index("prow") * rows).astype(jnp.int32).reshape(1)
    me = lax.axis_index("pcol").astype(jnp.int32).reshape(1)
    trailing = pltpu.with_memory_space_constraint(trailing, pltpu.HBM)

    def zsend(x, pairs):
        return lax.ppermute(x, "prow", pairs)

    p, m, q = [send(panel_t, hop(d, 0, True)) for d in (1, -1, 2)]

    top, disp, cnt, lst = pick(trailing, pivots, first, blk)
    more = zsend(top, [(i + 4, i) for i in range(4)])
    p, m, q, top = barrier((p, m, q, top))

    up, down, across = hop(0, 1, True), hop(0, -1, True), hop(0, 2, True)
    diag = stack([panel_t, p, m, q], 0, width, "stack_d")
    diag_q, diag_p, diag_m = send(diag, across), send(diag, up), send(diag, down)
    block = stack([panel_t, p, m, q], 0, rows, "stack_p")
    block, diag_q, diag_p, diag_m, top, more = barrier((block, diag_q, diag_p, diag_m, top, more))
    near, far = send(block, up), send(block, down)
    own = stack([diag, diag_p, diag_m, diag_q], 0, width, "stack_l")
    top = add(top, more)
    more = zsend(top, [(2, 0), (3, 1)])
    other = send(own, CORES)
    top = add(top, more)
    top, disp, other = barrier((top, disp, other))
    more = zsend(top, [(1, 0)])
    lower = zsend(disp, [(0, 2)])
    top, block2 = barrier((top, block))
    swap = send(block2, CORES)
    more, disp, lower = barrier((more, disp, lower))
    u = solve(me, own, other, top, more)
    disp = choose(first, rows, (2,), disp, lower)
    disp = choose(first, rows, (1, 3), disp, zsend(disp, [(0, 1), (2, 3)]))
    u, near, far, swap, disp = barrier((u, near, far, swap, disp))
    fa, fb = stack([near], 0, half, "stack_a"), stack([far], half, half, "stack_b")
    qa, qb = send(fa, up), send(fb, down)
    u = choose(first, rows, (2,), u, zsend(u, [(0, 2)]))
    u, near, far = barrier((u, near, far))
    other_near, other_far = send(near, CORES), send(far, CORES)
    ud = join(first, rows, (1, 3), u, zsend(u, [(0, 1), (2, 3)]), disp)
    rest = zsend(ud, [(i, i + 4) for i in range(4)])
    ahead = stack([qa, qb], 0, 128, "stack_q", 60)
    own = [block, near, far, qa, qb]
    parts = own + [swap, other_near, other_far, send(qa, CORES), send(qb, CORES)]
    return update(cnt, lst, pivots, first, me, trailing, ud, rest, ahead, parts, blk)


def solution(mesh):
    return jax.shard_map(
        body,
        mesh=mesh,
        in_specs=(P("prow", "pcol"), P("pcol", "prow"), P()),
        out_specs=P("prow", "pcol"),
        check_vma=False,
    )
```

```python
import functools

import jax
import jax.numpy as jnp
from jax import lax
from jax.experimental import pallas as pl
from jax.experimental.pallas import tpu as pltpu
from jax.sharding import PartitionSpec as P

NX = 4
NY = 4
OFFSETS = (0, -1, 1, 2)
NBLK = 6
SMEM = pl.BlockSpec(memory_space=pltpu.SMEM)
VMEM = pl.BlockSpec(memory_space=pltpu.VMEM)
HIGHEST = lax.Precision.HIGHEST


def place(x, y, c):
    return ((x % NX) * NY + (y % NY)) * 2 + c


def hop(dx, dy, turn):
    pairs = []
    for x in range(NX):
        for y in range(NY):
            for c in range(2):
                a, b = (dy, dx) if turn and c == 1 else (dx, dy)
                pairs.append((place(x, y, c), place(x + a, y + b, c)))
    return pairs


CORES = [(p, p ^ 1) for p in range(NX * NY * 2)]


def send(block, pairs):
    return lax.ppermute(block, "pcol", pairs)


def params(mib):
    return pltpu.CompilerParams(vmem_limit_bytes=mib << 20)


def cost(us):
    return pl.CostEstimate(flops=int(us * 1.1e9), bytes_accessed=int(us * 3.5e6), transcendentals=0)


def stack_kernel(start, step, *refs):
    def chunk(i, carry):
        src = pl.ds(pl.multiple_of(start + i * step, 128), step)
        dst = pl.ds(pl.multiple_of(i * step, 128), step)
        refs[-1][:, dst] = jnp.concatenate([r[:, src] for r in refs[:-1]], axis=0)
        return carry

    lax.fori_loop(0, refs[-1].shape[1] // step, chunk, 0)


def stack(parts, start, cols, name, us=1):
    rows = sum(p.shape[0] for p in parts)
    return pl.pallas_call(
        functools.partial(stack_kernel, start, min(cols, 1024)),
        in_specs=[VMEM] * len(parts),
        out_specs=VMEM,
        out_shape=jax.ShapeDtypeStruct((rows, cols), jnp.bfloat16),
        compiler_params=params(2),
        cost_estimate=cost(us),
        name=name,
    )(*parts)


def add_kernel(a_ref, b_ref, out_ref):
    out_ref[...] = (a_ref[...].astype(jnp.float32) + b_ref[...].astype(jnp.float32)).astype(jnp.bfloat16)


def add(a, b):
    return pl.pallas_call(
        add_kernel,
        in_specs=[VMEM, VMEM],
        out_specs=VMEM,
        out_shape=jax.ShapeDtypeStruct(a.shape, a.dtype),
        compiler_params=params(2),
        name="add",
    )(a, b)


def choose_kernel(rows, mask, first_ref, a_ref, b_ref, out_ref):
    other = (jnp.int32(mask) >> lax.div(first_ref[0], rows)) & 1

    @pl.when(other == 0)
    def _():
        out_ref[...] = a_ref[...]

    @pl.when(other == 1)
    def _():
        out_ref[...] = b_ref[...]


def choose(first, rows, others, a, b):
    return pl.pallas_call(
        functools.partial(choose_kernel, rows, sum(1 << z for z in others)),
        in_specs=[SMEM, VMEM, VMEM],
        out_specs=VMEM,
        out_shape=jax.ShapeDtypeStruct(a.shape, a.dtype),
        compiler_params=params(2),
        name="choose",
    )(first, a, b)


def join_kernel(rows, mask, first_ref, a_ref, b_ref, below_ref, out_ref):
    width = a_ref.shape[0]
    choose_kernel(rows, mask, first_ref, a_ref, b_ref, out_ref.at[pl.ds(0, width)])
    out_ref[width:, :] = below_ref[...]


def join(first, rows, others, a, b, below):
    width, cols = a.shape
    return pl.pallas_call(
        functools.partial(join_kernel, rows, sum(1 << z for z in others)),
        in_specs=[SMEM] + [VMEM] * 3,
        out_specs=VMEM,
        out_shape=jax.ShapeDtypeStruct((2 * width, cols), a.dtype),
        compiler_params=params(2),
        name="join",
    )(first, a, b, below)


def pick_kernel(blk, piv_ref, first_ref, trailing_ref, out_ref, head_ref, cnt_ref, lst_ref, own_ref, group_ref, rows_ref, sem, head_sem):
    width = piv_ref.shape[0]
    rows = trailing_ref.shape[0]
    first = first_ref[0]
    nblk = cnt_ref.shape[0]
    head = pltpu.make_async_copy(trailing_ref.at[pl.ds(0, width)], head_ref, head_sem)
    head.start()
    for b in range(nblk):
        cnt_ref[b] = 0

    def filt(i, n):
        loc = piv_ref[i] - first
        own_ref[n] = i
        return n + ((loc >= 0) & (loc < rows)).astype(jnp.int32)

    n = lax.fori_loop(0, width, filt, 0, unroll=8)

    def group(k):
        loc = piv_ref[own_ref[k]] - first
        base = pl.multiple_of(loc & ~15, 16)
        return pltpu.make_async_copy(trailing_ref.at[pl.ds(base, 16)], group_ref.at[k], sem)

    def begin(k, carry):
        group(k).start()
        i = own_ref[k]
        b = lax.div(piv_ref[i] - first, blk)
        m = cnt_ref[b]
        lst_ref[b * width + m] = i
        cnt_ref[b] = m + 1
        return carry

    def finish(k, carry):
        group(k).wait()
        return carry

    lax.fori_loop(0, n, begin, 0)
    rows_ref[...] = jnp.zeros_like(rows_ref)
    lax.fori_loop(0, n, finish, 0)
    sub = lax.broadcasted_iota(jnp.int32, (16, 128), 0)

    def extract(k, carry):
        i = own_ref[k]
        loc = piv_ref[i] - first
        tile = group_ref[k].astype(jnp.float32)
        row = jnp.sum(jnp.where(sub == (loc & 15), tile, 0.0), axis=0, keepdims=True)
        rows_ref[pl.ds(i, 1), :] = row
        return carry

    lax.fori_loop(0, n, extract, 0)
    out_ref[...] = rows_ref[...].astype(jnp.bfloat16)
    head.wait()


def pick(trailing, pivots, first, blk):
    rows, cols = trailing.shape
    width = pivots.shape[0]
    nblk = rows // blk
    return pl.pallas_call(
        functools.partial(pick_kernel, blk),
        in_specs=[SMEM, SMEM, pl.BlockSpec(memory_space=pltpu.HBM)],
        out_specs=[VMEM, VMEM, SMEM, SMEM],
        out_shape=[
            jax.ShapeDtypeStruct((width, cols), jnp.bfloat16),
            jax.ShapeDtypeStruct((width, cols), jnp.bfloat16),
            jax.ShapeDtypeStruct((nblk,), jnp.int32),
            jax.ShapeDtypeStruct((nblk * width,), jnp.int32),
        ],
        scratch_shapes=[
            pltpu.SMEM((width + 8,), jnp.int32),
            pltpu.VMEM((width, 16, cols), jnp.bfloat16),
            pltpu.VMEM((width, cols), jnp.float32),
            pltpu.SemaphoreType.DMA,
            pltpu.SemaphoreType.DMA,
        ],
        compiler_params=params(6),
        cost_estimate=cost(12),
        name="pick",
    )(pivots, first, trailing)


def dot(a, b):
    return lax.dot_general(
        a, b, (((1,), (0,)), ((), ())), precision=HIGHEST, preferred_element_type=jnp.float32
    )


def dot_exact(a, b):
    n = b.shape[1]
    hi = b.astype(jnp.bfloat16)
    rest = b - hi.astype(jnp.float32)
    mid = rest.astype(jnp.bfloat16)
    low = (rest - mid.astype(jnp.float32)).astype(jnp.bfloat16)
    r = lax.dot_general(
        a, jnp.concatenate([hi, mid, low], axis=1), (((1,), (0,)), ((), ())),
        preferred_element_type=jnp.float32,
    )
    return r[:, 2 * n :] + r[:, n : 2 * n] + r[:, :n]


def unit_inverse(strict):
    n = strict.shape[0]
    r = lax.broadcasted_iota(jnp.int32, (n, n), 0)
    c = lax.broadcasted_iota(jnp.int32, (n, n), 1)
    d = jnp.where((r >> 4) == (c >> 4), strict, 0.0)
    x = jnp.where(r == c, 1.0, 0.0) - d
    for step in range(3):
        d = dot_exact(d.astype(jnp.bfloat16), d) if step == 0 else dot(d, d)
        x = x + dot(x, d)
    for lg in (4, 5, 6):
        inside = ((r >> (lg + 1)) == (c >> (lg + 1))) & ((r >> lg) != (c >> lg))
        part = jnp.where(inside, strict, 0.0).astype(jnp.bfloat16)
        x = x - dot(x, dot_exact(part, x))
    return x


def blocks():
    return [(k, outer, inner) for k in range(2) for outer in OFFSETS for inner in OFFSETS]


def block_at(me, k, outer, inner):
    core = (me & 1) ^ k
    dx = jnp.where(core == 0, inner, outer)
    dy = jnp.where(core == 0, outer, inner)
    x = ((me >> 3) + dx) & 3
    y = ((me >> 1) + dy) & 3
    return pl.ds(pl.multiple_of(((x * 4 + y) * 2 + core) * 8, 8), 8)


def solve_kernel(me_ref, own_ref, other_ref, top_ref, more_ref, out_ref, a_ref, g_ref):
    n = top_ref.shape[0]
    h = n // 2
    me = me_ref[0]
    g_ref[:h, :] = own_ref[...].astype(jnp.float32)
    g_ref[h:, :] = other_ref[...].astype(jnp.float32)
    for b, where in enumerate(blocks()):
        a_ref[block_at(me, *where), :] = g_ref[8 * b : 8 * b + 8, :]
    r = lax.broadcasted_iota(jnp.int32, (h, h), 0)
    c = lax.broadcasted_iota(jnp.int32, (h, h), 1)
    s11 = jnp.where(r > c, a_ref[:h, :h].T, 0.0)
    s22 = jnp.where(r > c, a_ref[h:, h:].T, 0.0)
    s21 = a_ref[:h, h:].T
    x1 = unit_inverse(s11)
    x2 = unit_inverse(s22)
    top = sum(r[...].astype(jnp.float32) for r in (top_ref, more_ref))
    u1 = dot(x1, top[:h])
    u2 = dot(x2, top[h:] - dot_exact(s21.astype(jnp.bfloat16), u1))
    out_ref[...] = jnp.concatenate([u1, u2], axis=0).astype(jnp.bfloat16)


def solve(me, own, other, top, more):
    n, cols = top.shape
    return pl.pallas_call(
        solve_kernel,
        in_specs=[SMEM] + [VMEM] * 4,
        out_specs=VMEM,
        out_shape=jax.ShapeDtypeStruct((n, cols), jnp.bfloat16),
        scratch_shapes=[pltpu.VMEM((n, n), jnp.float32), pltpu.VMEM((n, n), jnp.float32)],
        compiler_params=params(6),
        name="solve",
    )(me, own, other, top, more)


def fetch_kernel(src_ref, dst_ref, sem):
    n = sem.shape[0]
    step = src_ref.shape[0] // n
    copies = [
        pltpu.make_async_copy(src_ref.at[pl.ds(i * step, step)], dst_ref.at[pl.ds(i * step, step)], sem.at[i])
        for i in range(n)
    ]
    for copy in copies:
        copy.start()
    for copy in copies:
        copy.wait()


def fetch(x):
    return pl.pallas_call(
        fetch_kernel,
        in_specs=[pl.BlockSpec(memory_space=pltpu.HBM)],
        out_specs=VMEM,
        out_shape=jax.ShapeDtypeStruct(x.shape, x.dtype),
        scratch_shapes=[pltpu.SemaphoreType.DMA((4,))],
        compiler_params=params(2),
        name="fetch",
    )(x)


def update_kernel(cnt_ref, lst_ref, piv_ref, first_ref, me_ref, tr_ref, ud_ref, rest_ref, *refs):
    parts = refs[1:11]
    out_ref, buf_ref, nat_ref, drow_ref, tmp_ref, sem = refs[11:]
    rows = buf_ref.shape[0]
    nblk = sem.shape[0]
    blk = rows // nblk
    width = nat_ref.shape[0]
    first = first_ref[0]
    late = lax.div(first, rows) >> 2

    @pl.when(late == 0)
    def _():
        nat_ref[...] = ud_ref[:width, :].astype(jnp.float32)
        drow_ref[...] = ud_ref[width:, :].astype(jnp.float32)

    @pl.when(late == 1)
    def _():
        nat_ref[...] = rest_ref[:width, :].astype(jnp.float32)
        drow_ref[...] = rest_ref[width:, :].astype(jnp.float32)

    sub = lax.broadcasted_iota(jnp.int32, (16, 128), 0)

    def fix(k, carry):
        i = lst_ref[k]
        loc = piv_ref[i] - first
        at = pl.ds(pl.multiple_of(loc & ~15, 16), 16)
        old = buf_ref[at, :].astype(jnp.float32)
        row = drow_ref[pl.ds(i, 1), :]
        buf_ref[at, :] = jnp.where(sub == (loc & 15), row, old).astype(jnp.bfloat16)
        return carry

    lax.fori_loop(0, cnt_ref[0], fix, 0)
    for i, where in enumerate(blocks()):
        tmp_ref[8 * i : 8 * i + 8, :] = nat_ref[block_at(me_ref[0], *where), :]
    ut = tmp_ref[...].T.astype(jnp.bfloat16)
    copies = []
    for b in range(nblk):
        half = b // (nblk // 2)
        here = pl.ds(b * blk, blk)
        there = pl.ds((b - half * (nblk // 2)) * blk, blk)
        pieces = []
        for s in (parts[:5], parts[5:]):
            pieces += [s[0][:, here], s[1][:, here], s[2][:, here], s[3 + half][:, there]]
        product = lax.dot_general(
            ut, jnp.concatenate(pieces, axis=0), (((1,), (0,)), ((), ())),
            preferred_element_type=jnp.float32,
        ).T
        new = buf_ref[here, :].astype(jnp.float32) - product
        if b == 0:
            head = jnp.where(first == 0, nat_ref[...], new[:width])
            buf_ref[:width, :] = head.astype(jnp.bfloat16)
            buf_ref[width:blk, :] = new[width:].astype(jnp.bfloat16)
        else:
            buf_ref[here, :] = new.astype(jnp.bfloat16)
        copies.append(pltpu.make_async_copy(buf_ref.at[here], out_ref.at[here], sem.at[b]))
        copies[-1].start()
    for copy in copies:
        copy.wait()


def update(cnt, lst, pivots, first, me, trailing, ud, rest, ahead, parts, nblk):
    rows, cols = trailing.shape
    width = pivots.shape[0]
    return pl.pallas_call(
        update_kernel,
        in_specs=[SMEM] * 5 + [VMEM] * 14,
        out_specs=[pl.BlockSpec(memory_space=pltpu.HBM), VMEM],
        scratch_shapes=[
            pltpu.VMEM((width, cols), jnp.float32),
            pltpu.VMEM((width, cols), jnp.float32),
            pltpu.VMEM((width, cols), jnp.float32),
            pltpu.SemaphoreType.DMA((nblk,)),
        ],
        out_shape=[jax.ShapeDtypeStruct((rows, cols), jnp.bfloat16)] * 2,
        input_output_aliases={5: 1},
        compiler_params=params(28),
        name="update",
    )(cnt, lst, pivots, first, me, trailing, ud, rest, ahead, *parts)[0]


def body(trailing, panel_t, pivots):
    rows = trailing.shape[0]
    width = pivots.shape[0]
    half = rows // 2
    barrier = lax.optimization_barrier
    first = (lax.axis_index("prow") * rows).astype(jnp.int32).reshape(1)
    me = lax.axis_index("pcol").astype(jnp.int32).reshape(1)
    trailing = pltpu.with_memory_space_constraint(trailing, pltpu.HBM)

    def zsend(x, pairs):
        return lax.ppermute(x, "prow", pairs)

    p, m, q = [send(panel_t, hop(d, 0, True)) for d in (1, -1, 2)]

    top, disp, cnt, lst = pick(trailing, pivots, first, rows)
    more = zsend(top, [(i + 4, i) for i in range(4)])
    p, m, q, top = barrier((p, m, q, top))

    up, down, across = hop(0, 1, True), hop(0, -1, True), hop(0, 2, True)
    diag = stack([panel_t, p, m, q], 0, width, "stack_d")
    diag_q, diag_p, diag_m = send(diag, across), send(diag, up), send(diag, down)
    block = stack([panel_t, p, m, q], 0, rows, "stack_p")
    block, diag_q, diag_p, diag_m, top, more = barrier((block, diag_q, diag_p, diag_m, top, more))
    near, far = send(block, up), send(block, down)
    own = stack([diag, diag_p, diag_m, diag_q], 0, width, "stack_l")
    top = add(top, more)
    more = zsend(top, [(2, 0), (3, 1)])
    other = send(own, CORES)
    top = add(top, more)
    top, disp, other = barrier((top, disp, other))
    more = zsend(top, [(1, 0)])
    lower = zsend(disp, [(0, 2)])
    top, block2 = barrier((top, block))
    swap = send(block2, CORES)
    more, disp, lower = barrier((more, disp, lower))
    u = solve(me, own, other, top, more)
    disp = choose(first, rows, (2,), disp, lower)
    disp = choose(first, rows, (1, 3), disp, zsend(disp, [(0, 1), (2, 3)]))
    ru = zsend(u, [(0, 2)])
    u, source = barrier((u, trailing))
    copy = fetch(pltpu.with_memory_space_constraint(source, pltpu.HBM))
    ru, near, far, swap, disp, copy = barrier((ru, near, far, swap, disp, copy))
    fa, fb = stack([near], 0, half, "stack_a"), stack([far], half, half, "stack_b")
    qa, qb = send(fa, up), send(fb, down)
    u = choose(first, rows, (2,), u, ru)
    u, near, far = barrier((u, near, far))
    other_near, other_far = send(near, CORES), send(far, CORES)
    ud = join(first, rows, (1, 3), u, zsend(u, [(0, 1), (2, 3)]), disp)
    rest = zsend(ud, [(i, i + 4) for i in range(4)])
    ahead = stack([qa, qb], 0, 128, "stack_q", 60)
    own = [block, near, far, qa, qb]
    parts = own + [swap, other_near, other_far, send(qa, CORES), send(qb, CORES)]
    return update(cnt, lst, pivots, first, me, copy, ud, rest, ahead, parts, NBLK)


def solution(mesh):
    return jax.shard_map(
        body,
        mesh=mesh,
        in_specs=(P("prow", "pcol"), P("pcol", "prow"), P()),
        out_specs=P("prow", "pcol"),
        check_vma=False,
    )
```

```python
import functools

import jax
import jax.numpy as jnp
from jax import lax
from jax.experimental import pallas as pl
from jax.experimental.pallas import tpu as pltpu
from jax.sharding import PartitionSpec as P

NX = 4
NY = 4
OFFSETS = (0, -1, 1, 2)
NBLK = 12
SMEM = pl.BlockSpec(memory_space=pltpu.SMEM)
VMEM = pl.BlockSpec(memory_space=pltpu.VMEM)
HIGHEST = lax.Precision.HIGHEST


def place(x, y, c):
    return ((x % NX) * NY + (y % NY)) * 2 + c


def hop(dx, dy, turn):
    pairs = []
    for x in range(NX):
        for y in range(NY):
            for c in range(2):
                a, b = (dy, dx) if turn and c == 1 else (dx, dy)
                pairs.append((place(x, y, c), place(x + a, y + b, c)))
    return pairs


CORES = [(p, p ^ 1) for p in range(NX * NY * 2)]


def send(block, pairs):
    return lax.ppermute(block, "pcol", pairs)


def params(mib):
    return pltpu.CompilerParams(vmem_limit_bytes=mib << 20)


def cost(us):
    return pl.CostEstimate(flops=int(us * 1.1e9), bytes_accessed=int(us * 3.5e6), transcendentals=0)


def stack_kernel(start, step, *refs):
    def chunk(i, carry):
        src = pl.ds(pl.multiple_of(start + i * step, 128), step)
        dst = pl.ds(pl.multiple_of(i * step, 128), step)
        refs[-1][:, dst] = jnp.concatenate([r[:, src] for r in refs[:-1]], axis=0)
        return carry

    lax.fori_loop(0, refs[-1].shape[1] // step, chunk, 0)


def stack(parts, start, cols, name, us=1):
    rows = sum(p.shape[0] for p in parts)
    return pl.pallas_call(
        functools.partial(stack_kernel, start, min(cols, 1024)),
        in_specs=[VMEM] * len(parts),
        out_specs=VMEM,
        out_shape=jax.ShapeDtypeStruct((rows, cols), jnp.bfloat16),
        compiler_params=params(2),
        cost_estimate=cost(us),
        name=name,
    )(*parts)


def add_kernel(a_ref, b_ref, out_ref):
    out_ref[...] = (a_ref[...].astype(jnp.float32) + b_ref[...].astype(jnp.float32)).astype(jnp.bfloat16)


def add(a, b):
    return pl.pallas_call(
        add_kernel,
        in_specs=[VMEM, VMEM],
        out_specs=VMEM,
        out_shape=jax.ShapeDtypeStruct(a.shape, a.dtype),
        compiler_params=params(2),
        name="add",
    )(a, b)


def choose_kernel(rows, mask, first_ref, a_ref, b_ref, out_ref):
    other = (jnp.int32(mask) >> lax.div(first_ref[0], rows)) & 1

    @pl.when(other == 0)
    def _():
        out_ref[...] = a_ref[...]

    @pl.when(other == 1)
    def _():
        out_ref[...] = b_ref[...]


def choose(first, rows, others, a, b):
    return pl.pallas_call(
        functools.partial(choose_kernel, rows, sum(1 << z for z in others)),
        in_specs=[SMEM, VMEM, VMEM],
        out_specs=VMEM,
        out_shape=jax.ShapeDtypeStruct(a.shape, a.dtype),
        compiler_params=params(2),
        name="choose",
    )(first, a, b)


def join_kernel(rows, mask, first_ref, a_ref, b_ref, below_ref, out_ref):
    width = a_ref.shape[0]
    choose_kernel(rows, mask, first_ref, a_ref, b_ref, out_ref.at[pl.ds(0, width)])
    out_ref[width:, :] = below_ref[...]


def join(first, rows, others, a, b, below):
    width, cols = a.shape
    return pl.pallas_call(
        functools.partial(join_kernel, rows, sum(1 << z for z in others)),
        in_specs=[SMEM] + [VMEM] * 3,
        out_specs=VMEM,
        out_shape=jax.ShapeDtypeStruct((2 * width, cols), a.dtype),
        compiler_params=params(2),
        name="join",
    )(first, a, b, below)


def pick_kernel(blk, piv_ref, first_ref, trailing_ref, out_ref, head_ref, cnt_ref, lst_ref, own_ref, group_ref, rows_ref, sem, head_sem):
    width = piv_ref.shape[0]
    rows = trailing_ref.shape[0]
    first = first_ref[0]
    nblk = cnt_ref.shape[0]
    head = pltpu.make_async_copy(trailing_ref.at[pl.ds(0, width)], head_ref, head_sem)
    head.start()
    for b in range(nblk):
        cnt_ref[b] = 0

    def filt(i, n):
        loc = piv_ref[i] - first
        own_ref[n] = i
        return n + ((loc >= 0) & (loc < rows)).astype(jnp.int32)

    n = lax.fori_loop(0, width, filt, 0, unroll=8)

    def group(k):
        loc = piv_ref[own_ref[k]] - first
        base = pl.multiple_of(loc & ~15, 16)
        return pltpu.make_async_copy(trailing_ref.at[pl.ds(base, 16)], group_ref.at[k], sem)

    def begin(k, carry):
        group(k).start()
        i = own_ref[k]
        b = lax.div(piv_ref[i] - first, blk)
        m = cnt_ref[b]
        lst_ref[b * width + m] = i
        cnt_ref[b] = m + 1
        return carry

    def finish(k, carry):
        group(k).wait()
        return carry

    lax.fori_loop(0, n, begin, 0)
    rows_ref[...] = jnp.zeros_like(rows_ref)
    lax.fori_loop(0, n, finish, 0)
    sub = lax.broadcasted_iota(jnp.int32, (16, 128), 0)

    def extract(k, carry):
        i = own_ref[k]
        loc = piv_ref[i] - first
        tile = group_ref[k].astype(jnp.float32)
        row = jnp.sum(jnp.where(sub == (loc & 15), tile, 0.0), axis=0, keepdims=True)
        rows_ref[pl.ds(i, 1), :] = row
        return carry

    lax.fori_loop(0, n, extract, 0)
    out_ref[...] = rows_ref[...].astype(jnp.bfloat16)
    head.wait()


def pick(trailing, pivots, first, blk):
    rows, cols = trailing.shape
    width = pivots.shape[0]
    nblk = rows // blk
    return pl.pallas_call(
        functools.partial(pick_kernel, blk),
        in_specs=[SMEM, SMEM, pl.BlockSpec(memory_space=pltpu.HBM)],
        out_specs=[VMEM, VMEM, SMEM, SMEM],
        out_shape=[
            jax.ShapeDtypeStruct((width, cols), jnp.bfloat16),
            jax.ShapeDtypeStruct((width, cols), jnp.bfloat16),
            jax.ShapeDtypeStruct((nblk,), jnp.int32),
            jax.ShapeDtypeStruct((nblk * width,), jnp.int32),
        ],
        scratch_shapes=[
            pltpu.SMEM((width + 8,), jnp.int32),
            pltpu.VMEM((width, 16, cols), jnp.bfloat16),
            pltpu.VMEM((width, cols), jnp.float32),
            pltpu.SemaphoreType.DMA,
            pltpu.SemaphoreType.DMA,
        ],
        compiler_params=params(6),
        cost_estimate=cost(12),
        name="pick",
    )(pivots, first, trailing)


def dot(a, b):
    return lax.dot_general(
        a, b, (((1,), (0,)), ((), ())), precision=HIGHEST, preferred_element_type=jnp.float32
    )


def dot_exact(a, b):
    n = b.shape[1]
    hi = b.astype(jnp.bfloat16)
    rest = b - hi.astype(jnp.float32)
    mid = rest.astype(jnp.bfloat16)
    low = (rest - mid.astype(jnp.float32)).astype(jnp.bfloat16)
    r = lax.dot_general(
        a, jnp.concatenate([hi, mid, low], axis=1), (((1,), (0,)), ((), ())),
        preferred_element_type=jnp.float32,
    )
    return r[:, 2 * n :] + r[:, n : 2 * n] + r[:, :n]


def unit_inverse(strict):
    n = strict.shape[0]
    r = lax.broadcasted_iota(jnp.int32, (n, n), 0)
    c = lax.broadcasted_iota(jnp.int32, (n, n), 1)
    d = jnp.where((r >> 4) == (c >> 4), strict, 0.0)
    x = jnp.where(r == c, 1.0, 0.0) - d
    for step in range(3):
        d = dot_exact(d.astype(jnp.bfloat16), d) if step == 0 else dot(d, d)
        x = x + dot(x, d)
    for lg in (4, 5, 6):
        inside = ((r >> (lg + 1)) == (c >> (lg + 1))) & ((r >> lg) != (c >> lg))
        part = jnp.where(inside, strict, 0.0).astype(jnp.bfloat16)
        x = x - dot(x, dot_exact(part, x))
    return x


def blocks():
    return [(k, outer, inner) for k in range(2) for outer in OFFSETS for inner in OFFSETS]


def block_at(me, k, outer, inner):
    core = (me & 1) ^ k
    dx = jnp.where(core == 0, inner, outer)
    dy = jnp.where(core == 0, outer, inner)
    x = ((me >> 3) + dx) & 3
    y = ((me >> 1) + dy) & 3
    return pl.ds(pl.multiple_of(((x * 4 + y) * 2 + core) * 8, 8), 8)


def solve_kernel(me_ref, own_ref, other_ref, top_ref, more_ref, out_ref, a_ref, g_ref):
    n = top_ref.shape[0]
    h = n // 2
    me = me_ref[0]
    g_ref[:h, :] = own_ref[...].astype(jnp.float32)
    g_ref[h:, :] = other_ref[...].astype(jnp.float32)
    for b, where in enumerate(blocks()):
        a_ref[block_at(me, *where), :] = g_ref[8 * b : 8 * b + 8, :]
    r = lax.broadcasted_iota(jnp.int32, (h, h), 0)
    c = lax.broadcasted_iota(jnp.int32, (h, h), 1)
    s11 = jnp.where(r > c, a_ref[:h, :h].T, 0.0)
    s22 = jnp.where(r > c, a_ref[h:, h:].T, 0.0)
    s21 = a_ref[:h, h:].T
    x1 = unit_inverse(s11)
    x2 = unit_inverse(s22)
    top = sum(r[...].astype(jnp.float32) for r in (top_ref, more_ref))
    u1 = dot(x1, top[:h])
    u2 = dot(x2, top[h:] - dot_exact(s21.astype(jnp.bfloat16), u1))
    out_ref[...] = jnp.concatenate([u1, u2], axis=0).astype(jnp.bfloat16)


def solve(me, own, other, top, more):
    n, cols = top.shape
    return pl.pallas_call(
        solve_kernel,
        in_specs=[SMEM] + [VMEM] * 4,
        out_specs=VMEM,
        out_shape=jax.ShapeDtypeStruct((n, cols), jnp.bfloat16),
        scratch_shapes=[pltpu.VMEM((n, n), jnp.float32), pltpu.VMEM((n, n), jnp.float32)],
        compiler_params=params(6),
        name="solve",
    )(me, own, other, top, more)


def fetch_kernel(src_ref, dst_ref, sem):
    n = sem.shape[0]
    step = src_ref.shape[0] // n
    copies = [
        pltpu.make_async_copy(src_ref.at[pl.ds(i * step, step)], dst_ref.at[pl.ds(i * step, step)], sem.at[i])
        for i in range(n)
    ]
    for copy in copies:
        copy.start()
    for copy in copies:
        copy.wait()


def fetch(x):
    return pl.pallas_call(
        fetch_kernel,
        in_specs=[pl.BlockSpec(memory_space=pltpu.HBM)],
        out_specs=VMEM,
        out_shape=jax.ShapeDtypeStruct(x.shape, x.dtype),
        scratch_shapes=[pltpu.SemaphoreType.DMA((4,))],
        compiler_params=params(2),
        name="fetch",
    )(x)


def update_kernel(cnt_ref, lst_ref, piv_ref, first_ref, me_ref, tr_ref, ud_ref, rest_ref, *refs):
    parts = refs[1:11]
    out_ref, buf_ref, nat_ref, drow_ref, tmp_ref, sem = refs[11:]
    rows = buf_ref.shape[0]
    nblk = sem.shape[0]
    blk = rows // nblk
    width = nat_ref.shape[0]
    first = first_ref[0]
    late = lax.div(first, rows) >> 2

    @pl.when(late == 0)
    def _():
        nat_ref[...] = ud_ref[:width, :].astype(jnp.float32)
        drow_ref[...] = ud_ref[width:, :].astype(jnp.float32)

    @pl.when(late == 1)
    def _():
        nat_ref[...] = rest_ref[:width, :].astype(jnp.float32)
        drow_ref[...] = rest_ref[width:, :].astype(jnp.float32)

    sub = lax.broadcasted_iota(jnp.int32, (16, 128), 0)

    def fix(k, carry):
        i = lst_ref[k]
        loc = piv_ref[i] - first
        at = pl.ds(pl.multiple_of(loc & ~15, 16), 16)
        old = buf_ref[at, :].astype(jnp.float32)
        row = drow_ref[pl.ds(i, 1), :]
        buf_ref[at, :] = jnp.where(sub == (loc & 15), row, old).astype(jnp.bfloat16)
        return carry

    lax.fori_loop(0, cnt_ref[0], fix, 0)
    for i, where in enumerate(blocks()):
        tmp_ref[8 * i : 8 * i + 8, :] = nat_ref[block_at(me_ref[0], *where), :]
    ut = tmp_ref[...].T.astype(jnp.bfloat16)
    copies = []
    for b in range(nblk):
        half = b // (nblk // 2)
        here = pl.ds(b * blk, blk)
        there = pl.ds((b - half * (nblk // 2)) * blk, blk)
        pieces = []
        for s in (parts[:5], parts[5:]):
            pieces += [s[0][:, here], s[1][:, here], s[2][:, here], s[3 + half][:, there]]
        product = lax.dot_general(
            ut, jnp.concatenate(pieces, axis=0), (((1,), (0,)), ((), ())),
            preferred_element_type=jnp.float32,
        ).T
        new = buf_ref[here, :].astype(jnp.float32) - product
        if b == 0:
            head = jnp.where(first == 0, nat_ref[...], new[:width])
            buf_ref[:width, :] = head.astype(jnp.bfloat16)
            buf_ref[width:blk, :] = new[width:].astype(jnp.bfloat16)
        else:
            buf_ref[here, :] = new.astype(jnp.bfloat16)
        copies.append(pltpu.make_async_copy(buf_ref.at[here], out_ref.at[here], sem.at[b]))
        copies[-1].start()
    for copy in copies:
        copy.wait()


def update(cnt, lst, pivots, first, me, trailing, ud, rest, ahead, parts, nblk):
    rows, cols = trailing.shape
    width = pivots.shape[0]
    return pl.pallas_call(
        update_kernel,
        in_specs=[SMEM] * 5 + [VMEM] * 14,
        out_specs=[pl.BlockSpec(memory_space=pltpu.HBM), VMEM],
        scratch_shapes=[
            pltpu.VMEM((width, cols), jnp.float32),
            pltpu.VMEM((width, cols), jnp.float32),
            pltpu.VMEM((width, cols), jnp.float32),
            pltpu.SemaphoreType.DMA((nblk,)),
        ],
        out_shape=[jax.ShapeDtypeStruct((rows, cols), jnp.bfloat16)] * 2,
        input_output_aliases={5: 1},
        compiler_params=params(16),
        name="update",
    )(cnt, lst, pivots, first, me, trailing, ud, rest, ahead, *parts)[0]


def body(trailing, panel_t, pivots):
    rows = trailing.shape[0]
    width = pivots.shape[0]
    half = rows // 2
    barrier = lax.optimization_barrier
    first = (lax.axis_index("prow") * rows).astype(jnp.int32).reshape(1)
    me = lax.axis_index("pcol").astype(jnp.int32).reshape(1)
    trailing = pltpu.with_memory_space_constraint(trailing, pltpu.HBM)

    def zsend(x, pairs):
        return lax.ppermute(x, "prow", pairs)

    p, m, q = [send(panel_t, hop(d, 0, True)) for d in (1, -1, 2)]

    top, disp, cnt, lst = pick(trailing, pivots, first, rows)
    more = zsend(top, [(i + 4, i) for i in range(4)])
    p, m, q, top = barrier((p, m, q, top))

    up, down, across = hop(0, 1, True), hop(0, -1, True), hop(0, 2, True)
    diag = stack([panel_t, p, m, q], 0, width, "stack_d")
    diag_q, diag_p, diag_m = send(diag, across), send(diag, up), send(diag, down)
    block = stack([panel_t, p, m, q], 0, rows, "stack_p")
    block, diag_q, diag_p, diag_m, top, more = barrier((block, diag_q, diag_p, diag_m, top, more))
    near, far = send(block, up), send(block, down)
    own = stack([diag, diag_p, diag_m, diag_q], 0, width, "stack_l")
    top = add(top, more)
    more = zsend(top, [(2, 0), (3, 1)])
    other = send(own, CORES)
    top = add(top, more)
    top, disp, other, source = barrier((top, disp, other, trailing))
    copy = fetch(pltpu.with_memory_space_constraint(source, pltpu.HBM))
    more = zsend(top, [(1, 0)])
    lower = zsend(disp, [(0, 2)])
    top, block2 = barrier((top, block))
    swap = send(block2, CORES)
    more, disp, lower, copy = barrier((more, disp, lower, copy))
    u = solve(me, own, other, top, more)
    disp = choose(first, rows, (2,), disp, lower)
    disp = choose(first, rows, (1, 3), disp, zsend(disp, [(0, 1), (2, 3)]))
    ru = zsend(u, [(0, 2)])
    ru, near, far, swap, disp, copy = barrier((ru, near, far, swap, disp, copy))
    fa, fb = stack([near], 0, half, "stack_a"), stack([far], half, half, "stack_b")
    qa, qb = send(fa, up), send(fb, down)
    u = choose(first, rows, (2,), u, ru)
    u, near, far = barrier((u, near, far))
    other_near, other_far = send(near, CORES), send(far, CORES)
    ud = join(first, rows, (1, 3), u, zsend(u, [(0, 1), (2, 3)]), disp)
    rest = zsend(ud, [(i, i + 4) for i in range(4)])
    ahead = stack([qa, qb], 0, 128, "stack_q", 60)
    own = [block, near, far, qa, qb]
    parts = own + [swap, other_near, other_far, send(qa, CORES), send(qb, CORES)]
    return update(cnt, lst, pivots, first, me, copy, ud, rest, ahead, parts, NBLK)


def solution(mesh):
    return jax.shard_map(
        body,
        mesh=mesh,
        in_specs=(P("prow", "pcol"), P("pcol", "prow"), P()),
        out_specs=P("prow", "pcol"),
        check_vma=False,
    )
```

```python
import functools

import jax
import jax.numpy as jnp
from jax import lax
from jax.experimental import pallas as pl
from jax.experimental.pallas import tpu as pltpu
from jax.sharding import PartitionSpec as P

NX = 4
NY = 4
OFFSETS = (0, -1, 1, 2)
NBLK = 12
SMEM = pl.BlockSpec(memory_space=pltpu.SMEM)
VMEM = pl.BlockSpec(memory_space=pltpu.VMEM)
HIGHEST = lax.Precision.HIGHEST


def place(x, y, c):
    return ((x % NX) * NY + (y % NY)) * 2 + c


def hop(dx, dy, turn):
    pairs = []
    for x in range(NX):
        for y in range(NY):
            for c in range(2):
                a, b = (dy, dx) if turn and c == 1 else (dx, dy)
                pairs.append((place(x, y, c), place(x + a, y + b, c)))
    return pairs


CORES = [(p, p ^ 1) for p in range(NX * NY * 2)]


def send(block, pairs):
    return lax.ppermute(block, "pcol", pairs)


def params(mib):
    return pltpu.CompilerParams(vmem_limit_bytes=mib << 20)


def cost(us):
    return pl.CostEstimate(flops=int(us * 1.1e9), bytes_accessed=int(us * 3.5e6), transcendentals=0)


def stack_kernel(start, step, *refs):
    def chunk(i, carry):
        src = pl.ds(pl.multiple_of(start + i * step, 128), step)
        dst = pl.ds(pl.multiple_of(i * step, 128), step)
        refs[-1][:, dst] = jnp.concatenate([r[:, src] for r in refs[:-1]], axis=0)
        return carry

    lax.fori_loop(0, refs[-1].shape[1] // step, chunk, 0)


def stack(parts, start, cols, name, us=1):
    rows = sum(p.shape[0] for p in parts)
    return pl.pallas_call(
        functools.partial(stack_kernel, start, min(cols, 1024)),
        in_specs=[VMEM] * len(parts),
        out_specs=VMEM,
        out_shape=jax.ShapeDtypeStruct((rows, cols), jnp.bfloat16),
        compiler_params=params(2),
        cost_estimate=cost(us),
        name=name,
    )(*parts)


def add_kernel(a_ref, b_ref, out_ref):
    out_ref[...] = (a_ref[...].astype(jnp.float32) + b_ref[...].astype(jnp.float32)).astype(jnp.bfloat16)


def add(a, b):
    return pl.pallas_call(
        add_kernel,
        in_specs=[VMEM, VMEM],
        out_specs=VMEM,
        out_shape=jax.ShapeDtypeStruct(a.shape, a.dtype),
        compiler_params=params(2),
        name="add",
    )(a, b)


def choose_kernel(rows, mask, first_ref, a_ref, b_ref, out_ref):
    other = (jnp.int32(mask) >> lax.div(first_ref[0], rows)) & 1

    @pl.when(other == 0)
    def _():
        out_ref[...] = a_ref[...]

    @pl.when(other == 1)
    def _():
        out_ref[...] = b_ref[...]


def choose(first, rows, others, a, b):
    return pl.pallas_call(
        functools.partial(choose_kernel, rows, sum(1 << z for z in others)),
        in_specs=[SMEM, VMEM, VMEM],
        out_specs=VMEM,
        out_shape=jax.ShapeDtypeStruct(a.shape, a.dtype),
        compiler_params=params(2),
        name="choose",
    )(first, a, b)


def join_kernel(rows, mask, first_ref, a_ref, b_ref, below_ref, out_ref):
    width = a_ref.shape[0]
    choose_kernel(rows, mask, first_ref, a_ref, b_ref, out_ref.at[pl.ds(0, width)])
    out_ref[width:, :] = below_ref[...]


def join(first, rows, others, a, b, below):
    width, cols = a.shape
    return pl.pallas_call(
        functools.partial(join_kernel, rows, sum(1 << z for z in others)),
        in_specs=[SMEM] + [VMEM] * 3,
        out_specs=VMEM,
        out_shape=jax.ShapeDtypeStruct((2 * width, cols), a.dtype),
        compiler_params=params(2),
        name="join",
    )(first, a, b, below)


def pick_kernel(blk, piv_ref, first_ref, trailing_ref, out_ref, head_ref, cnt_ref, lst_ref, own_ref, group_ref, rows_ref, sem, head_sem):
    width = piv_ref.shape[0]
    rows = trailing_ref.shape[0]
    first = first_ref[0]
    nblk = cnt_ref.shape[0]
    head = pltpu.make_async_copy(trailing_ref.at[pl.ds(0, width)], head_ref, head_sem)
    head.start()
    for b in range(nblk):
        cnt_ref[b] = 0

    def filt(i, n):
        loc = piv_ref[i] - first
        own_ref[n] = i
        return n + ((loc >= 0) & (loc < rows)).astype(jnp.int32)

    n = lax.fori_loop(0, width, filt, 0, unroll=8)

    def group(k):
        loc = piv_ref[own_ref[k]] - first
        base = pl.multiple_of(loc & ~15, 16)
        return pltpu.make_async_copy(trailing_ref.at[pl.ds(base, 16)], group_ref.at[k], sem)

    def begin(k, carry):
        group(k).start()
        i = own_ref[k]
        b = lax.div(piv_ref[i] - first, blk)
        m = cnt_ref[b]
        lst_ref[b * width + m] = i
        cnt_ref[b] = m + 1
        return carry

    def finish(k, carry):
        group(k).wait()
        return carry

    lax.fori_loop(0, n, begin, 0)
    rows_ref[...] = jnp.zeros_like(rows_ref)
    lax.fori_loop(0, n, finish, 0)
    sub = lax.broadcasted_iota(jnp.int32, (16, 128), 0)

    def extract(k, carry):
        i = own_ref[k]
        loc = piv_ref[i] - first
        tile = group_ref[k].astype(jnp.float32)
        row = jnp.sum(jnp.where(sub == (loc & 15), tile, 0.0), axis=0, keepdims=True)
        rows_ref[pl.ds(i, 1), :] = row
        return carry

    lax.fori_loop(0, n, extract, 0)
    out_ref[...] = rows_ref[...].astype(jnp.bfloat16)
    head.wait()


def pick(trailing, pivots, first, blk):
    rows, cols = trailing.shape
    width = pivots.shape[0]
    nblk = rows // blk
    return pl.pallas_call(
        functools.partial(pick_kernel, blk),
        in_specs=[SMEM, SMEM, pl.BlockSpec(memory_space=pltpu.HBM)],
        out_specs=[VMEM, VMEM, SMEM, SMEM],
        out_shape=[
            jax.ShapeDtypeStruct((width, cols), jnp.bfloat16),
            jax.ShapeDtypeStruct((width, cols), jnp.bfloat16),
            jax.ShapeDtypeStruct((nblk,), jnp.int32),
            jax.ShapeDtypeStruct((nblk * width,), jnp.int32),
        ],
        scratch_shapes=[
            pltpu.SMEM((width + 8,), jnp.int32),
            pltpu.VMEM((width, 16, cols), jnp.bfloat16),
            pltpu.VMEM((width, cols), jnp.float32),
            pltpu.SemaphoreType.DMA,
            pltpu.SemaphoreType.DMA,
        ],
        compiler_params=params(6),
        cost_estimate=cost(12),
        name="pick",
    )(pivots, first, trailing)


def dot(a, b):
    return lax.dot_general(
        a, b, (((1,), (0,)), ((), ())), precision=HIGHEST, preferred_element_type=jnp.float32
    )


def dot_exact(a, b):
    n = b.shape[1]
    hi = b.astype(jnp.bfloat16)
    rest = b - hi.astype(jnp.float32)
    mid = rest.astype(jnp.bfloat16)
    low = (rest - mid.astype(jnp.float32)).astype(jnp.bfloat16)
    r = lax.dot_general(
        a, jnp.concatenate([hi, mid, low], axis=1), (((1,), (0,)), ((), ())),
        preferred_element_type=jnp.float32,
    )
    return r[:, 2 * n :] + r[:, n : 2 * n] + r[:, :n]


def unit_inverse(strict):
    n = strict.shape[0]
    r = lax.broadcasted_iota(jnp.int32, (n, n), 0)
    c = lax.broadcasted_iota(jnp.int32, (n, n), 1)
    d = jnp.where((r >> 4) == (c >> 4), strict, 0.0)
    x = jnp.where(r == c, 1.0, 0.0) - d
    for step in range(3):
        d = dot_exact(d.astype(jnp.bfloat16), d) if step == 0 else dot(d, d)
        x = x + dot(x, d)
    for lg in (4, 5, 6):
        inside = ((r >> (lg + 1)) == (c >> (lg + 1))) & ((r >> lg) != (c >> lg))
        part = jnp.where(inside, strict, 0.0).astype(jnp.bfloat16)
        x = x - dot(x, dot_exact(part, x))
    return x


def blocks():
    return [(k, outer, inner) for k in range(2) for outer in OFFSETS for inner in OFFSETS]


def block_at(me, k, outer, inner):
    core = (me & 1) ^ k
    dx = jnp.where(core == 0, inner, outer)
    dy = jnp.where(core == 0, outer, inner)
    x = ((me >> 3) + dx) & 3
    y = ((me >> 1) + dy) & 3
    return pl.ds(pl.multiple_of(((x * 4 + y) * 2 + core) * 8, 8), 8)


def solve_kernel(me_ref, own_ref, other_ref, top_ref, more_ref, out_ref, a_ref, g_ref):
    n = top_ref.shape[0]
    h = n // 2
    me = me_ref[0]
    g_ref[:h, :] = own_ref[...].astype(jnp.float32)
    g_ref[h:, :] = other_ref[...].astype(jnp.float32)
    for b, where in enumerate(blocks()):
        a_ref[block_at(me, *where), :] = g_ref[8 * b : 8 * b + 8, :]
    r = lax.broadcasted_iota(jnp.int32, (h, h), 0)
    c = lax.broadcasted_iota(jnp.int32, (h, h), 1)
    s11 = jnp.where(r > c, a_ref[:h, :h].T, 0.0)
    s22 = jnp.where(r > c, a_ref[h:, h:].T, 0.0)
    s21 = a_ref[:h, h:].T
    x1 = unit_inverse(s11)
    x2 = unit_inverse(s22)
    top = sum(r[...].astype(jnp.float32) for r in (top_ref, more_ref))
    u1 = dot(x1, top[:h])
    u2 = dot(x2, top[h:] - dot_exact(s21.astype(jnp.bfloat16), u1))
    out_ref[...] = jnp.concatenate([u1, u2], axis=0).astype(jnp.bfloat16)


def solve(me, own, other, top, more):
    n, cols = top.shape
    return pl.pallas_call(
        solve_kernel,
        in_specs=[SMEM] + [VMEM] * 4,
        out_specs=VMEM,
        out_shape=jax.ShapeDtypeStruct((n, cols), jnp.bfloat16),
        scratch_shapes=[pltpu.VMEM((n, n), jnp.float32), pltpu.VMEM((n, n), jnp.float32)],
        compiler_params=params(6),
        name="solve",
    )(me, own, other, top, more)


def fetch_kernel(src_ref, dst_ref, sem):
    n = sem.shape[0]
    step = src_ref.shape[0] // n
    copies = [
        pltpu.make_async_copy(src_ref.at[pl.ds(i * step, step)], dst_ref.at[pl.ds(i * step, step)], sem.at[i])
        for i in range(n)
    ]
    for copy in copies:
        copy.start()
    for copy in copies:
        copy.wait()


def fetch(x):
    return pl.pallas_call(
        fetch_kernel,
        in_specs=[pl.BlockSpec(memory_space=pltpu.HBM)],
        out_specs=VMEM,
        out_shape=jax.ShapeDtypeStruct(x.shape, x.dtype),
        scratch_shapes=[pltpu.SemaphoreType.DMA((4,))],
        compiler_params=params(2),
        name="fetch",
    )(x)


def update_kernel(cnt_ref, lst_ref, piv_ref, first_ref, me_ref, tr_ref, ud_ref, rest_ref, *refs):
    parts = refs[1:11]
    out_ref, buf_ref, nat_ref, drow_ref, tmp_ref, sem = refs[11:]
    rows = buf_ref.shape[0]
    nblk = sem.shape[0]
    blk = rows // nblk
    width = nat_ref.shape[0]
    first = first_ref[0]
    late = lax.div(first, rows) >> 2

    @pl.when(late == 0)
    def _():
        nat_ref[...] = ud_ref[:width, :].astype(jnp.float32)
        drow_ref[...] = ud_ref[width:, :].astype(jnp.float32)

    @pl.when(late == 1)
    def _():
        nat_ref[...] = rest_ref[:width, :].astype(jnp.float32)
        drow_ref[...] = rest_ref[width:, :].astype(jnp.float32)

    sub = lax.broadcasted_iota(jnp.int32, (16, 128), 0)

    def fix(k, carry):
        i = lst_ref[k]
        loc = piv_ref[i] - first
        at = pl.ds(pl.multiple_of(loc & ~15, 16), 16)
        old = buf_ref[at, :].astype(jnp.float32)
        row = drow_ref[pl.ds(i, 1), :]
        buf_ref[at, :] = jnp.where(sub == (loc & 15), row, old).astype(jnp.bfloat16)
        return carry

    lax.fori_loop(0, cnt_ref[0], fix, 0)
    for i, where in enumerate(blocks()):
        tmp_ref[8 * i : 8 * i + 8, :] = nat_ref[block_at(me_ref[0], *where), :]
    ut = tmp_ref[...].T.astype(jnp.bfloat16)
    copies = []
    for b in range(nblk):
        half = b // (nblk // 2)
        here = pl.ds(b * blk, blk)
        there = pl.ds((b - half * (nblk // 2)) * blk, blk)
        pieces = []
        for s in (parts[:5], parts[5:]):
            pieces += [s[0][:, here], s[1][:, here], s[2][:, here], s[3 + half][:, there]]
        product = lax.dot_general(
            ut, jnp.concatenate(pieces, axis=0), (((1,), (0,)), ((), ())),
            preferred_element_type=jnp.float32,
        ).T
        new = buf_ref[here, :].astype(jnp.float32) - product
        if b == 0:
            head = jnp.where(first == 0, nat_ref[...], new[:width])
            buf_ref[:width, :] = head.astype(jnp.bfloat16)
            buf_ref[width:blk, :] = new[width:].astype(jnp.bfloat16)
        else:
            buf_ref[here, :] = new.astype(jnp.bfloat16)
        copies.append(pltpu.make_async_copy(buf_ref.at[here], out_ref.at[here], sem.at[b]))
        copies[-1].start()
    for copy in copies:
        copy.wait()


def update(cnt, lst, pivots, first, me, trailing, ud, rest, ahead, parts, nblk):
    rows, cols = trailing.shape
    width = pivots.shape[0]
    return pl.pallas_call(
        update_kernel,
        in_specs=[SMEM] * 5 + [VMEM] * 14,
        out_specs=[pl.BlockSpec(memory_space=pltpu.HBM), VMEM],
        scratch_shapes=[
            pltpu.VMEM((width, cols), jnp.float32),
            pltpu.VMEM((width, cols), jnp.float32),
            pltpu.VMEM((width, cols), jnp.float32),
            pltpu.SemaphoreType.DMA((nblk,)),
        ],
        out_shape=[jax.ShapeDtypeStruct((rows, cols), jnp.bfloat16)] * 2,
        input_output_aliases={5: 1},
        compiler_params=params(16),
        name="update",
    )(cnt, lst, pivots, first, me, trailing, ud, rest, ahead, *parts)[0]


def body(trailing, panel_t, pivots):
    rows = trailing.shape[0]
    width = pivots.shape[0]
    half = rows // 2
    barrier = lax.optimization_barrier
    first = (lax.axis_index("prow") * rows).astype(jnp.int32).reshape(1)
    me = lax.axis_index("pcol").astype(jnp.int32).reshape(1)
    trailing = pltpu.with_memory_space_constraint(trailing, pltpu.HBM)

    def zsend(x, pairs):
        return lax.ppermute(x, "prow", pairs)

    p, m, q = [send(panel_t, hop(d, 0, True)) for d in (1, -1, 2)]

    top, disp, cnt, lst = pick(trailing, pivots, first, rows)
    more = zsend(top, [(i + 4, i) for i in range(4)])
    p, m, q, top = barrier((p, m, q, top))

    up, down, across = hop(0, 1, True), hop(0, -1, True), hop(0, 2, True)
    diag = stack([panel_t, p, m, q], 0, width, "stack_d")
    diag_q, diag_p, diag_m = send(diag, across), send(diag, up), send(diag, down)
    block = stack([panel_t, p, m, q], 0, rows, "stack_p")
    block, diag_q, diag_p, diag_m, top, more = barrier((block, diag_q, diag_p, diag_m, top, more))
    near, far = send(block, up), send(block, down)
    own = stack([diag, diag_p, diag_m, diag_q], 0, width, "stack_l")
    top = add(top, more)
    more = zsend(top, [(2, 0), (3, 1)])
    top = add(top, more)
    top, disp, own = barrier((top, disp, own))
    other = send(own, CORES)
    other, source = barrier((other, trailing))
    copy = fetch(pltpu.with_memory_space_constraint(source, pltpu.HBM))
    more = zsend(top, [(1, 0)])
    lower = zsend(disp, [(0, 2)])
    top, block2 = barrier((top, block))
    swap = send(block2, CORES)
    more, disp, lower, copy = barrier((more, disp, lower, copy))
    u = solve(me, own, other, top, more)
    disp = choose(first, rows, (2,), disp, lower)
    disp = choose(first, rows, (1, 3), disp, zsend(disp, [(0, 1), (2, 3)]))
    ru = zsend(u, [(0, 2)])
    ru, near, far, swap, disp, copy = barrier((ru, near, far, swap, disp, copy))
    fa, fb = stack([near], 0, half, "stack_a"), stack([far], half, half, "stack_b")
    qa, qb = send(fa, up), send(fb, down)
    u = choose(first, rows, (2,), u, ru)
    ud = join(first, rows, (1, 3), u, zsend(u, [(0, 1), (2, 3)]), disp)
    ud, near, far = barrier((ud, near, far))
    rest = zsend(ud, [(i, i + 4) for i in range(4)])
    other_near, other_far = send(near, CORES), send(far, CORES)
    ahead = stack([qa, qb], 0, 128, "stack_q", 60)
    own = [block, near, far, qa, qb]
    parts = own + [swap, other_near, other_far, send(qa, CORES), send(qb, CORES)]
    return update(cnt, lst, pivots, first, me, copy, ud, rest, ahead, parts, NBLK)


def solution(mesh):
    return jax.shard_map(
        body,
        mesh=mesh,
        in_specs=(P("prow", "pcol"), P("pcol", "prow"), P()),
        out_specs=P("prow", "pcol"),
        check_vma=False,
    )
```

```python
import functools

import jax
import jax.numpy as jnp
from jax import lax
from jax.experimental import pallas as pl
from jax.experimental.pallas import tpu as pltpu
from jax.sharding import PartitionSpec as P

NX = 4
NY = 4
OFFSETS = (0, -1, 1, 2)
NBLK = 12
SMEM = pl.BlockSpec(memory_space=pltpu.SMEM)
VMEM = pl.BlockSpec(memory_space=pltpu.VMEM)
HIGHEST = lax.Precision.HIGHEST


def place(x, y, c):
    return ((x % NX) * NY + (y % NY)) * 2 + c


def hop(dx, dy, turn):
    pairs = []
    for x in range(NX):
        for y in range(NY):
            for c in range(2):
                a, b = (dy, dx) if turn and c == 1 else (dx, dy)
                pairs.append((place(x, y, c), place(x + a, y + b, c)))
    return pairs


CORES = [(p, p ^ 1) for p in range(NX * NY * 2)]


def send(block, pairs):
    return lax.ppermute(block, "pcol", pairs)


def params(mib):
    return pltpu.CompilerParams(vmem_limit_bytes=mib << 20)


def cost(us):
    return pl.CostEstimate(flops=int(us * 1.1e9), bytes_accessed=int(us * 3.5e6), transcendentals=0)


def stack_kernel(start, step, *refs):
    def chunk(i, carry):
        src = pl.ds(pl.multiple_of(start + i * step, 128), step)
        dst = pl.ds(pl.multiple_of(i * step, 128), step)
        refs[-1][:, dst] = jnp.concatenate([r[:, src] for r in refs[:-1]], axis=0)
        return carry

    lax.fori_loop(0, refs[-1].shape[1] // step, chunk, 0)


def stack(parts, start, cols, name, us=1):
    rows = sum(p.shape[0] for p in parts)
    return pl.pallas_call(
        functools.partial(stack_kernel, start, min(cols, 1024)),
        in_specs=[VMEM] * len(parts),
        out_specs=VMEM,
        out_shape=jax.ShapeDtypeStruct((rows, cols), jnp.bfloat16),
        compiler_params=params(2),
        cost_estimate=cost(us),
        name=name,
    )(*parts)


def add_kernel(a_ref, b_ref, out_ref):
    out_ref[...] = (a_ref[...].astype(jnp.float32) + b_ref[...].astype(jnp.float32)).astype(jnp.bfloat16)


def add(a, b):
    return pl.pallas_call(
        add_kernel,
        in_specs=[VMEM, VMEM],
        out_specs=VMEM,
        out_shape=jax.ShapeDtypeStruct(a.shape, a.dtype),
        compiler_params=params(2),
        name="add",
    )(a, b)


def choose_kernel(rows, mask, first_ref, a_ref, b_ref, out_ref):
    other = (jnp.int32(mask) >> lax.div(first_ref[0], rows)) & 1

    @pl.when(other == 0)
    def _():
        out_ref[...] = a_ref[...]

    @pl.when(other == 1)
    def _():
        out_ref[...] = b_ref[...]


def choose(first, rows, others, a, b):
    return pl.pallas_call(
        functools.partial(choose_kernel, rows, sum(1 << z for z in others)),
        in_specs=[SMEM, VMEM, VMEM],
        out_specs=VMEM,
        out_shape=jax.ShapeDtypeStruct(a.shape, a.dtype),
        compiler_params=params(2),
        name="choose",
    )(first, a, b)


def join_kernel(rows, mask, first_ref, a_ref, b_ref, below_ref, out_ref):
    width = a_ref.shape[0]
    choose_kernel(rows, mask, first_ref, a_ref, b_ref, out_ref.at[pl.ds(0, width)])
    out_ref[width:, :] = below_ref[...]


def join(first, rows, others, a, b, below):
    width, cols = a.shape
    return pl.pallas_call(
        functools.partial(join_kernel, rows, sum(1 << z for z in others)),
        in_specs=[SMEM] + [VMEM] * 3,
        out_specs=VMEM,
        out_shape=jax.ShapeDtypeStruct((2 * width, cols), a.dtype),
        compiler_params=params(2),
        name="join",
    )(first, a, b, below)


def pick_kernel(blk, piv_ref, first_ref, trailing_ref, out_ref, head_ref, cnt_ref, lst_ref, own_ref, group_ref, rows_ref, sem, head_sem):
    width = piv_ref.shape[0]
    rows = trailing_ref.shape[0]
    first = first_ref[0]
    nblk = cnt_ref.shape[0]
    head = pltpu.make_async_copy(trailing_ref.at[pl.ds(0, width)], head_ref, head_sem)
    head.start()
    for b in range(nblk):
        cnt_ref[b] = 0

    def filt(i, n):
        loc = piv_ref[i] - first
        own_ref[n] = i
        return n + ((loc >= 0) & (loc < rows)).astype(jnp.int32)

    n = lax.fori_loop(0, width, filt, 0, unroll=8)

    def group(k):
        loc = piv_ref[own_ref[k]] - first
        base = pl.multiple_of(loc & ~15, 16)
        return pltpu.make_async_copy(trailing_ref.at[pl.ds(base, 16)], group_ref.at[k], sem)

    def begin(k, carry):
        group(k).start()
        i = own_ref[k]
        b = lax.div(piv_ref[i] - first, blk)
        m = cnt_ref[b]
        lst_ref[b * width + m] = i
        cnt_ref[b] = m + 1
        return carry

    def finish(k, carry):
        group(k).wait()
        return carry

    lax.fori_loop(0, n, begin, 0)
    rows_ref[...] = jnp.zeros_like(rows_ref)
    lax.fori_loop(0, n, finish, 0)
    sub = lax.broadcasted_iota(jnp.int32, (16, 128), 0)

    def extract(k, carry):
        i = own_ref[k]
        loc = piv_ref[i] - first
        tile = group_ref[k].astype(jnp.float32)
        row = jnp.sum(jnp.where(sub == (loc & 15), tile, 0.0), axis=0, keepdims=True)
        rows_ref[pl.ds(i, 1), :] = row
        return carry

    lax.fori_loop(0, n, extract, 0)
    out_ref[...] = rows_ref[...].astype(jnp.bfloat16)
    head.wait()


def pick(trailing, pivots, first, blk):
    rows, cols = trailing.shape
    width = pivots.shape[0]
    nblk = rows // blk
    return pl.pallas_call(
        functools.partial(pick_kernel, blk),
        in_specs=[SMEM, SMEM, pl.BlockSpec(memory_space=pltpu.HBM)],
        out_specs=[VMEM, VMEM, SMEM, SMEM],
        out_shape=[
            jax.ShapeDtypeStruct((width, cols), jnp.bfloat16),
            jax.ShapeDtypeStruct((width, cols), jnp.bfloat16),
            jax.ShapeDtypeStruct((nblk,), jnp.int32),
            jax.ShapeDtypeStruct((nblk * width,), jnp.int32),
        ],
        scratch_shapes=[
            pltpu.SMEM((width + 8,), jnp.int32),
            pltpu.VMEM((width, 16, cols), jnp.bfloat16),
            pltpu.VMEM((width, cols), jnp.float32),
            pltpu.SemaphoreType.DMA,
            pltpu.SemaphoreType.DMA,
        ],
        compiler_params=params(6),
        cost_estimate=cost(12),
        name="pick",
    )(pivots, first, trailing)


def dot(a, b):
    return lax.dot_general(
        a, b, (((1,), (0,)), ((), ())), precision=HIGHEST, preferred_element_type=jnp.float32
    )


def dot_exact(a, b):
    n = b.shape[1]
    hi = b.astype(jnp.bfloat16)
    rest = b - hi.astype(jnp.float32)
    mid = rest.astype(jnp.bfloat16)
    low = (rest - mid.astype(jnp.float32)).astype(jnp.bfloat16)
    r = lax.dot_general(
        a, jnp.concatenate([hi, mid, low], axis=1), (((1,), (0,)), ((), ())),
        preferred_element_type=jnp.float32,
    )
    return r[:, 2 * n :] + r[:, n : 2 * n] + r[:, :n]


def unit_inverse(strict):
    n = strict.shape[0]
    r = lax.broadcasted_iota(jnp.int32, (n, n), 0)
    c = lax.broadcasted_iota(jnp.int32, (n, n), 1)
    d = jnp.where((r >> 4) == (c >> 4), strict, 0.0)
    x = jnp.where(r == c, 1.0, 0.0) - d
    for step in range(3):
        d = dot_exact(d.astype(jnp.bfloat16), d) if step == 0 else dot(d, d)
        x = x + dot(x, d)
    for lg in (4, 5, 6):
        inside = ((r >> (lg + 1)) == (c >> (lg + 1))) & ((r >> lg) != (c >> lg))
        part = jnp.where(inside, strict, 0.0).astype(jnp.bfloat16)
        x = x - dot(x, dot_exact(part, x))
    return x


def blocks():
    return [(k, outer, inner) for k in range(2) for outer in OFFSETS for inner in OFFSETS]


def block_at(me, k, outer, inner):
    core = (me & 1) ^ k
    dx = jnp.where(core == 0, inner, outer)
    dy = jnp.where(core == 0, outer, inner)
    x = ((me >> 3) + dx) & 3
    y = ((me >> 1) + dy) & 3
    return pl.ds(pl.multiple_of(((x * 4 + y) * 2 + core) * 8, 8), 8)


def solve_kernel(me_ref, own_ref, other_ref, top_ref, more_ref, out_ref, a_ref, g_ref):
    n = top_ref.shape[0]
    h = n // 2
    me = me_ref[0]
    g_ref[:h, :] = own_ref[...].astype(jnp.float32)
    g_ref[h:, :] = other_ref[...].astype(jnp.float32)
    for b, where in enumerate(blocks()):
        a_ref[block_at(me, *where), :] = g_ref[8 * b : 8 * b + 8, :]
    r = lax.broadcasted_iota(jnp.int32, (h, h), 0)
    c = lax.broadcasted_iota(jnp.int32, (h, h), 1)
    s11 = jnp.where(r > c, a_ref[:h, :h].T, 0.0)
    s22 = jnp.where(r > c, a_ref[h:, h:].T, 0.0)
    s21 = a_ref[:h, h:].T
    x1 = unit_inverse(s11)
    x2 = unit_inverse(s22)
    top = sum(r[...].astype(jnp.float32) for r in (top_ref, more_ref))
    u1 = dot(x1, top[:h])
    u2 = dot(x2, top[h:] - dot_exact(s21.astype(jnp.bfloat16), u1))
    out_ref[...] = jnp.concatenate([u1, u2], axis=0).astype(jnp.bfloat16)


def solve(me, own, other, top, more):
    n, cols = top.shape
    return pl.pallas_call(
        solve_kernel,
        in_specs=[SMEM] + [VMEM] * 4,
        out_specs=VMEM,
        out_shape=jax.ShapeDtypeStruct((n, cols), jnp.bfloat16),
        scratch_shapes=[pltpu.VMEM((n, n), jnp.float32), pltpu.VMEM((n, n), jnp.float32)],
        compiler_params=params(6),
        name="solve",
    )(me, own, other, top, more)


def fetch_kernel(src_ref, dst_ref, sem):
    n = sem.shape[0]
    step = src_ref.shape[0] // n
    copies = [
        pltpu.make_async_copy(src_ref.at[pl.ds(i * step, step)], dst_ref.at[pl.ds(i * step, step)], sem.at[i])
        for i in range(n)
    ]
    for copy in copies:
        copy.start()
    for copy in copies:
        copy.wait()


def fetch(x):
    return pl.pallas_call(
        fetch_kernel,
        in_specs=[pl.BlockSpec(memory_space=pltpu.HBM)],
        out_specs=VMEM,
        out_shape=jax.ShapeDtypeStruct(x.shape, x.dtype),
        scratch_shapes=[pltpu.SemaphoreType.DMA((4,))],
        compiler_params=params(2),
        name="fetch",
    )(x)


def update_kernel(cnt_ref, lst_ref, piv_ref, first_ref, me_ref, tr_ref, ud_ref, rest_ref, *refs):
    parts = refs[1:11]
    out_ref, buf_ref, nat_ref, drow_ref, tmp_ref, sem = refs[11:]
    rows = buf_ref.shape[0]
    nblk = sem.shape[0]
    blk = rows // nblk
    width = nat_ref.shape[0]
    first = first_ref[0]
    late = lax.div(first, rows) >> 2

    @pl.when(late == 0)
    def _():
        nat_ref[...] = ud_ref[:width, :].astype(jnp.float32)
        drow_ref[...] = ud_ref[width:, :].astype(jnp.float32)

    @pl.when(late == 1)
    def _():
        nat_ref[...] = rest_ref[:width, :].astype(jnp.float32)
        drow_ref[...] = rest_ref[width:, :].astype(jnp.float32)

    sub = lax.broadcasted_iota(jnp.int32, (16, 128), 0)

    def fix(k, carry):
        i = lst_ref[k]
        loc = piv_ref[i] - first
        at = pl.ds(pl.multiple_of(loc & ~15, 16), 16)
        old = buf_ref[at, :].astype(jnp.float32)
        row = drow_ref[pl.ds(i, 1), :]
        buf_ref[at, :] = jnp.where(sub == (loc & 15), row, old).astype(jnp.bfloat16)
        return carry

    lax.fori_loop(0, cnt_ref[0], fix, 0)
    for i, where in enumerate(blocks()):
        tmp_ref[8 * i : 8 * i + 8, :] = nat_ref[block_at(me_ref[0], *where), :]
    ut = tmp_ref[...].T.astype(jnp.bfloat16)
    copies = []
    for b in range(nblk):
        half = b // (nblk // 2)
        here = pl.ds(b * blk, blk)
        there = pl.ds((b - half * (nblk // 2)) * blk, blk)
        pieces = []
        for s in (parts[:5], parts[5:]):
            pieces += [s[0][:, here], s[1][:, here], s[2][:, here], s[3 + half][:, there]]
        product = lax.dot_general(
            ut, jnp.concatenate(pieces, axis=0), (((1,), (0,)), ((), ())),
            preferred_element_type=jnp.float32,
        ).T
        new = buf_ref[here, :].astype(jnp.float32) - product
        if b == 0:
            head = jnp.where(first == 0, nat_ref[...], new[:width])
            buf_ref[:width, :] = head.astype(jnp.bfloat16)
            buf_ref[width:blk, :] = new[width:].astype(jnp.bfloat16)
        else:
            buf_ref[here, :] = new.astype(jnp.bfloat16)
        copies.append(pltpu.make_async_copy(buf_ref.at[here], out_ref.at[here], sem.at[b]))
        copies[-1].start()
    for copy in copies:
        copy.wait()


def update(cnt, lst, pivots, first, me, trailing, ud, rest, ahead, parts, nblk):
    rows, cols = trailing.shape
    width = pivots.shape[0]
    return pl.pallas_call(
        update_kernel,
        in_specs=[SMEM] * 5 + [VMEM] * 14,
        out_specs=[pl.BlockSpec(memory_space=pltpu.HBM), VMEM],
        scratch_shapes=[
            pltpu.VMEM((width, cols), jnp.float32),
            pltpu.VMEM((width, cols), jnp.float32),
            pltpu.VMEM((width, cols), jnp.float32),
            pltpu.SemaphoreType.DMA((nblk,)),
        ],
        out_shape=[jax.ShapeDtypeStruct((rows, cols), jnp.bfloat16)] * 2,
        input_output_aliases={5: 1},
        compiler_params=params(16),
        name="update",
    )(cnt, lst, pivots, first, me, trailing, ud, rest, ahead, *parts)[0]


def body(trailing, panel_t, pivots):
    rows = trailing.shape[0]
    width = pivots.shape[0]
    half = rows // 2
    barrier = lax.optimization_barrier
    first = (lax.axis_index("prow") * rows).astype(jnp.int32).reshape(1)
    me = lax.axis_index("pcol").astype(jnp.int32).reshape(1)
    trailing = pltpu.with_memory_space_constraint(trailing, pltpu.HBM)

    def zsend(x, pairs):
        return lax.ppermute(x, "prow", pairs)

    p, m, q = [send(panel_t, hop(d, 0, True)) for d in (1, -1, 2)]

    top, disp, cnt, lst = pick(trailing, pivots, first, rows)
    more = zsend(top, [(i + 4, i) for i in range(4)])
    p, m, q, top = barrier((p, m, q, top))

    up, down, across = hop(0, 1, True), hop(0, -1, True), hop(0, 2, True)
    diag = stack([panel_t, p, m, q], 0, width, "stack_d")
    diag_q, diag_p, diag_m = send(diag, across), send(diag, up), send(diag, down)
    block = stack([panel_t, p, m, q], 0, rows, "stack_p")
    block, diag_q, diag_p, diag_m, top, more = barrier((block, diag_q, diag_p, diag_m, top, more))
    near, far = send(block, up), send(block, down)
    own = stack([diag, diag_p, diag_m, diag_q], 0, width, "stack_l")
    top = add(top, more)
    more = zsend(top, [(2, 0), (3, 1)])
    top = add(top, more)
    top, disp, own, block2 = barrier((top, disp, own, block))
    other = send(own, CORES)
    other, source = barrier((other, trailing))
    copy = fetch(pltpu.with_memory_space_constraint(source, pltpu.HBM))
    more = zsend(top, [(1, 0)])
    lower = zsend(disp, [(0, 2)])
    top, block2 = barrier((top, block))
    swap = send(block2, CORES)
    more, disp, lower, copy = barrier((more, disp, lower, copy))
    disp = choose(first, rows, (2,), disp, lower)
    disp = choose(first, rows, (1, 3), disp, zsend(disp, [(0, 1), (2, 3)]))
    more, disp, near, far, swap = barrier((more, disp, near, far, swap))
    fa, fb = stack([near], 0, half, "stack_a"), stack([far], half, half, "stack_b")
    qa, qb = send(fa, up), send(fb, down)
    u = solve(me, own, other, top, more)
    ru = zsend(u, [(0, 2)])
    u = choose(first, rows, (2,), u, ru)
    u, near, far = barrier((u, near, far))
    other_near, other_far = send(near, CORES), send(far, CORES)
    ud = join(first, rows, (1, 3), u, zsend(u, [(0, 1), (2, 3)]), disp)
    rest = zsend(ud, [(i, i + 4) for i in range(4)])
    ahead = stack([qa, qb], 0, 128, "stack_q", 60)
    own = [block, near, far, qa, qb]
    parts = own + [swap, other_near, other_far, send(qa, CORES), send(qb, CORES)]
    return update(cnt, lst, pivots, first, me, copy, ud, rest, ahead, parts, NBLK)


def solution(mesh):
    return jax.shard_map(
        body,
        mesh=mesh,
        in_specs=(P("prow", "pcol"), P("pcol", "prow"), P()),
        out_specs=P("prow", "pcol"),
        check_vma=False,
    )
```

```python
import functools

import jax
import jax.numpy as jnp
from jax import lax
from jax.experimental import pallas as pl
from jax.experimental.pallas import tpu as pltpu
from jax.sharding import PartitionSpec as P

NX = 4
NY = 4
OFFSETS = (0, -1, 1, 2)
NBLK = 12
SMEM = pl.BlockSpec(memory_space=pltpu.SMEM)
VMEM = pl.BlockSpec(memory_space=pltpu.VMEM)
HIGHEST = lax.Precision.HIGHEST


def place(x, y, c):
    return ((x % NX) * NY + (y % NY)) * 2 + c


def hop(dx, dy, turn):
    pairs = []
    for x in range(NX):
        for y in range(NY):
            for c in range(2):
                a, b = (dy, dx) if turn and c == 1 else (dx, dy)
                pairs.append((place(x, y, c), place(x + a, y + b, c)))
    return pairs


CORES = [(p, p ^ 1) for p in range(NX * NY * 2)]


def send(block, pairs):
    return lax.ppermute(block, "pcol", pairs)


def params(mib):
    return pltpu.CompilerParams(vmem_limit_bytes=mib << 20)


def cost(us):
    return pl.CostEstimate(flops=int(us * 1.1e9), bytes_accessed=int(us * 3.5e6), transcendentals=0)


def stack_kernel(start, step, *refs):
    def chunk(i, carry):
        src = pl.ds(pl.multiple_of(start + i * step, 128), step)
        dst = pl.ds(pl.multiple_of(i * step, 128), step)
        refs[-1][:, dst] = jnp.concatenate([r[:, src] for r in refs[:-1]], axis=0)
        return carry

    lax.fori_loop(0, refs[-1].shape[1] // step, chunk, 0)


def stack(parts, start, cols, name, us=1):
    rows = sum(p.shape[0] for p in parts)
    return pl.pallas_call(
        functools.partial(stack_kernel, start, min(cols, 1024)),
        in_specs=[VMEM] * len(parts),
        out_specs=VMEM,
        out_shape=jax.ShapeDtypeStruct((rows, cols), jnp.bfloat16),
        compiler_params=params(2),
        cost_estimate=cost(us),
        name=name,
    )(*parts)


def add_kernel(a_ref, b_ref, out_ref):
    out_ref[...] = (a_ref[...].astype(jnp.float32) + b_ref[...].astype(jnp.float32)).astype(jnp.bfloat16)


def add(a, b):
    return pl.pallas_call(
        add_kernel,
        in_specs=[VMEM, VMEM],
        out_specs=VMEM,
        out_shape=jax.ShapeDtypeStruct(a.shape, a.dtype),
        compiler_params=params(2),
        name="add",
    )(a, b)


def choose_kernel(rows, mask, first_ref, a_ref, b_ref, out_ref):
    other = (jnp.int32(mask) >> lax.div(first_ref[0], rows)) & 1

    @pl.when(other == 0)
    def _():
        out_ref[...] = a_ref[...]

    @pl.when(other == 1)
    def _():
        out_ref[...] = b_ref[...]


def choose(first, rows, others, a, b):
    return pl.pallas_call(
        functools.partial(choose_kernel, rows, sum(1 << z for z in others)),
        in_specs=[SMEM, VMEM, VMEM],
        out_specs=VMEM,
        out_shape=jax.ShapeDtypeStruct(a.shape, a.dtype),
        compiler_params=params(2),
        name="choose",
    )(first, a, b)


def join_kernel(rows, mask, first_ref, a_ref, b_ref, below_ref, out_ref):
    width = a_ref.shape[0]
    choose_kernel(rows, mask, first_ref, a_ref, b_ref, out_ref.at[pl.ds(0, width)])
    out_ref[width:, :] = below_ref[...]


def join(first, rows, others, a, b, below):
    width, cols = a.shape
    return pl.pallas_call(
        functools.partial(join_kernel, rows, sum(1 << z for z in others)),
        in_specs=[SMEM] + [VMEM] * 3,
        out_specs=VMEM,
        out_shape=jax.ShapeDtypeStruct((2 * width, cols), a.dtype),
        compiler_params=params(2),
        name="join",
    )(first, a, b, below)


def pick_kernel(blk, piv_ref, first_ref, trailing_ref, out_ref, head_ref, cnt_ref, lst_ref, own_ref, group_ref, rows_ref, sem, head_sem):
    width = piv_ref.shape[0]
    rows = trailing_ref.shape[0]
    first = first_ref[0]
    nblk = cnt_ref.shape[0]
    head = pltpu.make_async_copy(trailing_ref.at[pl.ds(0, width)], head_ref, head_sem)
    head.start()
    for b in range(nblk):
        cnt_ref[b] = 0

    def filt(i, n):
        loc = piv_ref[i] - first
        own_ref[n] = i
        return n + ((loc >= 0) & (loc < rows)).astype(jnp.int32)

    n = lax.fori_loop(0, width, filt, 0, unroll=8)

    def group(k):
        loc = piv_ref[own_ref[k]] - first
        base = pl.multiple_of(loc & ~15, 16)
        return pltpu.make_async_copy(trailing_ref.at[pl.ds(base, 16)], group_ref.at[k], sem)

    def begin(k, carry):
        group(k).start()
        i = own_ref[k]
        b = lax.div(piv_ref[i] - first, blk)
        m = cnt_ref[b]
        lst_ref[b * width + m] = i
        cnt_ref[b] = m + 1
        return carry

    def finish(k, carry):
        group(k).wait()
        return carry

    lax.fori_loop(0, n, begin, 0)
    rows_ref[...] = jnp.zeros_like(rows_ref)
    lax.fori_loop(0, n, finish, 0)
    sub = lax.broadcasted_iota(jnp.int32, (16, 128), 0)

    def extract(k, carry):
        i = own_ref[k]
        loc = piv_ref[i] - first
        tile = group_ref[k].astype(jnp.float32)
        row = jnp.sum(jnp.where(sub == (loc & 15), tile, 0.0), axis=0, keepdims=True)
        rows_ref[pl.ds(i, 1), :] = row
        return carry

    lax.fori_loop(0, n, extract, 0)
    out_ref[...] = rows_ref[...].astype(jnp.bfloat16)
    head.wait()


def pick(trailing, pivots, first, blk):
    rows, cols = trailing.shape
    width = pivots.shape[0]
    nblk = rows // blk
    return pl.pallas_call(
        functools.partial(pick_kernel, blk),
        in_specs=[SMEM, SMEM, pl.BlockSpec(memory_space=pltpu.HBM)],
        out_specs=[VMEM, VMEM, SMEM, SMEM],
        out_shape=[
            jax.ShapeDtypeStruct((width, cols), jnp.bfloat16),
            jax.ShapeDtypeStruct((width, cols), jnp.bfloat16),
            jax.ShapeDtypeStruct((nblk,), jnp.int32),
            jax.ShapeDtypeStruct((nblk * width,), jnp.int32),
        ],
        scratch_shapes=[
            pltpu.SMEM((width + 8,), jnp.int32),
            pltpu.VMEM((width, 16, cols), jnp.bfloat16),
            pltpu.VMEM((width, cols), jnp.float32),
            pltpu.SemaphoreType.DMA,
            pltpu.SemaphoreType.DMA,
        ],
        compiler_params=params(6),
        cost_estimate=cost(12),
        name="pick",
    )(pivots, first, trailing)


def dot(a, b):
    return lax.dot_general(
        a, b, (((1,), (0,)), ((), ())), precision=HIGHEST, preferred_element_type=jnp.float32
    )


def dot_exact(a, b):
    n = b.shape[1]
    hi = b.astype(jnp.bfloat16)
    rest = b - hi.astype(jnp.float32)
    mid = rest.astype(jnp.bfloat16)
    low = (rest - mid.astype(jnp.float32)).astype(jnp.bfloat16)
    r = lax.dot_general(
        a, jnp.concatenate([hi, mid, low], axis=1), (((1,), (0,)), ((), ())),
        preferred_element_type=jnp.float32,
    )
    return r[:, 2 * n :] + r[:, n : 2 * n] + r[:, :n]


def unit_inverse(strict):
    n = strict.shape[0]
    r = lax.broadcasted_iota(jnp.int32, (n, n), 0)
    c = lax.broadcasted_iota(jnp.int32, (n, n), 1)
    d = jnp.where((r >> 4) == (c >> 4), strict, 0.0)
    x = jnp.where(r == c, 1.0, 0.0) - d
    for step in range(3):
        d = dot_exact(d.astype(jnp.bfloat16), d) if step == 0 else dot(d, d)
        x = x + dot(x, d)
    for lg in (4, 5, 6):
        inside = ((r >> (lg + 1)) == (c >> (lg + 1))) & ((r >> lg) != (c >> lg))
        part = jnp.where(inside, strict, 0.0).astype(jnp.bfloat16)
        x = x - dot(x, dot_exact(part, x))
    return x


def blocks():
    return [(k, outer, inner) for k in range(2) for outer in OFFSETS for inner in OFFSETS]


def block_at(me, k, outer, inner):
    core = (me & 1) ^ k
    dx = jnp.where(core == 0, inner, outer)
    dy = jnp.where(core == 0, outer, inner)
    x = ((me >> 3) + dx) & 3
    y = ((me >> 1) + dy) & 3
    return pl.ds(pl.multiple_of(((x * 4 + y) * 2 + core) * 8, 8), 8)


def solve_kernel(me_ref, own_ref, other_ref, top_ref, more_ref, out_ref, a_ref, g_ref):
    n = top_ref.shape[0]
    h = n // 2
    me = me_ref[0]
    g_ref[:h, :] = own_ref[...].astype(jnp.float32)
    g_ref[h:, :] = other_ref[...].astype(jnp.float32)
    for b, where in enumerate(blocks()):
        a_ref[block_at(me, *where), :] = g_ref[8 * b : 8 * b + 8, :]
    r = lax.broadcasted_iota(jnp.int32, (h, h), 0)
    c = lax.broadcasted_iota(jnp.int32, (h, h), 1)
    s11 = jnp.where(r > c, a_ref[:h, :h].T, 0.0)
    s22 = jnp.where(r > c, a_ref[h:, h:].T, 0.0)
    s21 = a_ref[:h, h:].T
    x1 = unit_inverse(s11)
    x2 = unit_inverse(s22)
    top = sum(r[...].astype(jnp.float32) for r in (top_ref, more_ref))
    u1 = dot(x1, top[:h])
    u2 = dot(x2, top[h:] - dot_exact(s21.astype(jnp.bfloat16), u1))
    out_ref[...] = jnp.concatenate([u1, u2], axis=0).astype(jnp.bfloat16)


def solve(me, own, other, top, more):
    n, cols = top.shape
    return pl.pallas_call(
        solve_kernel,
        in_specs=[SMEM] + [VMEM] * 4,
        out_specs=VMEM,
        out_shape=jax.ShapeDtypeStruct((n, cols), jnp.bfloat16),
        scratch_shapes=[pltpu.VMEM((n, n), jnp.float32), pltpu.VMEM((n, n), jnp.float32)],
        compiler_params=params(6),
        name="solve",
    )(me, own, other, top, more)


def fetch_kernel(src_ref, dst_ref, sem):
    n = sem.shape[0]
    step = src_ref.shape[0] // n
    copies = [
        pltpu.make_async_copy(src_ref.at[pl.ds(i * step, step)], dst_ref.at[pl.ds(i * step, step)], sem.at[i])
        for i in range(n)
    ]
    for copy in copies:
        copy.start()
    for copy in copies:
        copy.wait()


def fetch(x):
    return pl.pallas_call(
        fetch_kernel,
        in_specs=[pl.BlockSpec(memory_space=pltpu.HBM)],
        out_specs=VMEM,
        out_shape=jax.ShapeDtypeStruct(x.shape, x.dtype),
        scratch_shapes=[pltpu.SemaphoreType.DMA((4,))],
        compiler_params=params(2),
        name="fetch",
    )(x)


def update_kernel(cnt_ref, lst_ref, piv_ref, first_ref, me_ref, tr_ref, ud_ref, rest_ref, *refs):
    parts = refs[1:11]
    out_ref, buf_ref, nat_ref, drow_ref, tmp_ref, sem = refs[11:]
    rows = buf_ref.shape[0]
    nblk = sem.shape[0]
    blk = rows // nblk
    width = nat_ref.shape[0]
    first = first_ref[0]
    late = lax.div(first, rows) >> 2

    @pl.when(late == 0)
    def _():
        nat_ref[...] = ud_ref[:width, :].astype(jnp.float32)
        drow_ref[...] = ud_ref[width:, :].astype(jnp.float32)

    @pl.when(late == 1)
    def _():
        nat_ref[...] = rest_ref[:width, :].astype(jnp.float32)
        drow_ref[...] = rest_ref[width:, :].astype(jnp.float32)

    sub = lax.broadcasted_iota(jnp.int32, (16, 128), 0)

    def fix(k, carry):
        i = lst_ref[k]
        loc = piv_ref[i] - first
        at = pl.ds(pl.multiple_of(loc & ~15, 16), 16)
        old = buf_ref[at, :].astype(jnp.float32)
        row = drow_ref[pl.ds(i, 1), :]
        buf_ref[at, :] = jnp.where(sub == (loc & 15), row, old).astype(jnp.bfloat16)
        return carry

    lax.fori_loop(0, cnt_ref[0], fix, 0)
    for i, where in enumerate(blocks()):
        tmp_ref[8 * i : 8 * i + 8, :] = nat_ref[block_at(me_ref[0], *where), :]
    ut = tmp_ref[...].T.astype(jnp.bfloat16)
    copies = []
    for b in range(nblk):
        half = b // (nblk // 2)
        here = pl.ds(b * blk, blk)
        there = pl.ds((b - half * (nblk // 2)) * blk, blk)
        pieces = []
        for s in (parts[:5], parts[5:]):
            pieces += [s[0][:, here], s[1][:, here], s[2][:, here], s[3 + half][:, there]]
        product = lax.dot_general(
            ut, jnp.concatenate(pieces, axis=0), (((1,), (0,)), ((), ())),
            preferred_element_type=jnp.float32,
        ).T
        new = buf_ref[here, :].astype(jnp.float32) - product
        if b == 0:
            head = jnp.where(first == 0, nat_ref[...], new[:width])
            buf_ref[:width, :] = head.astype(jnp.bfloat16)
            buf_ref[width:blk, :] = new[width:].astype(jnp.bfloat16)
        else:
            buf_ref[here, :] = new.astype(jnp.bfloat16)
        copies.append(pltpu.make_async_copy(buf_ref.at[here], out_ref.at[here], sem.at[b]))
        copies[-1].start()
    for copy in copies:
        copy.wait()


def update(cnt, lst, pivots, first, me, trailing, ud, rest, ahead, parts, nblk):
    rows, cols = trailing.shape
    width = pivots.shape[0]
    return pl.pallas_call(
        update_kernel,
        in_specs=[SMEM] * 5 + [VMEM] * 14,
        out_specs=[pl.BlockSpec(memory_space=pltpu.HBM), VMEM],
        scratch_shapes=[
            pltpu.VMEM((width, cols), jnp.float32),
            pltpu.VMEM((width, cols), jnp.float32),
            pltpu.VMEM((width, cols), jnp.float32),
            pltpu.SemaphoreType.DMA((nblk,)),
        ],
        out_shape=[jax.ShapeDtypeStruct((rows, cols), jnp.bfloat16)] * 2,
        input_output_aliases={5: 1},
        compiler_params=params(16),
        name="update",
    )(cnt, lst, pivots, first, me, trailing, ud, rest, ahead, *parts)[0]


def body(trailing, panel_t, pivots):
    rows = trailing.shape[0]
    width = pivots.shape[0]
    half = rows // 2
    barrier = lax.optimization_barrier
    first = (lax.axis_index("prow") * rows).astype(jnp.int32).reshape(1)
    me = lax.axis_index("pcol").astype(jnp.int32).reshape(1)
    trailing = pltpu.with_memory_space_constraint(trailing, pltpu.HBM)

    def zsend(x, pairs):
        return lax.ppermute(x, "prow", pairs)

    p, m, q = [send(panel_t, hop(d, 0, True)) for d in (1, -1, 2)]

    top, disp, cnt, lst = pick(trailing, pivots, first, rows)
    more = zsend(top, [(i + 4, i) for i in range(4)])
    p, m, q, top = barrier((p, m, q, top))

    up, down, across = hop(0, 1, True), hop(0, -1, True), hop(0, 2, True)
    diag = stack([panel_t, p, m, q], 0, width, "stack_d")
    diag_q, diag_p, diag_m = send(diag, across), send(diag, up), send(diag, down)
    block = stack([panel_t, p, m, q], 0, rows, "stack_p")
    block, diag_q, diag_p, diag_m, top, more = barrier((block, diag_q, diag_p, diag_m, top, more))
    near, far = send(block, up), send(block, down)
    own = stack([diag, diag_p, diag_m, diag_q], 0, width, "stack_l")
    top = add(top, more)
    more = zsend(top, [(2, 0), (3, 1)])
    top = add(top, more)
    top, disp, own, block2 = barrier((top, disp, own, block))
    other = send(own, CORES)
    more = zsend(top, [(1, 0)])
    lower = zsend(disp, [(0, 2)])
    top, block2 = barrier((top, block))
    swap = send(block2, CORES)
    more, disp, lower, other, near, far, swap = barrier((more, disp, lower, other, near, far, swap))
    fa, fb = stack([near], 0, half, "stack_a"), stack([far], half, half, "stack_b")
    qa, qb = send(fa, up), send(fb, down)
    u = solve(me, own, other, top, more)
    ru = zsend(u, [(0, 2)])
    u, source = barrier((u, trailing))
    copy = fetch(pltpu.with_memory_space_constraint(source, pltpu.HBM))
    ru, copy = barrier((ru, copy))
    disp = choose(first, rows, (2,), disp, lower)
    disp = choose(first, rows, (1, 3), disp, zsend(disp, [(0, 1), (2, 3)]))
    u = choose(first, rows, (2,), u, ru)
    u, near, far = barrier((u, near, far))
    other_near, other_far = send(near, CORES), send(far, CORES)
    ud = join(first, rows, (1, 3), u, zsend(u, [(0, 1), (2, 3)]), disp)
    rest = zsend(ud, [(i, i + 4) for i in range(4)])
    ahead = stack([qa, qb], 0, 128, "stack_q", 60)
    own = [block, near, far, qa, qb]
    parts = own + [swap, other_near, other_far, send(qa, CORES), send(qb, CORES)]
    return update(cnt, lst, pivots, first, me, copy, ud, rest, ahead, parts, NBLK)


def solution(mesh):
    return jax.shard_map(
        body,
        mesh=mesh,
        in_specs=(P("prow", "pcol"), P("pcol", "prow"), P()),
        out_specs=P("prow", "pcol"),
        check_vma=False,
    )
```

```python
import functools

import jax
import jax.numpy as jnp
from jax import lax
from jax.experimental import pallas as pl
from jax.experimental.pallas import tpu as pltpu
from jax.sharding import PartitionSpec as P

NX = 4
NY = 4
OFFSETS = (0, -1, 1, 2)
NBLK = 12
SMEM = pl.BlockSpec(memory_space=pltpu.SMEM)
VMEM = pl.BlockSpec(memory_space=pltpu.VMEM)
HIGHEST = lax.Precision.HIGHEST


def place(x, y, c):
    return ((x % NX) * NY + (y % NY)) * 2 + c


def hop(dx, dy, turn):
    pairs = []
    for x in range(NX):
        for y in range(NY):
            for c in range(2):
                a, b = (dy, dx) if turn and c == 1 else (dx, dy)
                pairs.append((place(x, y, c), place(x + a, y + b, c)))
    return pairs


CORES = [(p, p ^ 1) for p in range(NX * NY * 2)]


def send(block, pairs):
    return lax.ppermute(block, "pcol", pairs)


def params(mib):
    return pltpu.CompilerParams(vmem_limit_bytes=mib << 20)


def cost(us):
    return pl.CostEstimate(flops=int(us * 1.1e9), bytes_accessed=int(us * 3.5e6), transcendentals=0)


def stack_kernel(start, step, *refs):
    def chunk(i, carry):
        src = pl.ds(pl.multiple_of(start + i * step, 128), step)
        dst = pl.ds(pl.multiple_of(i * step, 128), step)
        refs[-1][:, dst] = jnp.concatenate([r[:, src] for r in refs[:-1]], axis=0)
        return carry

    lax.fori_loop(0, refs[-1].shape[1] // step, chunk, 0)


def stack(parts, start, cols, name, us=1):
    rows = sum(p.shape[0] for p in parts)
    return pl.pallas_call(
        functools.partial(stack_kernel, start, min(cols, 1024)),
        in_specs=[VMEM] * len(parts),
        out_specs=VMEM,
        out_shape=jax.ShapeDtypeStruct((rows, cols), jnp.bfloat16),
        compiler_params=params(2),
        cost_estimate=cost(us),
        name=name,
    )(*parts)


def add_kernel(a_ref, b_ref, out_ref):
    out_ref[...] = (a_ref[...].astype(jnp.float32) + b_ref[...].astype(jnp.float32)).astype(jnp.bfloat16)


def add(a, b):
    return pl.pallas_call(
        add_kernel,
        in_specs=[VMEM, VMEM],
        out_specs=VMEM,
        out_shape=jax.ShapeDtypeStruct(a.shape, a.dtype),
        compiler_params=params(2),
        name="add",
    )(a, b)


def choose_kernel(rows, mask, first_ref, a_ref, b_ref, out_ref):
    other = (jnp.int32(mask) >> lax.div(first_ref[0], rows)) & 1

    @pl.when(other == 0)
    def _():
        out_ref[...] = a_ref[...]

    @pl.when(other == 1)
    def _():
        out_ref[...] = b_ref[...]


def choose(first, rows, others, a, b):
    return pl.pallas_call(
        functools.partial(choose_kernel, rows, sum(1 << z for z in others)),
        in_specs=[SMEM, VMEM, VMEM],
        out_specs=VMEM,
        out_shape=jax.ShapeDtypeStruct(a.shape, a.dtype),
        compiler_params=params(2),
        name="choose",
    )(first, a, b)


def join_kernel(rows, mask, first_ref, a_ref, b_ref, below_ref, out_ref):
    width = a_ref.shape[0]
    choose_kernel(rows, mask, first_ref, a_ref, b_ref, out_ref.at[pl.ds(0, width)])
    out_ref[width:, :] = below_ref[...]


def join(first, rows, others, a, b, below):
    width, cols = a.shape
    return pl.pallas_call(
        functools.partial(join_kernel, rows, sum(1 << z for z in others)),
        in_specs=[SMEM] + [VMEM] * 3,
        out_specs=VMEM,
        out_shape=jax.ShapeDtypeStruct((2 * width, cols), a.dtype),
        compiler_params=params(2),
        name="join",
    )(first, a, b, below)


def pick_kernel(blk, piv_ref, first_ref, trailing_ref, out_ref, head_ref, cnt_ref, lst_ref, own_ref, group_ref, rows_ref, sem, head_sem):
    width = piv_ref.shape[0]
    rows = trailing_ref.shape[0]
    first = first_ref[0]
    nblk = cnt_ref.shape[0]
    head = pltpu.make_async_copy(trailing_ref.at[pl.ds(0, width)], head_ref, head_sem)
    head.start()
    for b in range(nblk):
        cnt_ref[b] = 0

    def filt(i, n):
        loc = piv_ref[i] - first
        own_ref[n] = i
        return n + ((loc >= 0) & (loc < rows)).astype(jnp.int32)

    n = lax.fori_loop(0, width, filt, 0, unroll=8)

    def group(k):
        loc = piv_ref[own_ref[k]] - first
        base = pl.multiple_of(loc & ~15, 16)
        return pltpu.make_async_copy(trailing_ref.at[pl.ds(base, 16)], group_ref.at[k], sem)

    def begin(k, carry):
        group(k).start()
        i = own_ref[k]
        b = lax.div(piv_ref[i] - first, blk)
        m = cnt_ref[b]
        lst_ref[b * width + m] = i
        cnt_ref[b] = m + 1
        return carry

    def finish(k, carry):
        group(k).wait()
        return carry

    lax.fori_loop(0, n, begin, 0)
    rows_ref[...] = jnp.zeros_like(rows_ref)
    lax.fori_loop(0, n, finish, 0)
    sub = lax.broadcasted_iota(jnp.int32, (16, 128), 0)

    def extract(k, carry):
        i = own_ref[k]
        loc = piv_ref[i] - first
        tile = group_ref[k].astype(jnp.float32)
        row = jnp.sum(jnp.where(sub == (loc & 15), tile, 0.0), axis=0, keepdims=True)
        rows_ref[pl.ds(i, 1), :] = row
        return carry

    lax.fori_loop(0, n, extract, 0)
    out_ref[...] = rows_ref[...].astype(jnp.bfloat16)
    head.wait()


def pick(trailing, pivots, first, blk):
    rows, cols = trailing.shape
    width = pivots.shape[0]
    nblk = rows // blk
    return pl.pallas_call(
        functools.partial(pick_kernel, blk),
        in_specs=[SMEM, SMEM, pl.BlockSpec(memory_space=pltpu.HBM)],
        out_specs=[VMEM, VMEM, SMEM, SMEM],
        out_shape=[
            jax.ShapeDtypeStruct((width, cols), jnp.bfloat16),
            jax.ShapeDtypeStruct((width, cols), jnp.bfloat16),
            jax.ShapeDtypeStruct((nblk,), jnp.int32),
            jax.ShapeDtypeStruct((nblk * width,), jnp.int32),
        ],
        scratch_shapes=[
            pltpu.SMEM((width + 8,), jnp.int32),
            pltpu.VMEM((width, 16, cols), jnp.bfloat16),
            pltpu.VMEM((width, cols), jnp.float32),
            pltpu.SemaphoreType.DMA,
            pltpu.SemaphoreType.DMA,
        ],
        compiler_params=params(6),
        cost_estimate=cost(12),
        name="pick",
    )(pivots, first, trailing)


def dot(a, b):
    return lax.dot_general(
        a, b, (((1,), (0,)), ((), ())), precision=HIGHEST, preferred_element_type=jnp.float32
    )


def dot_exact(a, b):
    n = b.shape[1]
    hi = b.astype(jnp.bfloat16)
    rest = b - hi.astype(jnp.float32)
    mid = rest.astype(jnp.bfloat16)
    low = (rest - mid.astype(jnp.float32)).astype(jnp.bfloat16)
    r = lax.dot_general(
        a, jnp.concatenate([hi, mid, low], axis=1), (((1,), (0,)), ((), ())),
        preferred_element_type=jnp.float32,
    )
    return r[:, 2 * n :] + r[:, n : 2 * n] + r[:, :n]


def unit_inverse(strict):
    n = strict.shape[0]
    r = lax.broadcasted_iota(jnp.int32, (n, n), 0)
    c = lax.broadcasted_iota(jnp.int32, (n, n), 1)
    d = jnp.where((r >> 4) == (c >> 4), strict, 0.0)
    x = jnp.where(r == c, 1.0, 0.0) - d
    for step in range(3):
        d = dot_exact(d.astype(jnp.bfloat16), d) if step == 0 else dot(d, d)
        x = x + dot(x, d)
    for lg in (4, 5, 6):
        inside = ((r >> (lg + 1)) == (c >> (lg + 1))) & ((r >> lg) != (c >> lg))
        part = jnp.where(inside, strict, 0.0).astype(jnp.bfloat16)
        x = x - dot(x, dot_exact(part, x))
    return x


def blocks():
    return [(k, outer, inner) for k in range(2) for outer in OFFSETS for inner in OFFSETS]


def block_at(me, k, outer, inner):
    core = (me & 1) ^ k
    dx = jnp.where(core == 0, inner, outer)
    dy = jnp.where(core == 0, outer, inner)
    x = ((me >> 3) + dx) & 3
    y = ((me >> 1) + dy) & 3
    return pl.ds(pl.multiple_of(((x * 4 + y) * 2 + core) * 8, 8), 8)


def solve_kernel(me_ref, own_ref, other_ref, top_ref, more_ref, out_ref, a_ref, g_ref):
    n = top_ref.shape[0]
    h = n // 2
    me = me_ref[0]
    g_ref[:h, :] = own_ref[...].astype(jnp.float32)
    g_ref[h:, :] = other_ref[...].astype(jnp.float32)
    for b, where in enumerate(blocks()):
        a_ref[block_at(me, *where), :] = g_ref[8 * b : 8 * b + 8, :]
    r = lax.broadcasted_iota(jnp.int32, (h, h), 0)
    c = lax.broadcasted_iota(jnp.int32, (h, h), 1)
    s11 = jnp.where(r > c, a_ref[:h, :h].T, 0.0)
    s22 = jnp.where(r > c, a_ref[h:, h:].T, 0.0)
    s21 = a_ref[:h, h:].T
    x1 = unit_inverse(s11)
    x2 = unit_inverse(s22)
    top = sum(r[...].astype(jnp.float32) for r in (top_ref, more_ref))
    u1 = dot(x1, top[:h])
    u2 = dot(x2, top[h:] - dot_exact(s21.astype(jnp.bfloat16), u1))
    out_ref[...] = jnp.concatenate([u1, u2], axis=0).astype(jnp.bfloat16)


def solve(me, own, other, top, more):
    n, cols = top.shape
    return pl.pallas_call(
        solve_kernel,
        in_specs=[SMEM] + [VMEM] * 4,
        out_specs=VMEM,
        out_shape=jax.ShapeDtypeStruct((n, cols), jnp.bfloat16),
        scratch_shapes=[pltpu.VMEM((n, n), jnp.float32), pltpu.VMEM((n, n), jnp.float32)],
        compiler_params=params(6),
        name="solve",
    )(me, own, other, top, more)


def fetch_kernel(src_ref, dst_ref, sem):
    n = sem.shape[0]
    step = src_ref.shape[0] // n
    copies = [
        pltpu.make_async_copy(src_ref.at[pl.ds(i * step, step)], dst_ref.at[pl.ds(i * step, step)], sem.at[i])
        for i in range(n)
    ]
    for copy in copies:
        copy.start()
    for copy in copies:
        copy.wait()


def fetch(x):
    return pl.pallas_call(
        fetch_kernel,
        in_specs=[pl.BlockSpec(memory_space=pltpu.HBM)],
        out_specs=VMEM,
        out_shape=jax.ShapeDtypeStruct(x.shape, x.dtype),
        scratch_shapes=[pltpu.SemaphoreType.DMA((4,))],
        compiler_params=params(2),
        name="fetch",
    )(x)


def update_kernel(cnt_ref, lst_ref, piv_ref, first_ref, me_ref, tr_ref, ud_ref, rest_ref, *refs):
    parts = refs[1:11]
    out_ref, buf_ref, nat_ref, drow_ref, tmp_ref, sem = refs[11:]
    rows = buf_ref.shape[0]
    nblk = sem.shape[0]
    blk = rows // nblk
    width = nat_ref.shape[0]
    first = first_ref[0]
    late = lax.div(first, rows) >> 2

    @pl.when(late == 0)
    def _():
        nat_ref[...] = ud_ref[:width, :].astype(jnp.float32)
        drow_ref[...] = ud_ref[width:, :].astype(jnp.float32)

    @pl.when(late == 1)
    def _():
        nat_ref[...] = rest_ref[:width, :].astype(jnp.float32)
        drow_ref[...] = rest_ref[width:, :].astype(jnp.float32)

    sub = lax.broadcasted_iota(jnp.int32, (16, 128), 0)

    def fix(k, carry):
        i = lst_ref[k]
        loc = piv_ref[i] - first
        at = pl.ds(pl.multiple_of(loc & ~15, 16), 16)
        old = buf_ref[at, :].astype(jnp.float32)
        row = drow_ref[pl.ds(i, 1), :]
        buf_ref[at, :] = jnp.where(sub == (loc & 15), row, old).astype(jnp.bfloat16)
        return carry

    lax.fori_loop(0, cnt_ref[0], fix, 0)
    for i, where in enumerate(blocks()):
        tmp_ref[8 * i : 8 * i + 8, :] = nat_ref[block_at(me_ref[0], *where), :]
    ut = tmp_ref[...].T.astype(jnp.bfloat16)
    copies = []
    for b in range(nblk):
        half = b // (nblk // 2)
        here = pl.ds(b * blk, blk)
        there = pl.ds((b - half * (nblk // 2)) * blk, blk)
        pieces = []
        for s in (parts[:5], parts[5:]):
            pieces += [s[0][:, here], s[1][:, here], s[2][:, here], s[3 + half][:, there]]
        product = lax.dot_general(
            ut, jnp.concatenate(pieces, axis=0), (((1,), (0,)), ((), ())),
            preferred_element_type=jnp.float32,
        ).T
        new = buf_ref[here, :].astype(jnp.float32) - product
        if b == 0:
            head = jnp.where(first == 0, nat_ref[...], new[:width])
            buf_ref[:width, :] = head.astype(jnp.bfloat16)
            buf_ref[width:blk, :] = new[width:].astype(jnp.bfloat16)
        else:
            buf_ref[here, :] = new.astype(jnp.bfloat16)
        copies.append(pltpu.make_async_copy(buf_ref.at[here], out_ref.at[here], sem.at[b]))
        copies[-1].start()
    for copy in copies:
        copy.wait()


def update(cnt, lst, pivots, first, me, trailing, ud, rest, ahead, parts, nblk):
    rows, cols = trailing.shape
    width = pivots.shape[0]
    return pl.pallas_call(
        update_kernel,
        in_specs=[SMEM] * 5 + [VMEM] * 14,
        out_specs=[pl.BlockSpec(memory_space=pltpu.HBM), VMEM],
        scratch_shapes=[
            pltpu.VMEM((width, cols), jnp.float32),
            pltpu.VMEM((width, cols), jnp.float32),
            pltpu.VMEM((width, cols), jnp.float32),
            pltpu.SemaphoreType.DMA((nblk,)),
        ],
        out_shape=[jax.ShapeDtypeStruct((rows, cols), jnp.bfloat16)] * 2,
        input_output_aliases={5: 1},
        compiler_params=params(16),
        name="update",
    )(cnt, lst, pivots, first, me, trailing, ud, rest, ahead, *parts)[0]


def body(trailing, panel_t, pivots):
    rows = trailing.shape[0]
    width = pivots.shape[0]
    half = rows // 2
    barrier = lax.optimization_barrier
    first = (lax.axis_index("prow") * rows).astype(jnp.int32).reshape(1)
    me = lax.axis_index("pcol").astype(jnp.int32).reshape(1)
    trailing = pltpu.with_memory_space_constraint(trailing, pltpu.HBM)

    def zsend(x, pairs):
        return lax.ppermute(x, "prow", pairs)

    p, m, q = [send(panel_t, hop(d, 0, True)) for d in (1, -1, 2)]

    top, disp, cnt, lst = pick(trailing, pivots, first, rows)
    more = zsend(top, [(i + 4, i) for i in range(4)])
    p, m, q, top = barrier((p, m, q, top))

    up, down, across = hop(0, 1, True), hop(0, -1, True), hop(0, 2, True)
    diag = stack([panel_t, p, m, q], 0, width, "stack_d")
    diag_q, diag_p, diag_m = send(diag, across), send(diag, up), send(diag, down)
    block = stack([panel_t, p, m, q], 0, rows, "stack_p")
    block, diag_q, diag_p, diag_m, top, more = barrier((block, diag_q, diag_p, diag_m, top, more))
    near, far = send(block, up), send(block, down)
    own = stack([diag, diag_p, diag_m, diag_q], 0, width, "stack_l")
    top = add(top, more)
    more = zsend(top, [(2, 0), (3, 1)])
    other = send(own, CORES)
    top = add(top, more)
    top, disp, other, source = barrier((top, disp, other, trailing))
    copy = fetch(pltpu.with_memory_space_constraint(source, pltpu.HBM))
    more = zsend(top, [(1, 0)])
    lower = zsend(disp, [(0, 2)])
    top, block2 = barrier((top, block))
    swap = send(block2, CORES)
    more, disp, lower, copy = barrier((more, disp, lower, copy))
    u = solve(me, own, other, top, more)
    disp = choose(first, rows, (2,), disp, lower)
    disp = choose(first, rows, (1, 3), disp, zsend(disp, [(0, 1), (2, 3)]))
    ru = zsend(u, [(0, 2)])
    ru, near, far, swap, disp, copy = barrier((ru, near, far, swap, disp, copy))
    fa, fb = stack([near], 0, half, "stack_a"), stack([far], half, half, "stack_b")
    qa, qb = send(fa, up), send(fb, down)
    u = choose(first, rows, (2,), u, ru)
    ud = join(first, rows, (1, 3), u, zsend(u, [(0, 1), (2, 3)]), disp)
    ud, near, far = barrier((ud, near, far))
    rest = zsend(ud, [(i, i + 4) for i in range(4)])
    other_near, other_far = send(near, CORES), send(far, CORES)
    ahead = stack([qa, qb], 0, 128, "stack_q", 60)
    own = [block, near, far, qa, qb]
    parts = own + [swap, other_near, other_far, send(qa, CORES), send(qb, CORES)]
    return update(cnt, lst, pivots, first, me, copy, ud, rest, ahead, parts, NBLK)


def solution(mesh):
    return jax.shard_map(
        body,
        mesh=mesh,
        in_specs=(P("prow", "pcol"), P("pcol", "prow"), P()),
        out_specs=P("prow", "pcol"),
        check_vma=False,
    )
```
